32 devices in a mesh: dp: 8 (over y, x, core), fsdp: 4 (over z).
Axes of the slice: x: 2, y: 2, z: 4, core: 2. Of those that a mesh axis runs over, the one named last changes fastest.
Arguments:
- tokens: bfloat16 [2, 32, 512, 768], P(None, ('dp', 'fsdp')), may hold values from -6 to 6
- cotangent: bfloat16 [2, 32, 512, 768], P(None, ('dp', 'fsdp')), may hold values from -6 to 6
- doc_start: int32 [2, 32, 512], P(None, ('dp', 'fsdp')), may hold values 0 or 1
- memory_init: float32 [32, 512, 768], P(('dp', 'fsdp')), may hold values from -6 to 6
- norm1_gain: bfloat16 [768], P(('dp', 'fsdp')), may hold values from 0.25 to 1.75
- norm1_bias: bfloat16 [768], P(('dp', 'fsdp')), may hold values from -3 to 3
- qkv_weight: bfloat16 [768, 2304], P(('dp', 'fsdp')), may hold values from -0.21875 to 0.21875
- query_bias: bfloat16 [768], P(('dp', 'fsdp')), may hold values from -3 to 3
- value_bias: bfloat16 [768], P(('dp', 'fsdp')), may hold values from -3 to 3
- out_weight: bfloat16 [768, 768], P(('dp', 'fsdp')), may hold values from -1.75 to 1.75
- out_bias: bfloat16 [768], P(('dp', 'fsdp')), may hold values from -3 to 3
- norm2_gain: bfloat16 [768], P(('dp', 'fsdp')), may hold values from 0.25 to 1.75
- norm2_bias: bfloat16 [768], P(('dp', 'fsdp')), may hold values from -3 to 3
- up_weight: bfloat16 [768, 3072], P(('dp', 'fsdp')), may hold values from -0.21875 to 0.21875
- up_bias: bfloat16 [3072], P(('dp', 'fsdp')), may hold values from -3 to 3
- down_weight: bfloat16 [3072, 768], P(('dp', 'fsdp')), may hold values from -0.109375 to 0.109375
- down_bias: bfloat16 [768], P(('dp', 'fsdp')), may hold values from -3 to 3
Outputs:
- block_output: bfloat16 [2, 32, 512, 768], P(None, ('dp', 'fsdp'))
- tokens_grad: bfloat16 [2, 32, 512, 768], P(None, ('dp', 'fsdp'))
- norm1_gain_grad: float32 [768], P(('dp', 'fsdp'))
- norm1_bias_grad: float32 [768], P(('dp', 'fsdp'))
- qkv_weight_grad: float32 [768, 2304], P(('dp', 'fsdp'))
- query_bias_grad: float32 [768], P(('dp', 'fsdp'))
- value_bias_grad: float32 [768], P(('dp', 'fsdp'))
- out_weight_grad: float32 [768, 768], P(('dp', 'fsdp'))
- out_bias_grad: float32 [768], P(('dp', 'fsdp'))
- norm2_gain_grad: float32 [768], P(('dp', 'fsdp'))
- norm2_bias_grad: float32 [768], P(('dp', 'fsdp'))
- up_weight_grad: float32 [768, 3072], P(('dp', 'fsdp'))
- up_bias_grad: float32 [3072], P(('dp', 'fsdp'))
- down_weight_grad: float32 [3072, 768], P(('dp', 'fsdp'))
- down_bias_grad: float32 [768], P(('dp', 'fsdp'))
The draws below stay inside these ranges and needn't reach their ends.
Inputs may be any that keep to these rules, and one draw needn't show every extreme that they name: `doc_start`: 1 marks the first token of a document.
All inputs are finite; a program needn't handle non-finite values. No bound on the sum of `doc_start` on one device may be relied on, other than what follows from the above.
Results may differ from the reference program's by a relative error of at most 0.012.
Values may be sent and summed in bfloat16 or wider, within the bound.
No kernel may reach another device: no remote copies, remote signals or barrier semaphores. Data moves between devices by JAX's collectives and lax.ppermute only.
A program may use at most 320 MiB of HBM per device.

```python
import jax
import jax.numpy as jnp
from jax import lax

D = 768
H = 12
HD = 64
FF = 3072
L = 512
NB = 512
MICRO = 2
SEQS = 32


def plant(array, own_key, low, high):
    longest = array.shape.index(max(array.shape))
    spots = []
    for shift in (0, 1):
        where = [jax.random.randint(jax.random.fold_in(own_key, axis), (), 0, length) for axis, length in enumerate(array.shape)]
        where[longest] = (where[longest] + shift) % array.shape[longest]
        spots.append(tuple(where))
    return array.at[spots[0]].set(low).at[spots[1]].set(high)


def block_scale(stream_key, dims, shards, low, top_value):
    factor_of, own = 1.0, jax.random.fold_in(stream_key, 6)
    for dim, parts in shards:
        steps = jnp.exp(jax.random.uniform(jax.random.fold_in(own, dim), (parts,), jnp.float32, low / len(shards), top_value / len(shards)))
        factor_of = factor_of * jnp.repeat(steps, dims[dim] // parts).reshape([-1 if axis == dim else 1 for axis in range(len(dims))])
    return factor_of


def normal_values(key, shape, scale, bound, shards=(), kind=jnp.bfloat16):
    level = block_scale(key, shape, shards, -0.22, 0.18) if shards else 1.0
    array = jax.random.normal(key, shape, jnp.float32) * scale * level
    return jnp.minimum(jnp.maximum(array, -bound), bound).astype(kind)


def setup_inputs(seed: int = 0) -> dict:
    seeds = jax.random.split(jax.random.key(seed), 18)
    tokens = normal_values(seeds[0], (MICRO, SEQS, L, D), 1.0, 6.0, ((1, 32),))
    cotangent = normal_values(seeds[1], (MICRO, SEQS, L, D), 1.0, 6.0, ((1, 32),))
    doc_start = plant((jax.random.randint(seeds[2], (MICRO, SEQS, L), 0, L // 2) < 1).astype(jnp.int32), jax.random.fold_in(seeds[2], 1), 0, 1)
    memory_init = normal_values(seeds[3], (SEQS, NB, D), 1.0, 6.0, ((0, 32),), jnp.float32)
    norm1_gain = jnp.clip(1.0 + 0.15 * jax.random.normal(seeds[4], (D,), jnp.float32), 0.25, 1.75).astype(jnp.bfloat16)
    norm1_bias = normal_values(seeds[5], (D,), 0.3, 3.0, ((0, 32),))
    qkv_weight = normal_values(seeds[6], (D, 3 * D), D ** -0.5, 0.21875, ((0, 32),))
    query_bias = normal_values(seeds[7], (D,), 0.5, 3.0, ((0, 32),))
    value_bias = normal_values(seeds[8], (D,), 0.5, 3.0, ((0, 32),))
    out_weight = normal_values(seeds[9], (D, D), (D // 64) ** -0.5, 1.75, ((0, 32),))
    out_bias = normal_values(seeds[10], (D,), 0.3, 3.0, ((0, 32),))
    norm2_gain = jnp.clip(1.0 + 0.15 * jax.random.normal(seeds[11], (D,), jnp.float32), 0.25, 1.75).astype(jnp.bfloat16)
    norm2_bias = normal_values(seeds[12], (D,), 0.3, 3.0, ((0, 32),))
    up_weight = normal_values(seeds[13], (D, FF), D ** -0.5, 0.21875, ((0, 32),))
    up_bias = normal_values(seeds[14], (FF,), 0.5, 3.0, ((0, 32),))
    down_weight = normal_values(seeds[15], (FF, D), FF ** -0.5, 0.109375, ((0, 32),))
    down_bias = normal_values(seeds[16], (D,), 0.3, 3.0, ((0, 32),))
    return dict(tokens=tokens, cotangent=cotangent, doc_start=doc_start, memory_init=memory_init, norm1_gain=norm1_gain, norm1_bias=norm1_bias, qkv_weight=qkv_weight, query_bias=query_bias, value_bias=value_bias, out_weight=out_weight, out_bias=out_bias, norm2_gain=norm2_gain, norm2_bias=norm2_bias, up_weight=up_weight, up_bias=up_bias, down_weight=down_weight, down_bias=down_bias)


@jax.custom_vjp
def low(v):
    return lax.optimization_barrier(v.astype(jnp.bfloat16)).astype(jnp.float32)

@jax.custom_vjp
def low_back(v):
    return v

def low_keep(v):
    return (low(v), None)

def low_pass(kept, grad):
    return (grad,)

def back_keep(v):
    return (v, None)

def back_low(kept, grad):
    return (low(grad),)
low.defvjp(low_keep, low_pass)
low_back.defvjp(back_keep, back_low)
highest = lax.Precision.HIGHEST
epsilon = 1e-05
masked_fill = -1000000000.0

def product_high(left, right):
    return jnp.dot(left, right, precision=highest)

def rbf_tables():
    centers = (jnp.arange(NB, dtype=jnp.float32) + 0.5) / NB

    def bumps(points):
        return jnp.exp(-0.5 * jnp.square((centers[:, None] - points[None, :]) * NB))
    old_points = 0.75 * centers
    new_points = 0.75 + 0.25 * (jnp.arange(L, dtype=jnp.float32) + 0.5) / L
    phi_old = bumps(old_points)
    phi_new = bumps(new_points)
    totals = lax.optimization_barrier(jnp.sum(phi_old, axis=1)) + lax.optimization_barrier(jnp.sum(phi_new, axis=1))
    recon = bumps(centers)
    recon = recon / lax.optimization_barrier(jnp.sum(recon, axis=0, keepdims=True))
    carry_table = product_high(phi_old, recon.T) / totals[:, None]
    fresh_table = phi_new / totals[:, None]
    return (carry_table, fresh_table)

def build_masks(starts):
    documents = jnp.cumsum(starts)
    positions = jnp.arange(L)
    local_mask = (positions[None, :] <= positions[:, None]) & (documents[None, :] == documents[:, None])
    memory_mask = documents == 0
    keep_share = jnp.where(documents[L - 1] == 0, 1.0, 0.0).astype(jnp.float32)
    return (local_mask, memory_mask, keep_share)

def layer_norm(values, gain, bias):
    center = values - lax.optimization_barrier(jnp.mean(values, axis=-1, keepdims=True))
    spread = lax.optimization_barrier(jnp.mean(center * center, axis=-1, keepdims=True))
    return center * lax.rsqrt(spread + epsilon) * gain + bias

def segment(tokens_f, params, memory_low, local_mask, memory_mask):
    norm1_gain, norm1_bias, qkv_weight, query_bias, value_bias, out_weight, out_bias, norm2_gain, norm2_bias, up_weight, up_bias, down_weight, down_bias = params
    normed = layer_norm(tokens_f, norm1_gain, norm1_bias)
    normed_low = low(normed)
    projected = product_high(normed_low, qkv_weight)
    queries = low(low_back((projected[:, :D] + query_bias) * 0.125))
    local_keys = low(low_back(projected[:, D:2 * D]))
    local_values = low(low_back(projected[:, 2 * D:] + value_bias))
    memory_proj = product_high(memory_low, qkv_weight[:, D:])
    memory_keys = low(low_back(memory_proj[:, :D]))
    memory_values = low(low_back(memory_proj[:, D:] + value_bias))
    key_rows = jnp.concatenate([local_keys, memory_keys], axis=0).reshape(L + NB, H, HD)
    value_rows = jnp.concatenate([local_values, memory_values], axis=0).reshape(L + NB, H, HD)
    query_heads = queries.reshape(L, H, HD)
    scores = low_back(jnp.einsum('ihd,jhd->hij', query_heads, key_rows, precision=highest))
    memory_cols = jnp.broadcast_to(memory_mask[:, None], (L, NB))
    allowed = jnp.concatenate([local_mask, memory_cols], axis=1)
    scores = jnp.where(allowed[None], scores, masked_fill)
    probs = jax.nn.softmax(scores, axis=-1)
    mixture = jnp.einsum('hij,jhd->ihd', low(probs), value_rows, precision=highest).reshape(L, D)
    mixture = low(low_back(mixture))
    attended = low_back(product_high(mixture, out_weight) + out_bias)
    residual = tokens_f + attended
    normed2 = low(layer_norm(residual, norm2_gain, norm2_bias))
    up_pre = low_back(product_high(normed2, up_weight) + up_bias)
    activated = low(jax.nn.gelu(up_pre, approximate=True))
    output = residual + product_high(activated, down_weight) + down_bias
    return (output, normed)

def reference(tokens, cotangent, doc_start, memory_init, norm1_gain, norm1_bias, qkv_weight, query_bias, value_bias, out_weight, out_bias, norm2_gain, norm2_bias, up_weight, up_bias, down_weight, down_bias):
    params = tuple((p.astype(jnp.float32) for p in (norm1_gain, norm1_bias, qkv_weight, query_bias, value_bias, out_weight, out_bias, norm2_gain, norm2_bias, up_weight, up_bias, down_weight, down_bias)))
    carry_table, fresh_table = rbf_tables()

    def one_stream(totals, inputs):
        stream_tokens, stream_cots, stream_starts, memory = inputs
        outputs = []
        input_grads = []
        for batch_index in range(MICRO):
            local_mask, memory_mask, keep_share = build_masks(stream_starts[batch_index])
            tokens_f = stream_tokens[batch_index].astype(jnp.float32)
            memory_low = low(memory)

            def run(values, weights):
                return segment(values, weights, memory_low, local_mask, memory_mask)
            output, pull, normed = jax.vjp(run, tokens_f, params, has_aux=True)
            tokens_grad, params_grad = pull(stream_cots[batch_index].astype(jnp.float32))
            totals = tuple((t + g for t, g in zip(totals, params_grad)))
            memory = keep_share * product_high(carry_table, memory) + product_high(fresh_table, normed)
            outputs.append(output.astype(jnp.bfloat16))
            input_grads.append(tokens_grad.astype(jnp.bfloat16))
        return (totals, (jnp.stack(outputs), jnp.stack(input_grads)))
    start_totals = tuple((jnp.zeros(p.shape, jnp.float32) for p in params))
    totals, (outputs, input_grads) = lax.scan(one_stream, start_totals, (jnp.swapaxes(tokens, 0, 1), jnp.swapaxes(cotangent, 0, 1), jnp.swapaxes(doc_start, 0, 1), memory_init))
    block_output = jnp.swapaxes(outputs, 0, 1)
    tokens_grad = jnp.swapaxes(input_grads, 0, 1)
    return (block_output, tokens_grad, totals[0], totals[1], totals[2], totals[3], totals[4], totals[5], totals[6], totals[7], totals[8], totals[9], totals[10], totals[11], totals[12])
```

```python
import functools

import jax
import jax.numpy as jnp
from jax import lax
from jax.experimental import pallas as pl
from jax.experimental.pallas import tpu as pltpu
from jax.sharding import PartitionSpec as P

HD = 64


highest = lax.Precision.HIGHEST
epsilon = 1e-05
masked_fill = -1000000000.0


def product_high(left, right):
    return jnp.dot(left, right, precision=highest)


def product_low(left, right):
    return jnp.dot(left, right, preferred_element_type=jnp.float32)


def product_left(left, right):
    return lax.dot_general(
        left, right, (((0,), (0,)), ((), ())), preferred_element_type=jnp.float32
    )


def product_right(left, right):
    return lax.dot_general(
        left, right, (((1,), (1,)), ((), ())), preferred_element_type=jnp.float32
    )


def rbf_tables(seg_rows, basis):
    centers = (jnp.arange(basis, dtype=jnp.float32) + 0.5) / basis

    def bumps(points):
        return jnp.exp(-0.5 * jnp.square((centers[:, None] - points[None, :]) * basis))

    old_points = 0.75 * centers
    new_points = 0.75 + 0.25 * (jnp.arange(seg_rows, dtype=jnp.float32) + 0.5) / seg_rows
    phi_old = bumps(old_points)
    phi_new = bumps(new_points)
    totals = jnp.sum(phi_old, axis=1) + jnp.sum(phi_new, axis=1)
    recon = bumps(centers)
    recon = recon / jnp.sum(recon, axis=0, keepdims=True)
    carry_table = product_high(phi_old, recon.T) / totals[:, None]
    fresh_table = phi_new / totals[:, None]
    return (carry_table, fresh_table)


def build_masks(starts):
    positions = jnp.arange(starts.shape[0])
    before = positions[None, :] <= positions[:, None]
    documents = jnp.sum(jnp.where(before, starts[None, :], 0), axis=1)
    local_mask = before & (documents[None, :] == documents[:, None])
    memory_mask = documents == 0
    keep_share = jnp.where(documents[-1] == 0, 1.0, 0.0).astype(jnp.float32)
    return (local_mask, memory_mask, keep_share)


def layer_norm(values, gain, bias):
    center = values - jnp.mean(values, axis=-1, keepdims=True)
    spread = jnp.mean(center * center, axis=-1, keepdims=True)
    return center * lax.rsqrt(spread + epsilon) * gain + bias


def attention_probs(query_heads, key_rows, local_mask, memory_mask):
    scores = jnp.einsum("ihd,jhd->hij", query_heads, key_rows, preferred_element_type=jnp.float32)
    memory_cols = jnp.broadcast_to(
        memory_mask[:, None], (local_mask.shape[0], key_rows.shape[0] - local_mask.shape[1])
    )
    allowed = jnp.concatenate([local_mask, memory_cols], axis=1)
    return jax.nn.softmax(jnp.where(allowed[None], scores, masked_fill), axis=-1)


class Links:
    def __init__(self, mesh):
        self.across = mesh.shape["dp"] // 2
        self.deep = mesh.shape["fsdp"]
        self.count = self.across * 2 * self.deep

    def place(self):
        outer = lax.axis_index("dp")
        return (outer // 2, outer % 2, lax.axis_index("fsdp"))

    def swap(self, value, column=0, core=0, depth=0):
        pairs = []
        for device in range(self.count):
            outer, inner = divmod(device, self.deep)
            target = (((outer // 2) ^ column) * 2 + ((outer % 2) ^ core)) * self.deep + (
                inner ^ depth
            )
            pairs.append((device, target))
        return lax.ppermute(value, ("dp", "fsdp"), pairs)

    def gather(self, shard):
        column, core, depth = self.place()
        pieces = [shard] + [self.swap(shard, depth=s) for s in range(1, self.deep)]
        line = jnp.concatenate(
            [lax.select_n(depth ^ j, *pieces) for j in range(self.deep)], axis=0
        )
        lines = [line] + [self.swap(line, column=s) for s in range(1, self.across)]
        others = [self.swap(part, core=1) for part in lines]
        return self.assemble(lines + others)

    def assemble(self, parts):
        across = self.across
        rows, width = parts[0].shape

        def kernel(*refs):
            sources, target, sems = refs[: 2 * across], refs[2 * across], refs[2 * across + 1]
            outer = lax.axis_index("dp")
            copies = []
            for k in range(2 * across):
                s, c = k % across, k // across
                spot = ((outer // 2) ^ s) * 2 + ((outer % 2) ^ c)
                copies.append(pltpu.make_async_copy(sources[k], target.at[spot], sems.at[k]))
            for copy in copies:
                copy.start()
            for copy in copies:
                copy.wait()

        whole = pl.pallas_call(
            kernel,
            out_shape=jax.ShapeDtypeStruct((2 * across, rows, width), parts[0].dtype),
            in_specs=[pl.BlockSpec(memory_space=pl.ANY)] * (2 * across),
            out_specs=pl.BlockSpec(memory_space=pl.ANY),
            scratch_shapes=[pltpu.SemaphoreType.DMA((2 * across,))],
            name="assemble",
        )(*parts)
        return whole.reshape(2 * across * rows, width)

    def scatter(self, grads):
        column, core, depth = self.place()
        _, rows, width = grads.shape
        grads = grads.reshape(self.across, 2, self.deep, rows, width)
        pick = lambda v, i, axis: lax.dynamic_index_in_dim(v, i, axis, keepdims=False)
        came = self.swap(pick(grads, 1 - core, 1).astype(jnp.bfloat16), core=1)
        total = pick(grads, core, 1) + came.astype(jnp.float32)
        came = [
            self.swap(pick(total, column ^ s, 0).astype(jnp.bfloat16), column=s)
            for s in range(1, self.across)
        ]
        total = sum((part.astype(jnp.float32) for part in came), pick(total, column, 0))
        came = [
            self.swap(pick(total, depth ^ s, 0).astype(jnp.bfloat16), depth=s)
            for s in range(1, self.deep)
        ]
        return sum((part.astype(jnp.float32) for part in came), pick(total, depth, 0))


def forward(tokens_f, params, memory_low, local_mask, memory_mask):
    (
        norm1_gain,
        norm1_bias,
        qkv_weight,
        query_bias,
        value_bias,
        out_weight,
        out_bias,
        norm2_gain,
        norm2_bias,
        up_weight,
        up_bias,
        down_weight,
        down_bias,
    ) = params
    rows_here = tokens_f.shape[0]
    width = tokens_f.shape[1]
    head_count = width // HD
    normed = layer_norm(tokens_f, norm1_gain.astype(jnp.float32), norm1_bias.astype(jnp.float32))
    normed_low = normed.astype(jnp.bfloat16)
    projected = product_low(normed_low, qkv_weight)
    value_shift = value_bias.astype(jnp.float32)
    queries = ((projected[:, :width] + query_bias.astype(jnp.float32)) * 0.125).astype(jnp.bfloat16)
    local_keys = projected[:, width : 2 * width].astype(jnp.bfloat16)
    local_values = (projected[:, 2 * width :] + value_shift).astype(jnp.bfloat16)
    memory_proj = product_low(memory_low, qkv_weight[:, width:])
    memory_keys = memory_proj[:, :width].astype(jnp.bfloat16)
    memory_values = (memory_proj[:, width:] + value_shift).astype(jnp.bfloat16)
    key_rows = jnp.concatenate([local_keys, memory_keys], axis=0).reshape(-1, head_count, HD)
    value_rows = jnp.concatenate([local_values, memory_values], axis=0).reshape(-1, head_count, HD)
    query_heads = queries.reshape(rows_here, head_count, HD)
    probs = attention_probs(query_heads, key_rows, local_mask, memory_mask)
    mixture = (
        jnp.einsum(
            "hij,jhd->ihd",
            probs.astype(jnp.bfloat16),
            value_rows,
            preferred_element_type=jnp.float32,
        )
        .reshape(rows_here, width)
        .astype(jnp.bfloat16)
    )
    residual = tokens_f + product_low(mixture, out_weight) + out_bias.astype(jnp.float32)
    normed2_low = layer_norm(
        residual, norm2_gain.astype(jnp.float32), norm2_bias.astype(jnp.float32)
    ).astype(jnp.bfloat16)
    up_pre = product_low(normed2_low, up_weight) + up_bias.astype(jnp.float32)
    activated = jax.nn.gelu(up_pre, approximate=True).astype(jnp.bfloat16)
    output = residual + product_low(activated, down_weight) + down_bias.astype(jnp.float32)
    saved = (
        normed,
        normed_low,
        query_heads,
        key_rows,
        value_rows,
        mixture,
        residual,
        normed2_low,
        up_pre,
        activated,
    )
    return (output.astype(jnp.bfloat16), saved)


def backward(saved, cot_low, tokens_f, params, memory_low, local_mask, memory_mask):
    (
        norm1_gain,
        norm1_bias,
        qkv_weight,
        query_bias,
        value_bias,
        out_weight,
        out_bias,
        norm2_gain,
        norm2_bias,
        up_weight,
        up_bias,
        down_weight,
        down_bias,
    ) = params
    (
        normed,
        normed_low,
        query_heads,
        key_rows,
        value_rows,
        mixture,
        residual,
        normed2_low,
        up_pre,
        activated,
    ) = saved
    rows_here = tokens_f.shape[0]
    width = tokens_f.shape[1]
    head_count = width // HD
    cot_f = cot_low.astype(jnp.float32)
    down_bias_grad = jnp.sum(cot_f, axis=0)
    down_weight_grad = product_left(activated, cot_low)
    act_grad = product_right(cot_low, down_weight)
    gelu_pull = jax.vjp(lambda inner: jax.nn.gelu(inner, approximate=True), up_pre)[1]
    up_grad = gelu_pull(act_grad)[0].astype(jnp.bfloat16)
    up_bias_grad = jnp.sum(up_grad.astype(jnp.float32), axis=0)
    up_weight_grad = product_left(normed2_low, up_grad)
    norm2_in_grad = product_right(up_grad, up_weight)
    norm2_pull = jax.vjp(
        layer_norm, residual, norm2_gain.astype(jnp.float32), norm2_bias.astype(jnp.float32)
    )[1]
    residual_part, norm2_gain_grad, norm2_bias_grad = norm2_pull(norm2_in_grad)
    residual_grad = cot_f + residual_part
    attn_grad = residual_grad.astype(jnp.bfloat16)
    out_bias_grad = jnp.sum(attn_grad.astype(jnp.float32), axis=0)
    out_weight_grad = product_left(mixture, attn_grad)
    mixture_grad = product_right(attn_grad, out_weight).astype(jnp.bfloat16)
    grad_heads = mixture_grad.reshape(rows_here, head_count, HD)
    probs = attention_probs(query_heads, key_rows, local_mask, memory_mask)
    prob_grad = jnp.einsum(
        "ihd,jhd->hij", grad_heads, value_rows, preferred_element_type=jnp.float32
    )
    value_rows_grad = jnp.einsum(
        "hij,ihd->jhd", probs.astype(jnp.bfloat16), grad_heads, preferred_element_type=jnp.float32
    ).astype(jnp.bfloat16)
    score_grad = (probs * (prob_grad - jnp.sum(prob_grad * probs, axis=-1, keepdims=True))).astype(
        jnp.bfloat16
    )
    query_grad = (
        jnp.einsum("hij,jhd->ihd", score_grad, key_rows, preferred_element_type=jnp.float32)
        .astype(jnp.bfloat16)
        .reshape(rows_here, width)
    )
    key_rows_grad = (
        jnp.einsum("hij,ihd->jhd", score_grad, query_heads, preferred_element_type=jnp.float32)
        .astype(jnp.bfloat16)
        .reshape(-1, width)
    )
    value_rows_grad = value_rows_grad.reshape(-1, width)
    scaled_query_grad = query_grad * jnp.bfloat16(0.125)
    qkv_grad = jnp.concatenate(
        [scaled_query_grad, key_rows_grad[:rows_here], value_rows_grad[:rows_here]], axis=1
    )
    memory_grad = jnp.concatenate([key_rows_grad[rows_here:], value_rows_grad[rows_here:]], axis=1)
    query_bias_grad = jnp.sum(scaled_query_grad.astype(jnp.float32), axis=0)
    value_bias_grad = jnp.sum(value_rows_grad.astype(jnp.float32), axis=0)
    local_part = product_left(normed_low, qkv_grad)
    memory_part = product_left(memory_low, memory_grad)
    qkv_weight_grad = jnp.concatenate(
        [local_part[:, :width], local_part[:, width:] + memory_part], axis=1
    )
    normed_grad = product_right(qkv_grad, qkv_weight)
    norm1_pull = jax.vjp(
        layer_norm, tokens_f, norm1_gain.astype(jnp.float32), norm1_bias.astype(jnp.float32)
    )[1]
    tokens_part, norm1_gain_grad, norm1_bias_grad = norm1_pull(normed_grad)
    tokens_grad = (residual_grad + tokens_part).astype(jnp.bfloat16)
    grads = (
        norm1_gain_grad,
        norm1_bias_grad,
        qkv_weight_grad,
        query_bias_grad,
        value_bias_grad,
        out_weight_grad,
        out_bias_grad,
        norm2_gain_grad,
        norm2_bias_grad,
        up_weight_grad,
        up_bias_grad,
        down_weight_grad,
        down_bias_grad,
    )
    return (grads, tokens_grad)


def body(links, tokens, cotangent, doc_start, memory_init, *shards):
    (
        norm1_gain,
        norm1_bias,
        qkv_weight,
        query_bias,
        value_bias,
        out_weight,
        out_bias,
        norm2_gain,
        norm2_bias,
        up_weight,
        up_bias,
        down_weight,
        down_bias,
    ) = shards
    own, width = out_weight.shape
    hidden = up_weight.shape[1]
    fold = hidden // width
    n = links.count
    small = (norm1_gain, norm1_bias, query_bias, value_bias, out_bias, norm2_gain, norm2_bias, down_bias)
    small_row = jnp.concatenate(small + (up_bias,))
    small_size = small_row.shape[0]
    small_rows = jnp.zeros((8, 3 * width), jnp.bfloat16).at[0, :small_size].set(small_row)
    first = links.gather(jnp.concatenate([qkv_weight, small_rows], axis=0))
    first = first.reshape(n, own + 8, 3 * width)
    qkv_full = first[:, :own].reshape(n * own, 3 * width)
    small_all = first[:, own, :small_size]
    vectors = [small_all[:, k * own : (k + 1) * own].reshape(width) for k in range(8)]
    up_bias_full = small_all[:, 8 * own :].reshape(hidden)
    second = jnp.concatenate(
        [out_weight] + [up_weight[:, k * width : (k + 1) * width] for k in range(fold)], axis=1
    )
    second = links.gather(second)
    out_full = second[:, :width]
    up_full = second[:, width:]
    down_full = links.gather(down_weight)
    params = (
        vectors[0],
        vectors[1],
        qkv_full,
        vectors[2],
        vectors[3],
        out_full,
        vectors[4],
        vectors[5],
        vectors[6],
        up_full,
        up_bias_full,
        down_full,
        vectors[7],
    )
    carry_table, fresh_table = rbf_tables(tokens.shape[2], memory_init.shape[1])
    memory = memory_init[0]
    grad_totals = None
    outputs = []
    input_grads = []
    for batch_index in range(tokens.shape[0]):
        local_mask, memory_mask, keep_share = build_masks(doc_start[batch_index, 0])
        tokens_f = tokens[batch_index, 0].astype(jnp.float32)
        memory_low = memory.astype(jnp.bfloat16)
        output, saved = forward(tokens_f, params, memory_low, local_mask, memory_mask)
        grads, tokens_grad = backward(
            saved,
            cotangent[batch_index, 0],
            tokens_f,
            params,
            memory_low,
            local_mask,
            memory_mask,
        )
        if grad_totals is None:
            grad_totals = grads
        else:
            grad_totals = tuple((total + part for total, part in zip(grad_totals, grads)))
        if batch_index + 1 < tokens.shape[0]:
            memory = keep_share * product_high(carry_table, memory) + product_high(
                fresh_table, saved[0]
            )
        outputs.append(output)
        input_grads.append(tokens_grad)
    g = grad_totals
    small_grads = [g[k].reshape(n, own) for k in (0, 1, 3, 4, 6, 7, 8, 12)] + [g[10].reshape(n, -1)]
    small_grads = jnp.concatenate(small_grads, axis=1)
    small_grads = jnp.pad(small_grads[:, None], ((0, 0), (0, 7), (0, 3 * width - small_size)))
    down_grad = links.scatter(g[11].reshape(n, -1, width))
    second_grad = links.scatter(jnp.concatenate([g[5], g[9]], axis=1).reshape(n, own, -1))
    first_grad = links.scatter(
        jnp.concatenate([g[2].reshape(n, own, 3 * width), small_grads], axis=1)
    )
    vec = [first_grad[own, k * own : (k + 1) * own] for k in range(8)]
    block_output = jnp.stack(outputs)[:, None]
    tokens_grad_all = jnp.stack(input_grads)[:, None]
    return (
        block_output,
        tokens_grad_all,
        vec[0],
        vec[1],
        first_grad[:own],
        vec[2],
        vec[3],
        second_grad[:, :width],
        vec[4],
        vec[5],
        vec[6],
        second_grad[:, width:],
        first_grad[own, 8 * own : small_size],
        down_grad,
        vec[7],
    )


def solution(mesh):
    placed = (
        P(None, ("dp", "fsdp"), None, None),
        P(None, ("dp", "fsdp"), None, None),
        P(None, ("dp", "fsdp"), None),
        P(("dp", "fsdp"), None, None),
        P(("dp", "fsdp")),
        P(("dp", "fsdp")),
        P(("dp", "fsdp"), None),
        P(("dp", "fsdp")),
        P(("dp", "fsdp")),
        P(("dp", "fsdp"), None),
        P(("dp", "fsdp")),
        P(("dp", "fsdp")),
        P(("dp", "fsdp")),
        P(("dp", "fsdp"), None),
        P(("dp", "fsdp")),
        P(("dp", "fsdp"), None),
        P(("dp", "fsdp")),
    )
    return jax.shard_map(
        functools.partial(body, Links(mesh)),
        mesh=mesh,
        in_specs=placed,
        out_specs=(
            P(None, ("dp", "fsdp"), None, None),
            P(None, ("dp", "fsdp"), None, None),
            P(("dp", "fsdp")),
            P(("dp", "fsdp")),
            P(("dp", "fsdp"), None),
            P(("dp", "fsdp")),
            P(("dp", "fsdp")),
            P(("dp", "fsdp"), None),
            P(("dp", "fsdp")),
            P(("dp", "fsdp")),
            P(("dp", "fsdp")),
            P(("dp", "fsdp"), None),
            P(("dp", "fsdp")),
            P(("dp", "fsdp"), None),
            P(("dp", "fsdp")),
        ),
        check_vma=False,
    )
```

```python
import functools

import jax
import jax.numpy as jnp
from jax import lax
from jax.experimental import pallas as pl
from jax.experimental.pallas import tpu as pltpu
from jax.sharding import PartitionSpec as P

HD = 64
PAIR = 2 * HD
GROUPS = 2
epsilon = 1e-05
hidden_score = -1e30
bf16 = jnp.bfloat16
f32 = jnp.float32
VMEM = 60 * 2**20


def dot(left, right):
    return jnp.dot(left, right, preferred_element_type=f32)


def dot_right(left, right):
    return lax.dot_general(left, right, (((1,), (1,)), ((), ())), preferred_element_type=f32)


def dot_left(left, right):
    return lax.dot_general(left, right, (((0,), (0,)), ((), ())), preferred_element_type=f32)


def call(
    kernel,
    out_shape,
    *,
    grid=(1,),
    in_specs,
    out_specs,
    scratch=(),
    name,
    flops,
    traffic,
    exps=0,
    after=(),
):
    count = len(in_specs)

    def run(*refs):
        return kernel(*refs[:count], *refs[count + len(after) :])

    made = pl.pallas_call(
        run,
        out_shape=out_shape,
        grid=grid,
        in_specs=list(in_specs) + [hbm()] * len(after),
        out_specs=out_specs,
        scratch_shapes=list(scratch),
        compiler_params=pltpu.CompilerParams(vmem_limit_bytes=VMEM),
        cost_estimate=pl.CostEstimate(flops=flops, bytes_accessed=traffic, transcendentals=exps),
        name=name,
    )
    return lambda *operands: made(*operands, *after)


def shape(dims, dtype):
    return jax.ShapeDtypeStruct(dims, dtype)


def hbm():
    return pl.BlockSpec(memory_space=pl.ANY)


def spec(block, index):
    return pl.BlockSpec(block, index)


def fixed(dims):
    return pl.BlockSpec(dims, lambda *_: (0,) * len(dims))


class Links:
    def __init__(self, mesh):
        self.outer = mesh.shape["dp"]
        self.across = self.outer // 2
        self.deep = mesh.shape["fsdp"]
        self.count = self.outer * self.deep

    def place(self):
        outer = lax.axis_index("dp")
        return (outer // 2, outer % 2, lax.axis_index("fsdp"))

    def swap(self, value, column=0, core=0, depth=0):
        pairs = []
        for device in range(self.count):
            outer, inner = divmod(device, self.deep)
            target = (((outer // 2) ^ column) * 2 + ((outer % 2) ^ core)) * self.deep + (
                inner ^ depth
            )
            pairs.append((device, target))
        return lax.ppermute(value, ("dp", "fsdp"), pairs)

    def line(self, shard, segments, after=()):
        pieces = [shard] + [self.swap(shard, depth=s) for s in range(1, self.deep)]
        rows, width = shard.shape

        def kernel(*refs):
            target = refs[self.deep]
            depth = lax.axis_index("fsdp")
            values = [ref[...].astype(f32) for ref in refs[: self.deep]]
            turned = []
            for j in range(self.deep):
                value = values[0]
                for s in range(1, self.deep):
                    value = jnp.where(depth == s ^ j, values[s], value)
                turned.append(value)
            out = []
            at = 0
            for count in segments:
                out += [value[at : at + count] for value in turned]
                at += count
            target[...] = jnp.concatenate(out, axis=0).astype(bf16)

        return call(
            kernel,
            shape((self.deep * rows, width), bf16),
            in_specs=[fixed((rows, width))] * self.deep,
            out_specs=fixed((self.deep * rows, width)),
            name="line",
            flops=self.deep**2 * rows * width,
            traffic=4 * self.deep * rows * width,
            after=after,
        )(*pieces)

    def spread(self, line):
        lines = [line] + [self.swap(line, column=s) for s in range(1, self.across)]
        out = []
        for part in lines:
            out += [part, self.swap(part, core=1)]
        return (out, lines)

    def merge_core(self, send, keep, small=None, after=()):
        came = self.swap(send, core=1)
        across, rows, width = send.shape
        units = width // 128
        tile = 128 * max(k for k in range(1, 7) if units % k == 0)
        if small is None:
            smalls, wide = (), width
        else:
            small = small.astype(bf16)
            smalls, wide = (small, self.swap(small, core=1)), width + small.shape[2]
            tile = width

        def kernel(keep_ref, came_ref, *refs):
            outs = refs[len(smalls) :]
            column, core, _ = self.place()
            for s in range(across):
                value = keep_ref[column ^ s].astype(f32) + came_ref[column ^ s].astype(f32)
                outs[s][:, :tile] = value.astype(outs[s].dtype)
                if smalls:
                    value = sum(ref[(column ^ s) * 2 + core].astype(f32) for ref in refs[:2])
                    outs[s][:, tile:] = value.astype(outs[s].dtype)

        whole = pl.BlockSpec((across, rows, tile), lambda i: (0, 0, i))
        part = pl.BlockSpec((rows, wide if smalls else tile), lambda i: (0, i))
        return call(
            kernel,
            (shape((rows, wide), f32),) + (shape((rows, wide), bf16),) * (across - 1),
            grid=(width // tile,),
            in_specs=[whole, whole] + [fixed(v.shape) for v in smalls],
            out_specs=(part,) * across,
            name="merge_core",
            flops=across * rows * width,
            traffic=6 * across * rows * width,
            after=after,
        )(keep, came, *smalls)

    def merge_line(self, own, *sends, after=()):
        came = [self.swap(sends[s - 1], column=s) for s in range(1, self.across)]
        rows, width = own.shape
        main = rows // self.deep

        def kernel(own_ref, *refs):
            total = own_ref[...]
            for ref in refs[: self.across - 1]:
                total = total + ref[...].astype(f32)
            outs = refs[self.across - 1 :]
            parts = [total[j * main : (j + 1) * main] for j in range(self.deep)]
            depth = lax.axis_index("fsdp")
            for s in range(self.deep):
                value = parts[0]
                for j in range(1, self.deep):
                    value = jnp.where(depth == s ^ j, parts[j], value)
                outs[s][...] = value.astype(outs[s].dtype)

        return call(
            kernel,
            (shape((main, width), f32),) + (shape((main, width), bf16),) * (self.deep - 1),
            in_specs=[fixed((rows, width))] * self.across,
            out_specs=(fixed((main, width)),) * self.deep,
            name="merge_line",
            flops=(self.across + self.deep) * rows * width,
            traffic=14 * rows * width,
            after=after,
        )(own, *came)

    def merge_depth(self, own, *sends):
        came = [self.swap(sends[s - 1], depth=s) for s in range(1, self.deep)]
        return sum((part.astype(f32) for part in came), own)

    def load(self, parts, rows, at, target, sems, base=0):
        outer = lax.axis_index("dp")
        copies = []
        for k, part in enumerate(parts):
            spot = pl.multiple_of((outer ^ k) * rows, 16)
            copies.append(
                pltpu.make_async_copy(
                    part.at[pl.ds(at, rows), pl.ds(0, target.shape[1])],
                    target.at[pl.ds(spot, rows)],
                    sems.at[base + k],
                )
            )
        for copy in copies:
            copy.start()
        return copies


def rbf_tables(seg_rows, basis):
    centers = (jnp.arange(basis, dtype=f32) + 0.5) / basis

    def bumps(points):
        return jnp.exp(-0.5 * jnp.square((centers[:, None] - points[None, :]) * basis))

    old_points = 0.75 * centers
    new_points = 0.75 + 0.25 * (jnp.arange(seg_rows, dtype=f32) + 0.5) / seg_rows
    phi_old = bumps(old_points)
    phi_new = bumps(new_points)
    totals = jnp.sum(phi_old, axis=1) + jnp.sum(phi_new, axis=1)
    recon = bumps(centers)
    recon = recon / jnp.sum(recon, axis=0, keepdims=True)
    carry_table = jnp.dot(phi_old, recon.T, precision=lax.Precision.HIGH) / totals[:, None]
    fresh_table = phi_new / totals[:, None]
    return (carry_table, fresh_table)


def standardize(values):
    center = values - jnp.mean(values, axis=-1, keepdims=True)
    spread = jnp.mean(center * center, axis=-1, keepdims=True)
    scale = lax.rsqrt(spread + epsilon)
    return (center * scale, scale)


def norm_back(grad, gain, unit, scale):
    inner = grad * gain
    shift = jnp.mean(inner, axis=-1, keepdims=True)
    slope = jnp.mean(inner * unit, axis=-1, keepdims=True)
    return (inner - shift - unit * slope) * scale


def project(links, tokens, memory_low, vectors, first):
    batch, rows, width = tokens.shape
    basis = memory_low.shape[1]
    line_rows = width // links.outer

    def kernel(tokens_ref, memory_ref, vec_ref, *refs):
        parts, refs = refs[: links.outer], refs[links.outer :]
        q_ref, k_ref, v_ref, n_ref, weight, sems = refs

        @pl.when(pl.program_id(0) == 0)
        def _():
            for copy in links.load(parts, line_rows, 0, weight, sems):
                copy.wait()

        vec = vec_ref[...].astype(f32)
        unit, _ = standardize(tokens_ref[0].astype(f32))
        normed = (unit * vec[0:1] + vec[1:2]).astype(bf16)
        n_ref[0] = normed
        q_ref[0] = ((dot(normed, weight[:, :width]) + vec[2:3]) * 0.125).astype(bf16)
        k_ref[0, :rows] = dot(normed, weight[:, width : 2 * width]).astype(bf16)
        v_ref[0, :rows] = (dot(normed, weight[:, 2 * width :]) + vec[3:4]).astype(bf16)
        memory = memory_ref[0]
        k_ref[0, rows:] = dot(memory, weight[:, width : 2 * width]).astype(bf16)
        v_ref[0, rows:] = (dot(memory, weight[:, 2 * width :]) + vec[3:4]).astype(bf16)

    keys = rows + basis
    one = lambda r: spec((1, r, width), lambda m: (m, 0, 0))
    return call(
        kernel,
        (
            shape((batch, rows, width), bf16),
            shape((batch, keys, width), bf16),
            shape((batch, keys, width), bf16),
            shape((batch, rows, width), bf16),
        ),
        grid=(batch,),
        in_specs=[one(rows), one(basis), fixed(vectors.shape)] + [hbm()] * links.outer,
        out_specs=(one(rows), one(keys), one(keys), one(rows)),
        scratch=[pltpu.VMEM((width, 3 * width), bf16), pltpu.SemaphoreType.DMA((links.outer,))],
        name="project",
        flops=2 * batch * width * width * (3 * rows + 2 * basis),
        traffic=2 * (batch * width * 8 * rows + 3 * width * width),
    )(tokens, memory_low, vectors, *first)


def lanes(head):
    lane = lax.broadcasted_iota(jnp.int32, (1, PAIR), 1)
    return (lane // HD == head, (lane == (1 - head) * HD))


def attend(queries, keys, values, starts_col, starts_row):
    batch, rows, width = queries.shape
    total = keys.shape[1]
    heads = width // HD
    half = rows // 2

    def kernel(q_ref, k_ref, v_ref, col_ref, row_ref, mix_ref, inv_ref, e_ref, mask):
        @pl.when(pl.program_id(1) == 0)
        def _():
            i = lax.broadcasted_iota(jnp.int32, (rows, rows), 0)
            j = lax.broadcasted_iota(jnp.int32, (rows, rows), 1)
            allowed = (j <= i) & (col_ref[0] == row_ref[0])
            mask[...] = jnp.where(allowed, 0.0, hidden_score)

        q, k, v = q_ref[0], k_ref[0], v_ref[0]
        memory_bias = jnp.where(col_ref[0] == 0, 0.0, hidden_score).astype(bf16)
        outs = []
        for head in range(2):
            inside, first = lanes(head)
            qh = jnp.where(inside, q, jnp.where(first, memory_bias, 0).astype(bf16))
            kl = jnp.where(inside, k[:rows], 0).astype(bf16)
            km = jnp.where(inside, k[rows:], jnp.where(first, 1, 0).astype(bf16))
            vh = jnp.where(inside, v, 1).astype(bf16)
            parts = []
            for block in range(2):
                top, wide = block * half, (block + 1) * half
                here = qh[top : top + half]
                sl = dot_right(here, kl[:wide]) + mask[top : top + half, :wide]
                sm = dot_right(here, km)
                peak = jnp.maximum(
                    jnp.max(sl, axis=-1, keepdims=True), jnp.max(sm, axis=-1, keepdims=True)
                )
                el = jnp.exp(sl - peak).astype(bf16)
                em = jnp.exp(sm - peak).astype(bf16)
                e_ref[0, head, top : top + half, :wide] = el
                e_ref[0, head, top : top + half, rows:] = em
                parts.append(dot(el, vh[:wide]) + dot(em, vh[rows:]))
            outs.append(jnp.concatenate(parts, axis=0))
        inside, _ = lanes(0)
        mixed = jnp.where(inside, outs[0], outs[1])
        inverse = 1.0 / pltpu.roll(jnp.where(inside, outs[1], outs[0]), HD, 1)
        mix_ref[0] = (mixed * inverse).astype(bf16)
        inv_ref[0] = inverse

    pair = lambda r: spec((1, r, PAIR), lambda m, p: (m, 0, p))
    return call(
        kernel,
        (
            shape((batch, rows, width), bf16),
            shape((batch, rows, width), f32),
            shape((batch, heads, rows, total), bf16),
        ),
        grid=(batch, heads // 2),
        in_specs=[
            pair(rows),
            pair(total),
            pair(total),
            spec((1, rows, 1), lambda m, p: (m, 0, 0)),
            spec((1, 1, rows), lambda m, p: (m, 0, 0)),
        ],
        out_specs=(
            pair(rows),
            pair(rows),
            spec((1, 2, rows, total), lambda m, p: (m, p, 0, 0)),
        ),
        scratch=[pltpu.VMEM((rows, rows), f32)],
        name="attend",
        flops=16 * batch * heads * rows * total * HD,
        traffic=2 * batch * heads * rows * total,
        exps=batch * heads * rows * total,
    )(queries, keys, values, starts_col, starts_row)


def attend_back(queries, keys, values, exps, mixture, scaled, base, count, after=()):
    batch, rows, width = queries.shape
    total = keys.shape[1]
    half = rows // 2

    def kernel(q_ref, k_ref, v_ref, e_ref, mix_ref, g_ref, dq_ref, dk_ref, dv_ref, ds):
        q, k, v, g = q_ref[0], k_ref[0], v_ref[0], g_ref[0]
        product = -(g.astype(f32) * mix_ref[0].astype(f32))
        product = pltpu.roll(product, HD, 1).astype(bf16)
        dqs, dks, dvs = [], [], []
        for head in range(2):
            inside, _ = lanes(head)
            gh = jnp.where(inside, g, product)
            vh = jnp.where(inside, v, 1).astype(bf16)
            parts = []
            for block in range(2):
                top, wide = block * half, (block + 1) * half
                here = gh[top : top + half]
                el = e_ref[0, head, top : top + half, :wide]
                em = e_ref[0, head, top : top + half, rows:]
                dl = (el.astype(f32) * dot_right(here, vh[:wide])).astype(bf16)
                dm = (em.astype(f32) * dot_right(here, vh[rows:])).astype(bf16)
                ds[top : top + half, :wide] = dl
                ds[top : top + half, rows:] = dm
                parts.append(dot(dl, k[:wide]) + dot(dm, k[rows:]))
            dqs.append(jnp.concatenate(parts, axis=0))
            e = e_ref[0, head]
            dks.append(
                [
                    dot_left(ds[:, :half], q),
                    dot_left(ds[half:, half:rows], q[half:]),
                    dot_left(ds[:, rows:], q),
                ]
            )
            dvs.append(
                [
                    dot_left(e[:, :half], g),
                    dot_left(e[half:, half:rows], g[half:]),
                    dot_left(e[:, rows:], g),
                ]
            )
        inside, _ = lanes(0)
        dq_ref[0] = (jnp.where(inside, dqs[0], dqs[1]) * 0.125).astype(bf16)
        for ref, pieces in ((dk_ref, dks), (dv_ref, dvs)):
            for i, (lo, hi) in enumerate(((0, half), (half, rows), (rows, total))):
                ref[0, lo:hi] = jnp.where(inside, pieces[0][i], pieces[1][i]).astype(bf16)

    pair = lambda r: spec((1, r, PAIR), lambda m, p: (m, 0, p + base))
    out = lambda r: spec((1, r, PAIR), lambda m, p: (m, 0, p))
    return call(
        kernel,
        (
            shape((batch, rows, count * PAIR), bf16),
            shape((batch, total, count * PAIR), bf16),
            shape((batch, total, count * PAIR), bf16),
        ),
        grid=(batch, count),
        in_specs=[
            pair(rows),
            pair(total),
            pair(total),
            spec((1, 2, rows, total), lambda m, p: (m, p + base, 0, 0)),
            pair(rows),
            pair(rows),
        ],
        out_specs=(out(rows), out(total), out(total)),
        scratch=[pltpu.VMEM((rows, total), bf16)],
        name="attend_back",
        flops=64 * batch * count * rows * total * HD,
        traffic=4 * batch * count * rows * total,
        after=after,
    )(queries, keys, values, exps, mixture, scaled)


def lift(links, tokens, mixture, vectors, up_bias, second, hidden):
    rows, width = tokens.shape
    fold = hidden // width
    line_rows = width // links.outer
    step = 256

    def kernel(x_ref, mix_ref, vec_ref, bias_ref, *refs):
        parts, refs = refs[: links.outer], refs[links.outer :]
        res_ref, n_ref, act_ref, slope_ref, out_w, up_w, sems = refs

        @pl.when(pl.program_id(0) == 0)
        def _():
            copies = links.load(parts, line_rows, 0, out_w, sems)
            for j in range(fold):
                copies += links.load(
                    parts, line_rows, (1 + j) * line_rows, up_w.at[j], sems, (1 + j) * links.outer
                )
            for copy in copies:
                copy.wait()

        vec = vec_ref[...].astype(f32)
        residual = x_ref[...].astype(f32) + dot(mix_ref[...], out_w[...]) + vec[4:5]
        res_ref[...] = residual
        unit, _ = standardize(residual)
        normed = (unit * vec[5:6] + vec[6:7]).astype(bf16)
        n_ref[...] = normed
        for j in range(fold):
            cols = slice(j * width, (j + 1) * width)
            u = dot(normed, up_w[j]) + bias_ref[:, cols].astype(f32)
            c0 = 0.7978845608028654
            square = u * u
            t = jnp.tanh(u * (c0 + (c0 * 0.044715) * square))
            half_up = 0.5 + 0.5 * t
            act_ref[:, cols] = (u * half_up).astype(bf16)
            slope = half_up + (0.5 * u) * (1.0 - t * t) * (c0 + (3 * c0 * 0.044715) * square)
            slope_ref[:, cols] = slope.astype(bf16)

    one = lambda w: spec((step, w), lambda i: (i, 0))
    return call(
        kernel,
        (
            shape((rows, width), f32),
            shape((rows, width), bf16),
            shape((rows, hidden), bf16),
            shape((rows, hidden), bf16),
        ),
        grid=(rows // step,),
        in_specs=[one(width), one(width), fixed(vectors.shape), fixed(up_bias.shape)]
        + [hbm()] * links.outer,
        out_specs=(one(width), one(width), one(hidden), one(hidden)),
        scratch=[
            pltpu.VMEM((width, width), bf16),
            pltpu.VMEM((fold, width, width), bf16),
            pltpu.SemaphoreType.DMA(((1 + fold) * links.outer,)),
        ],
        name="lift",
        flops=2 * rows * width * (width + hidden),
        traffic=4 * rows * hidden + 10 * rows * width,
        exps=rows * hidden,
    )(tokens, mixture, vectors, up_bias, *second)


def settle(links, residual, activated, slopes, cot, inverse, vectors, second, third, hidden, after=()):
    rows, width = residual.shape
    fold = hidden // width
    line_rows = width // links.outer
    step = 256

    def kernel(res_ref, act_ref, slope_ref, cot_ref, inv_ref, vec_ref, *refs):
        parts, refs = refs[: links.outer], refs[links.outer :]
        tops, refs = refs[: links.outer], refs[links.outer :]
        y_ref, ug_ref, ag_ref, mg_ref, sums_ref, ub_ref, out_w, up_w, down_w, sems = refs

        @pl.when(pl.program_id(0) == 0)
        def _():
            copies = links.load(parts, line_rows, 0, out_w, sems)
            for j in range(fold):
                copies += links.load(
                    parts, line_rows, (1 + j) * line_rows, up_w.at[j], sems, (1 + j) * links.outer
                )
            copies += links.load(
                tops, fold * line_rows, 0, down_w, sems, (1 + fold) * links.outer
            )
            for copy in copies:
                copy.wait()
            sums_ref[...] = jnp.zeros_like(sums_ref)
            ub_ref[...] = jnp.zeros_like(ub_ref)

        vec = vec_ref[...].astype(f32)
        residual = res_ref[...]
        y_ref[...] = (residual + dot(act_ref[...], down_w[...]) + vec[7:8]).astype(bf16)
        cot = cot_ref[...]
        cot_f = cot.astype(f32)
        into = jnp.zeros((step, width), f32)
        for j in range(fold):
            cols = slice(j * width, (j + 1) * width)
            grad = dot_right(cot, down_w[cols, :]) * slope_ref[:, cols].astype(f32)
            low = grad.astype(bf16)
            ug_ref[:, cols] = low
            ub_ref[0:1, cols] += jnp.sum(grad, axis=0, keepdims=True)
            into += dot_right(low, up_w[j])
        unit, scale = standardize(residual)
        residual_grad = cot_f + norm_back(into, vec[5:6], unit, scale)
        low = residual_grad.astype(bf16)
        ag_ref[...] = low
        mg_ref[...] = (dot_right(low, out_w[...]) * inv_ref[...]).astype(bf16)
        total = lambda v: jnp.sum(v, axis=0, keepdims=True)
        sums_ref[0:1] += total(residual_grad)
        sums_ref[1:2] += total(into * unit)
        sums_ref[2:3] += total(into)
        sums_ref[3:4] += total(cot_f)

    one = lambda w: spec((step, w), lambda i: (i, 0))
    return call(
        kernel,
        (
            shape((rows, width), bf16),
            shape((rows, hidden), bf16),
            shape((rows, width), bf16),
            shape((rows, width), bf16),
            shape((8, width), f32),
            shape((8, hidden), f32),
        ),
        grid=(rows // step,),
        in_specs=[one(width), one(hidden), one(hidden), one(width), one(width), fixed(vectors.shape)]
        + [hbm()] * (2 * links.outer),
        out_specs=(
            one(width),
            one(hidden),
            one(width),
            one(width),
            fixed((8, width)),
            fixed((8, hidden)),
        ),
        scratch=[
            pltpu.VMEM((width, width), bf16),
            pltpu.VMEM((fold, width, width), bf16),
            pltpu.VMEM((hidden, width), bf16),
            pltpu.SemaphoreType.DMA(((2 + fold) * links.outer,)),
        ],
        name="settle",
        flops=2 * rows * width * (width + 3 * hidden),
        traffic=6 * rows * hidden + 16 * rows * width,
        after=after,
    )(residual, activated, slopes, cot, inverse, vectors, *second, *third)


def finish(links, tokens, attn_grad, groups, vectors, first, after=()):
    batch, rows, width = tokens.shape
    line_rows = width // links.outer
    total_rows = groups[0][1].shape[1]
    wide = groups[0][0].shape[2]

    def kernel(x_ref, ag_ref, vec_ref, *refs):
        grads, refs = refs[: 3 * len(groups)], refs[3 * len(groups) :]
        parts, refs = refs[: links.outer], refs[links.outer :]
        tg_ref, sums_ref, weight, sems = refs

        @pl.when(pl.program_id(0) == 0)
        def _():
            for copy in links.load(parts, line_rows, 0, weight, sems):
                copy.wait()
            sums_ref[...] = jnp.zeros_like(sums_ref)

        total = lambda v: jnp.sum(v.astype(f32), axis=0, keepdims=True)
        vec = vec_ref[...].astype(f32)
        grad = jnp.zeros((rows, width), f32)
        for g in range(len(groups)):
            dq_ref, dk_ref, dv_ref = grads[3 * g : 3 * g + 3]
            for kind, value in enumerate((dq_ref[0], dk_ref[0, :rows], dv_ref[0, :rows])):
                at = kind * width + g * wide
                grad += dot_right(value, weight[:, at : at + wide])
            cols = slice(g * wide, (g + 1) * wide)
            sums_ref[2:3, cols] += total(dq_ref[0])
            sums_ref[3:4, cols] += total(dv_ref[0])
        unit, scale = standardize(x_ref[0].astype(f32))
        tg_ref[0] = (ag_ref[0].astype(f32) + norm_back(grad, vec[0:1], unit, scale)).astype(bf16)
        sums_ref[0:1] += total(grad * unit)
        sums_ref[1:2] += total(grad)

    one = lambda r, w=width: spec((1, r, w), lambda m: (m, 0, 0))
    return call(
        kernel,
        (shape((batch, rows, width), bf16), shape((8, width), f32)),
        grid=(batch,),
        in_specs=[one(rows), one(rows), fixed(vectors.shape)]
        + [one(rows, wide), one(total_rows, wide), one(total_rows, wide)] * len(groups)
        + [hbm()] * links.outer,
        out_specs=(one(rows), fixed((8, width))),
        scratch=[pltpu.VMEM((width, 3 * width), bf16), pltpu.SemaphoreType.DMA((links.outer,))],
        name="finish",
        flops=6 * batch * rows * width * width,
        traffic=12 * batch * rows * width,
        after=after,
    )(tokens, attn_grad, vectors, *[v for group in groups for v in group], *first)


def split_rows(links, acc, send_ref, keep_ref, block, groups, cols):
    core = lax.axis_index("dp") % 2
    for a in range(groups):
        there = pl.multiple_of((2 * a + 1 - core) * block, 8)
        here = pl.multiple_of((2 * a + core) * block, 8)
        send_ref[a, 0:block, cols] = acc[pl.ds(there, block)].astype(bf16)
        keep_ref[a, 0:block, cols] = acc[pl.ds(here, block)].astype(bf16)


def down_grads(links, activated, cot):
    rows, hidden = activated.shape
    width = cot.shape[1]
    block = hidden // links.outer

    def kernel(act_ref, cot_ref, send_ref, keep_ref, acc):
        acc[...] = dot_left(act_ref[...], cot_ref[...])
        split_rows(links, acc, send_ref, keep_ref, block, 1, slice(0, width))

    out = spec((1, block, width), lambda i: (i, 0, 0))
    return call(
        kernel,
        (shape((links.across, block, width), bf16),) * 2,
        grid=(links.across,),
        in_specs=[spec((rows, 2 * block), lambda i: (0, i)), fixed((rows, width))],
        out_specs=(out, out),
        scratch=[pltpu.VMEM((2 * block, width), f32)],
        name="down_grads",
        flops=2 * rows * hidden * width,
        traffic=2 * hidden * (rows + width),
    )(activated, cot)


def up_out_grads(links, mixture, attn_grad, normed2, up_grad, after=()):
    rows, width = mixture.shape
    hidden = up_grad.shape[1]
    fold = hidden // width
    block = width // links.outer

    def kernel(mix_ref, ag_ref, n_ref, ug_ref, send_ref, keep_ref, acc):
        step = pl.program_id(0)

        @pl.when(step == 0)
        def _():
            acc[...] = dot_left(mix_ref[...], ag_ref[...])

        @pl.when(step > 0)
        def _():
            acc[...] = dot_left(n_ref[...], ug_ref[...])

        split_rows(links, acc, send_ref, keep_ref, block, links.across, slice(0, width))

    out = spec((links.across, block, width), lambda i: (0, 0, i))
    return call(
        kernel,
        (shape((links.across, block, width + hidden), bf16),) * 2,
        grid=(1 + fold,),
        in_specs=[
            fixed((rows, width)),
            fixed((rows, width)),
            fixed((rows, width)),
            spec((rows, width), lambda i: (0, jnp.maximum(i - 1, 0))),
        ],
        out_specs=(out, out),
        scratch=[pltpu.VMEM((width, width), f32)],
        name="up_out_grads",
        flops=2 * rows * width * (hidden + width),
        traffic=2 * (rows + width) * (hidden + width),
        after=after,
    )(mixture, attn_grad, normed2, up_grad)


def qkv_grads(links, normed, memory_low, groups, after=()):
    batch, rows, width = normed.shape
    total = groups[0][1].shape[1]
    wide = groups[0][0].shape[2]
    block = width // links.outer
    basis = memory_low.shape[1]
    count = len(groups)

    def kernel(n_ref, mem_ref, *refs):
        grads, refs = refs[: 3 * count], refs[3 * count :]
        send_ref, keep_ref, acc = refs
        step = pl.program_id(0)
        for at in range(3 * count):

            @pl.when(step == at)
            def _(at=at):
                ref = grads[3 * (at % count) + at // count]
                if at < count:
                    acc[...] = sum(dot_left(n_ref[m], ref[m]) for m in range(batch))
                else:
                    acc[...] = sum(
                        dot_left(n_ref[m], ref[m, :rows]) + dot_left(mem_ref[m], ref[m, rows:])
                        for m in range(batch)
                    )

        split_rows(links, acc, send_ref, keep_ref, block, links.across, slice(0, wide))

    out = spec((links.across, block, wide), lambda i: (0, 0, i))
    return call(
        kernel,
        (shape((links.across, block, 3 * width), bf16),) * 2,
        grid=(3 * count,),
        in_specs=[fixed((batch, rows, width)), fixed((batch, basis, width))]
        + [fixed((batch, rows, wide)), fixed((batch, total, wide)), fixed((batch, total, wide))] * count,
        out_specs=(out, out),
        scratch=[pltpu.VMEM((width, wide), f32)],
        name="qkv_grads",
        flops=2 * batch * width * width * (3 * rows + 2 * basis),
        traffic=2 * batch * width * 7 * rows,
        after=after,
    )(normed, memory_low, *[v for group in groups for v in group])


def untangle(links, value):
    outer = lax.axis_index("dp")
    bit = 1
    while bit < links.outer:
        split = value.reshape((links.outer // (2 * bit), 2, bit) + value.shape[1:])
        value = jnp.where(outer & bit, split[:, ::-1], split).reshape(value.shape)
        bit *= 2
    return value


def body(links, tokens, cotangent, doc_start, memory_init, *shards):
    (
        norm1_gain,
        norm1_bias,
        qkv_weight,
        query_bias,
        value_bias,
        out_weight,
        out_bias,
        norm2_gain,
        norm2_bias,
        up_weight,
        up_bias,
        down_weight,
        down_bias,
    ) = shards
    own, width = out_weight.shape
    hidden = up_weight.shape[1]
    fold = hidden // width
    n = links.count
    tokens, cotangent, doc_start, memory_init = (
        tokens[:, 0],
        cotangent[:, 0],
        doc_start[:, 0],
        memory_init[0],
    )
    batch, rows, _ = tokens.shape

    small = (norm1_gain, norm1_bias, query_bias, value_bias, out_bias, norm2_gain, norm2_bias, down_bias, up_bias)
    slots = [(k % own, 64 * (k // own)) for k in range(len(small))]

    def lay(values):
        total = 0
        for (row, lane), value in zip(slots, values):
            lead = ((0, 0),) * (value.ndim - 1)
            edge = ((row, own - 1 - row), (lane, 128 - lane - value.shape[-1]))
            total = total + jnp.pad(value[..., None, :], lead + edge)
        return total

    line = links.line(jnp.concatenate([qkv_weight, lay(small)], axis=1), [own])
    first, crossed = links.spread(line)
    middle = jnp.concatenate(
        [out_weight] + [up_weight[:, k * width : (k + 1) * width] for k in range(fold)], axis=0
    )
    line = links.line(middle, [own] * (1 + fold), after=crossed[1:])
    second, crossed = links.spread(line)
    line = links.line(down_weight, [fold * own], after=crossed[1:])
    third, _ = links.spread(line)

    small_all = jnp.stack([part[:, 3 * width :] for part in first])
    small_all = untangle(links, small_all).reshape(n, own, 128)
    take = lambda k, size: small_all[:, slots[k][0], slots[k][1] : slots[k][1] + size]
    vectors = jnp.stack([take(k, own) for k in range(8)]).reshape(8, width)
    up_bias_full = take(8, fold * own).reshape(1, hidden)

    positions = jnp.arange(rows)
    before = positions[None, :] <= positions[:, None]
    documents = jnp.sum(jnp.where(before, doc_start[:, None, :], 0), axis=2)

    carry_table, fresh_table = rbf_tables(rows, memory_init.shape[0])
    high = functools.partial(jnp.dot, precision=lax.Precision.HIGH)
    memories = [memory_init.astype(bf16)]
    carried, gained, biased = memory_init, None, None
    for m in range(batch - 1):
        keep_share = jnp.where(documents[m, -1] == 0, 1.0, 0.0)
        unit, _ = standardize(tokens[m].astype(f32))
        table = keep_share * carry_table
        carried = high(table, carried)
        new_gained = high(fresh_table, unit)
        new_biased = jnp.sum(fresh_table, axis=1, keepdims=True)
        if m:
            new_gained += high(table, gained)
            new_biased += high(table, biased)
        gained, biased = new_gained, new_biased
        gain, bias = vectors[0].astype(f32), vectors[1].astype(f32)
        memories.append((carried + gained * gain + biased * bias).astype(bf16))
    memory_low = jnp.stack(memories)

    queries, keys, values, normed = project(links, tokens, memory_low, vectors, first)
    mixture, inverse, exps = attend(
        queries, keys, values, documents[:, :, None], documents[:, None, :]
    )
    flat = lambda v: v.reshape(batch * rows, v.shape[-1])
    full = lambda v: v.reshape(batch, rows, v.shape[-1])
    residual, normed2, activated, slopes = lift(
        links, flat(tokens), flat(mixture), vectors, up_bias_full, second, hidden
    )
    down_parts = down_grads(links, activated, flat(cotangent))
    output, up_grad, attn_grad, scaled, sums2, up_sums = settle(
        links,
        residual,
        activated,
        slopes,
        flat(cotangent),
        flat(inverse),
        vectors,
        second,
        third,
        hidden,
        after=down_parts[:1],
    )
    down_parts = links.merge_core(*down_parts, after=[attn_grad])
    up_parts = up_out_grads(links, flat(mixture), attn_grad, normed2, up_grad, after=down_parts[1:2])
    pairs = width // PAIR
    count = pairs // GROUPS
    back = functools.partial(attend_back, queries, keys, values, exps, mixture, full(scaled))
    groups = [back(0, count, after=up_parts[:1])]
    for g in range(1, GROUPS):
        if g == 1:
            down_parts = links.merge_line(*down_parts, after=groups[-1][:1])
            up_parts = links.merge_core(*up_parts, after=groups[-1][:1])
        groups.append(back(g * count, count, after=(down_parts[1], up_parts[1])))
    up_parts = links.merge_line(*up_parts, after=groups[-1][:1])
    qkv_parts = qkv_grads(links, normed, memory_low, groups, after=up_parts[1:2])
    tokens_grad, sums1 = finish(
        links, tokens, full(attn_grad), groups, vectors, first, after=qkv_parts[:1]
    )
    sums = [sums1[k] for k in range(4)] + [sums2[k] for k in range(4)] + [up_sums[0]]
    small_grads = lay([v.reshape(n, -1) for v in sums]).reshape(links.outer, links.deep * own, 128)
    qkv_parts = links.merge_line(*links.merge_core(*qkv_parts, small_grads))

    down_grad = links.merge_depth(*down_parts)
    up_grad = links.merge_depth(*up_parts)
    qkv_grad = links.merge_depth(*qkv_parts)
    vec = [
        qkv_grad[row, 3 * width + lane : 3 * width + lane + size]
        for (row, lane), size in zip(slots, [own] * 8 + [fold * own])
    ]
    lead = lambda v: v[:, None]
    return (
        lead(full(output)),
        lead(tokens_grad),
        vec[0],
        vec[1],
        qkv_grad[:, : 3 * width],
        vec[2],
        vec[3],
        up_grad[:, :width],
        vec[4],
        vec[5],
        vec[6],
        up_grad[:, width:],
        vec[8],
        down_grad,
        vec[7],
    )


def solution(mesh):
    both = ("dp", "fsdp")
    vector, matrix = P(both), P(both, None)
    params = (
        vector,
        vector,
        matrix,
        vector,
        vector,
        matrix,
        vector,
        vector,
        vector,
        matrix,
        vector,
        matrix,
        vector,
    )
    stream = P(None, both, None, None)
    return jax.shard_map(
        functools.partial(body, Links(mesh)),
        mesh=mesh,
        in_specs=(stream, stream, P(None, both, None), P(both, None, None)) + params,
        out_specs=(stream, stream) + params,
        check_vma=False,
    )
```

```python
import functools

import jax
import jax.numpy as jnp
from jax import lax
from jax.experimental import pallas as pl
from jax.experimental.pallas import tpu as pltpu
from jax.sharding import PartitionSpec as P

HD = 64
PAIR = 2 * HD
GROUPS = 1
BACK = 2
epsilon = 1e-05
hidden_score = -1e30
bf16 = jnp.bfloat16
f32 = jnp.float32
VMEM = 60 * 2**20


def dot(left, right):
    return jnp.dot(left, right, preferred_element_type=f32)


def dot_right(left, right):
    return lax.dot_general(left, right, (((1,), (1,)), ((), ())), preferred_element_type=f32)


def dot_left(left, right):
    return lax.dot_general(left, right, (((0,), (0,)), ((), ())), preferred_element_type=f32)


def call(
    kernel,
    out_shape,
    *,
    grid=(1,),
    in_specs,
    out_specs,
    scratch=(),
    name,
    flops,
    traffic,
    exps=0,
    after=(),
):
    count = len(in_specs)

    def run(*refs):
        return kernel(*refs[:count], *refs[count + len(after) :])

    made = pl.pallas_call(
        run,
        out_shape=out_shape,
        grid=grid,
        in_specs=list(in_specs) + [hbm()] * len(after),
        out_specs=out_specs,
        scratch_shapes=list(scratch),
        compiler_params=pltpu.CompilerParams(vmem_limit_bytes=VMEM),
        cost_estimate=pl.CostEstimate(flops=flops, bytes_accessed=traffic, transcendentals=exps),
        name=name,
    )
    return lambda *operands: made(*operands, *after)


def shape(dims, dtype):
    return jax.ShapeDtypeStruct(dims, dtype)


def hbm():
    return pl.BlockSpec(memory_space=pl.ANY)


def spec(block, index):
    return pl.BlockSpec(block, index)


def fixed(dims):
    return pl.BlockSpec(dims, lambda *_: (0,) * len(dims))


class Links:
    def __init__(self, mesh):
        self.outer = mesh.shape["dp"]
        self.across = self.outer // 2
        self.deep = mesh.shape["fsdp"]
        self.count = self.outer * self.deep

    def place(self):
        outer = lax.axis_index("dp")
        return (outer // 2, outer % 2, lax.axis_index("fsdp"))

    def swap(self, value, column=0, core=0, depth=0):
        pairs = []
        for device in range(self.count):
            outer, inner = divmod(device, self.deep)
            target = (((outer // 2) ^ column) * 2 + ((outer % 2) ^ core)) * self.deep + (
                inner ^ depth
            )
            pairs.append((device, target))
        return lax.ppermute(value, ("dp", "fsdp"), pairs)

    def line(self, shard, segments, after=()):
        pieces = [shard] + [self.swap(shard, depth=s) for s in range(1, self.deep)]
        rows, width = shard.shape

        def kernel(*refs):
            target = refs[self.deep]
            depth = lax.axis_index("fsdp")
            values = [ref[...].astype(f32) for ref in refs[: self.deep]]
            turned = []
            for j in range(self.deep):
                value = values[0]
                for s in range(1, self.deep):
                    value = jnp.where(depth == s ^ j, values[s], value)
                turned.append(value)
            out = []
            at = 0
            for count in segments:
                out += [value[at : at + count] for value in turned]
                at += count
            target[...] = jnp.concatenate(out, axis=0).astype(bf16)

        return call(
            kernel,
            shape((self.deep * rows, width), bf16),
            in_specs=[fixed((rows, width))] * self.deep,
            out_specs=fixed((self.deep * rows, width)),
            name="line",
            flops=self.deep**2 * rows * width,
            traffic=4 * self.deep * rows * width,
            after=after,
        )(*pieces)

    def spread(self, line, after=()):
        lines = [line] + [self.swap(line, column=s) for s in range(1, self.across)]
        if after:
            lines = gate(lines, after)
        out = []
        for part in lines:
            out += [part, self.swap(part, core=1)]
        return out

    def merge_core(self, send, keep, send_more=None, keep_more=None, after=()):
        across, rows, width = send.shape
        came = self.swap(send, core=1)
        if send_more is None:
            more, wide = (), width
            units = width // 128
            tile = 128 * max(k for k in range(1, 7) if units % k == 0)
        else:
            more = (keep_more, self.swap(send_more, core=1))
            wide, tile = width + send_more.shape[2], width

        def kernel(keep_ref, came_ref, *refs):
            outs = refs[len(more) :]
            column = lax.axis_index("dp") // 2
            for s in range(across):
                value = keep_ref[column ^ s].astype(f32) + came_ref[column ^ s].astype(f32)
                outs[s][:, :tile] = value.astype(outs[s].dtype)
                if more:
                    value = refs[0][column ^ s].astype(f32) + refs[1][column ^ s].astype(f32)
                    outs[s][:, tile:] = value.astype(outs[s].dtype)

        whole = pl.BlockSpec((across, rows, tile), lambda i: (0, 0, i))
        part = pl.BlockSpec((rows, wide if more else tile), lambda i: (0, i))
        return call(
            kernel,
            (shape((rows, wide), f32),) + (shape((rows, wide), bf16),) * (across - 1),
            grid=(width // tile,),
            in_specs=[whole, whole] + [fixed(v.shape) for v in more],
            out_specs=(part,) * across,
            name="merge_core",
            flops=across * rows * width,
            traffic=6 * across * rows * width,
            after=after,
        )(keep, came, *more)

    def merge_columns(self, own, *sends, after=()):
        came = [self.swap(sends[s - 1], column=s) for s in range(1, self.across)]
        rows, width = own.shape
        tile = 768 if width % 768 == 0 else 128

        def kernel(own_ref, *refs):
            total = own_ref[...]
            for ref in refs[:-1]:
                total = total + ref[...].astype(f32)
            refs[-1][...] = total

        part = pl.BlockSpec((rows, tile), lambda i: (0, i))
        return call(
            kernel,
            shape((rows, width), f32),
            grid=(width // tile,),
            in_specs=[part] * self.across,
            out_specs=part,
            name="merge_columns",
            flops=self.across * rows * width,
            traffic=14 * rows * width,
            after=after,
        )(own, *came)

    def merge_deep(self, total):
        return lax.psum_scatter(total, "fsdp", scatter_dimension=0, tiled=True)

    def merge_line(self, own, *sends, after=()):
        came = [self.swap(sends[s - 1], column=s) for s in range(1, self.across)]
        rows, width = own.shape
        main = rows // self.deep

        def kernel(own_ref, *refs):
            total = own_ref[...]
            for ref in refs[: self.across - 1]:
                total = total + ref[...].astype(f32)
            outs = refs[self.across - 1 :]
            parts = [total[j * main : (j + 1) * main] for j in range(self.deep)]
            depth = lax.axis_index("fsdp")
            for s in range(self.deep):
                value = parts[0]
                for j in range(1, self.deep):
                    value = jnp.where(depth == s ^ j, parts[j], value)
                outs[s][...] = value.astype(outs[s].dtype)

        return call(
            kernel,
            (shape((main, width), f32),) + (shape((main, width), bf16),) * (self.deep - 1),
            in_specs=[fixed((rows, width))] * self.across,
            out_specs=(fixed((main, width)),) * self.deep,
            name="merge_line",
            flops=(self.across + self.deep) * rows * width,
            traffic=14 * rows * width,
            after=after,
        )(own, *came)

    def merge_depth(self, own, *sends):
        came = [self.swap(sends[s - 1], depth=s) for s in range(1, self.deep)]
        return sum((part.astype(f32) for part in came), own)

    def load(self, parts, rows, at, target, sems, base=0):
        outer = lax.axis_index("dp")
        copies = []
        for k, part in enumerate(parts):
            spot = pl.multiple_of((outer ^ k) * rows, 16)
            copies.append(
                pltpu.make_async_copy(
                    part.at[pl.ds(at, rows), pl.ds(0, target.shape[1])],
                    target.at[pl.ds(spot, rows)],
                    sems.at[base + k],
                )
            )
        for copy in copies:
            copy.start()
        return copies


def rbf_tables(seg_rows, basis):
    centers = (jnp.arange(basis, dtype=f32) + 0.5) / basis

    def bumps(points):
        return jnp.exp(-0.5 * jnp.square((centers[:, None] - points[None, :]) * basis))

    old_points = 0.75 * centers
    new_points = 0.75 + 0.25 * (jnp.arange(seg_rows, dtype=f32) + 0.5) / seg_rows
    phi_old = bumps(old_points)
    phi_new = bumps(new_points)
    totals = jnp.sum(phi_old, axis=1) + jnp.sum(phi_new, axis=1)
    recon = bumps(centers)
    recon = recon / jnp.sum(recon, axis=0, keepdims=True)
    carry_table = jnp.dot(phi_old, recon.T, precision=lax.Precision.HIGH) / totals[:, None]
    fresh_table = phi_new / totals[:, None]
    return (carry_table, fresh_table)


def standardize(values):
    center = values - jnp.mean(values, axis=-1, keepdims=True)
    spread = jnp.mean(center * center, axis=-1, keepdims=True)
    scale = lax.rsqrt(spread + epsilon)
    return (center * scale, scale)


def norm_back(grad, gain, unit, scale):
    inner = grad * gain
    shift = jnp.mean(inner, axis=-1, keepdims=True)
    slope = jnp.mean(inner * unit, axis=-1, keepdims=True)
    return (inner - shift - unit * slope) * scale


def gate(values, after):
    count = len(values)

    def kernel(*refs):
        pass

    return pl.pallas_call(
        kernel,
        out_shape=[shape(v.shape, v.dtype) for v in values],
        in_specs=[hbm()] * (count + len(after)),
        out_specs=[hbm()] * count,
        input_output_aliases={k: k for k in range(count)},
        name="gate",
    )(*values, *after)


def pack(pieces, width, least, after=()):
    rows = max(sum(v.size for v in pieces) // width, least)

    def kernel(*refs):
        value = [ref[...].astype(f32) for ref in refs[:-1]]
        value = [
            v[:, k * width : (k + 1) * width] for v in value for k in range(v.shape[1] // width)
        ]
        value = jnp.concatenate(value, axis=0).astype(bf16)
        refs[-1][: value.shape[0]] = value
        if value.shape[0] < rows:
            refs[-1][value.shape[0] :] = jnp.zeros((rows - value.shape[0], width), bf16)

    return call(
        kernel,
        shape((rows, width), bf16),
        in_specs=[fixed(v.shape) for v in pieces],
        out_specs=fixed((rows, width)),
        name="pack",
        flops=rows * width,
        traffic=4 * rows * width,
        after=after,
    )(*pieces)


def regroup(deep, packed, first, height, blocks, segments, after=()):
    step, unit = packed.shape[0] // deep, packed.shape[1]
    rows, width = segments * deep * height, blocks * unit

    def kernel(packed_ref, target_ref):
        out = []
        for segment in range(segments):
            for z in range(deep):
                at = z * step + first + segment * blocks * height
                row = [
                    packed_ref[at + k * height : at + (k + 1) * height].astype(f32)
                    for k in range(blocks)
                ]
                out.append(jnp.concatenate(row, axis=1))
        target_ref[...] = jnp.concatenate(out, axis=0).astype(bf16)

    return call(
        kernel,
        shape((rows, width), bf16),
        in_specs=[fixed(packed.shape)],
        out_specs=fixed((rows, width)),
        name="regroup",
        flops=rows * width,
        traffic=4 * rows * width,
        after=after,
    )(packed)


def unpack(links, parts, width):
    line_rows = width // links.outer
    at = parts[0].shape[1] // 128 - 1

    def kernel(*refs):
        parts, (rows_ref, cols_ref) = refs[: links.outer], refs[links.outer :]
        outer = lax.axis_index("dp")
        for k, part in enumerate(parts):
            spot = pl.multiple_of((outer ^ k) * line_rows, 8)
            cols_ref[pl.ds(spot, line_rows)] = part[...].astype(f32)
        rows_ref[...] = cols_ref[...].T[:16]

    return call(
        kernel,
        (shape((16, width), f32), shape((width, 128), f32)),
        in_specs=[spec((line_rows, 128), lambda i: (0, at))] * links.outer,
        out_specs=(fixed((16, width)), fixed((width, 128))),
        name="unpack",
        flops=width * 128,
        traffic=8 * width * 128,
    )(*parts)


def project(links, tokens, memories, memory_low, vectors, group, parts, after=()):
    batch, rows, width = tokens.shape
    line_rows = width // links.outer
    wide = width // GROUPS
    leads = [v for memory in memories for v in memory] if memory_low is None else [memory_low]
    basis = leads[0].shape[-2]
    mine = slice(group * wide, (group + 1) * wide)

    def kernel(tokens_ref, vec_ref, *refs):
        lead, refs = refs[: len(leads)], refs[len(leads) :]
        parts, refs = refs[: links.outer], refs[links.outer :]
        q_ref, k_ref, v_ref = refs[:3]
        weight, sems = refs[-2:]
        step = pl.program_id(0)

        @pl.when(step == 0)
        def _():
            for copy in links.load(parts, line_rows, 0, weight, sems):
                copy.wait()

        vec = vec_ref[...]
        if memory_low is None:
            unit_ref, low_ref = refs[3:5]
            at = 0
            for m, memory in enumerate(memories):

                @pl.when(step == m)
                def _(at=at, memory=memory):
                    value = lead[at][...]
                    if len(memory) > 1:
                        value = value + lead[at + 1][...] * vec[0:1] + lead[at + 2][...] * vec[1:2]
                    low_ref[0] = value.astype(bf16)

                at += len(memory)
        else:
            low_ref = lead[0]
        unit, _ = standardize(tokens_ref[0].astype(f32))
        normed = (unit * vec[0:1] + vec[1:2]).astype(bf16)
        if memory_low is None:
            unit_ref[0] = unit.astype(bf16)
        memory = low_ref[0]
        q_ref[0] = ((dot(normed, weight[:, :wide]) + vec[2:3, mine]) * 0.125).astype(bf16)
        k_ref[0, :rows] = dot(normed, weight[:, wide : 2 * wide]).astype(bf16)
        v_ref[0, :rows] = (dot(normed, weight[:, 2 * wide :]) + vec[3:4, mine]).astype(bf16)
        k_ref[0, rows:] = dot(memory, weight[:, wide : 2 * wide]).astype(bf16)
        v_ref[0, rows:] = (dot(memory, weight[:, 2 * wide :]) + vec[3:4, mine]).astype(bf16)

    keys = rows + basis
    one = lambda r, w: spec((1, r, w), lambda m: (m, 0, 0))
    kinds = [(rows, wide), (keys, wide), (keys, wide)]
    if memory_low is None:
        kinds += [(rows, width), (basis, width)]
        lead_specs = [fixed(v.shape) for v in leads]
    else:
        lead_specs = [one(basis, width)]
    return call(
        kernel,
        tuple(shape((batch, r, w), bf16) for r, w in kinds),
        grid=(batch,),
        in_specs=[one(rows, width), fixed(vectors.shape)] + lead_specs + [hbm()] * links.outer,
        out_specs=tuple(one(r, w) for r, w in kinds),
        scratch=[pltpu.VMEM((width, 3 * wide), bf16), pltpu.SemaphoreType.DMA((links.outer,))],
        name="project",
        flops=2 * batch * width * wide * (3 * rows + 2 * basis),
        traffic=2 * (batch * width * 8 * rows + 3 * width * wide),
        after=after,
    )(tokens, vectors, *leads, *parts)


def lanes(head):
    lane = lax.broadcasted_iota(jnp.int32, (1, PAIR), 1)
    return (lane // HD == head, (lane == (1 - head) * HD))


def attend(queries, keys, values, starts_col, starts_row, after=()):
    batch, rows, width = queries.shape
    total = keys.shape[1]
    heads = width // HD
    half = rows // 2

    def kernel(q_ref, k_ref, v_ref, col_ref, row_ref, mix_ref, inv_ref, e_ref, mask):
        @pl.when(pl.program_id(1) == 0)
        def _():
            i = lax.broadcasted_iota(jnp.int32, (rows, rows), 0)
            j = lax.broadcasted_iota(jnp.int32, (rows, rows), 1)
            allowed = (j <= i) & (col_ref[0] == row_ref[0])
            mask[...] = jnp.where(allowed, 0.0, hidden_score)

        q, k, v = q_ref[0], k_ref[0], v_ref[0]
        memory_bias = jnp.where(col_ref[0] == 0, 0.0, hidden_score).astype(bf16)
        outs = []
        for head in range(2):
            inside, first = lanes(head)
            qh = jnp.where(inside, q, jnp.where(first, memory_bias, 0).astype(bf16))
            kl = jnp.where(inside, k[:rows], 0).astype(bf16)
            km = jnp.where(inside, k[rows:], jnp.where(first, 1, 0).astype(bf16))
            vh = jnp.where(inside, v, 1).astype(bf16)
            parts = []
            for block in range(2):
                top, wide = block * half, (block + 1) * half
                here = qh[top : top + half]
                sl = dot_right(here, kl[:wide]) + mask[top : top + half, :wide]
                sm = dot_right(here, km)
                peak = jnp.maximum(
                    jnp.max(sl, axis=-1, keepdims=True), jnp.max(sm, axis=-1, keepdims=True)
                )
                el = jnp.exp(sl - peak).astype(bf16)
                em = jnp.exp(sm - peak).astype(bf16)
                e_ref[0, head, top : top + half, :wide] = el
                e_ref[0, head, top : top + half, rows:] = em
                parts.append(dot(el, vh[:wide]) + dot(em, vh[rows:]))
            outs.append(jnp.concatenate(parts, axis=0))
        inside, _ = lanes(0)
        mixed = jnp.where(inside, outs[0], outs[1])
        inverse = 1.0 / pltpu.roll(jnp.where(inside, outs[1], outs[0]), HD, 1)
        mix_ref[0] = (mixed * inverse).astype(bf16)
        inv_ref[0] = inverse

    pair = lambda r: spec((1, r, PAIR), lambda m, p: (m, 0, p))
    return call(
        kernel,
        (
            shape((batch, rows, width), bf16),
            shape((batch, rows, width), f32),
            shape((batch, heads, rows, total), bf16),
        ),
        grid=(batch, heads // 2),
        in_specs=[
            pair(rows),
            pair(total),
            pair(total),
            spec((1, rows, 1), lambda m, p: (m, 0, 0)),
            spec((1, 1, rows), lambda m, p: (m, 0, 0)),
        ],
        out_specs=(
            pair(rows),
            pair(rows),
            spec((1, 2, rows, total), lambda m, p: (m, p, 0, 0)),
        ),
        scratch=[pltpu.VMEM((rows, rows), f32)],
        name="attend",
        flops=16 * batch * heads * rows * total * HD,
        traffic=2 * batch * heads * rows * total,
        exps=batch * heads * rows * total,
        after=after,
    )(queries, keys, values, starts_col, starts_row)


def attend_back(queries, keys, values, exps, mixture, scaled, base, count, after=()):
    batch, rows, width = queries.shape
    total = keys.shape[1]
    half = rows // 2

    def kernel(q_ref, k_ref, v_ref, e_ref, mix_ref, g_ref, dq_ref, dk_ref, dv_ref):
        q, k, v, g = q_ref[0], k_ref[0], v_ref[0], g_ref[0]
        product = -(g.astype(f32) * mix_ref[0].astype(f32))
        product = pltpu.roll(product, HD, 1).astype(bf16)
        dqs, dks, dvs = [], [], []
        for head in range(2):
            inside, _ = lanes(head)
            gh = jnp.where(inside, g, product)
            vh = jnp.where(inside, v, 1).astype(bf16)
            near = (e_ref[0, head, :, :half].astype(f32) * dot_right(gh, vh[:half])).astype(bf16)
            late = e_ref[0, head, half:, half:rows].astype(f32) * dot_right(gh[half:], vh[half:rows])
            late = late.astype(bf16)
            far = (e_ref[0, head, :, rows:].astype(f32) * dot_right(gh, vh[rows:])).astype(bf16)
            mixed = dot(near, k[:half]) + dot(far, k[rows:])
            dqs.append(
                jnp.concatenate([mixed[:half], mixed[half:] + dot(late, k[half:rows])], axis=0)
            )
            e = e_ref[0, head]
            dks.append(
                [
                    dot_left(near, q),
                    dot_left(late, q[half:]),
                    dot_left(far, q),
                ]
            )
            dvs.append(
                [
                    dot_left(e[:, :half], g),
                    dot_left(e[half:, half:rows], g[half:]),
                    dot_left(e[:, rows:], g),
                ]
            )
        inside, _ = lanes(0)
        dq_ref[0] = (jnp.where(inside, dqs[0], dqs[1]) * 0.125).astype(bf16)
        for ref, pieces in ((dk_ref, dks), (dv_ref, dvs)):
            for i, (lo, hi) in enumerate(((0, half), (half, rows), (rows, total))):
                ref[0, lo:hi] = jnp.where(inside, pieces[0][i], pieces[1][i]).astype(bf16)

    pair = lambda r: spec((1, r, PAIR), lambda m, p: (m, 0, p + base))
    out = lambda r: spec((1, r, PAIR), lambda m, p: (m, 0, p))
    return call(
        kernel,
        (
            shape((batch, rows, count * PAIR), bf16),
            shape((batch, total, count * PAIR), bf16),
            shape((batch, total, count * PAIR), bf16),
        ),
        grid=(batch, count),
        in_specs=[
            pair(rows),
            pair(total),
            pair(total),
            spec((1, 2, rows, total), lambda m, p: (m, p + base, 0, 0)),
            pair(rows),
            pair(rows),
        ],
        out_specs=(out(rows), out(total), out(total)),
        name="attend_back",
        flops=64 * batch * count * rows * total * HD,
        traffic=4 * batch * count * rows * total,
        after=after,
    )(queries, keys, values, exps, mixture, scaled)


def tops(links, parts, rows, out_w, up_w, sems):
    copies = links.load(parts, rows, 0, out_w, sems)
    for j in range(up_w.shape[0]):
        copies += links.load(parts, rows, (1 + j) * rows, up_w.at[j], sems, (1 + j) * links.outer)
    return copies


def lift(links, tokens, cot, mixture, vectors, up_bias, second, hidden, after=()):
    rows, width = tokens.shape
    fold = hidden // width
    line_rows = width // links.outer
    block = hidden // links.outer
    step = 256
    steps = rows // step

    def kernel(x_ref, cot_ref, mix_ref, vec_ref, bias_ref, *refs):
        parts, refs = refs[: links.outer], refs[links.outer :]
        res_ref, n_ref, act_ref, slope_ref, send_ref, keep_ref, acts, out_w, up_w, sems = refs
        at = pl.program_id(0)

        @pl.when(at < steps)
        def _():
            @pl.when(at == 0)
            def _():
                for copy in tops(links, parts, line_rows, out_w, up_w, sems):
                    copy.wait()

            residual = x_ref[...].astype(f32) + vec_ref[4:5] + dot(mix_ref[...], out_w[...])
            res_ref[...] = residual
            unit, _ = standardize(residual)
            normed = (unit * vec_ref[5:6] + vec_ref[6:7]).astype(bf16)
            n_ref[...] = normed
            here = pl.ds(pl.multiple_of(at * step, step), step)
            for j in range(fold):
                cols = slice(j * width, (j + 1) * width)
                u = dot(normed, up_w[j]) + bias_ref[:, cols]
                c0 = 0.7978845608028654
                square = u * u
                t = jnp.tanh(u * (c0 + (c0 * 0.044715) * square))
                half_up = 0.5 + 0.5 * t
                low = (u * half_up).astype(bf16)
                act_ref[:, cols] = low
                acts[j, here] = low
                slope = half_up + (u * (c0 + (3 * c0 * 0.044715) * square)) * (half_up * (1.0 - t))
                slope_ref[:, cols] = slope.astype(bf16)

        for j in range(fold):

            @pl.when(at == steps + j)
            def _(j=j):
                split_rows(dot_left(acts[j], cot_ref[...]), send_ref, keep_ref)

    early = lambda w: spec((step, w), lambda i: (jnp.minimum(i, steps - 1), 0))
    late = spec((width // (2 * block), block, width), lambda i: (jnp.maximum(i - steps, 0), 0, 0))
    return call(
        kernel,
        (
            shape((rows, width), f32),
            shape((rows, width), bf16),
            shape((rows, hidden), bf16),
            shape((rows, hidden), bf16),
        )
        + (shape((links.across, block, width), bf16),) * 2,
        grid=(steps + fold,),
        in_specs=[
            early(width),
            fixed((rows, width)),
            early(width),
            fixed(vectors.shape),
            fixed(up_bias.shape),
        ]
        + [hbm()] * links.outer,
        out_specs=(early(width), early(width), early(hidden), early(hidden), late, late),
        scratch=[
            pltpu.VMEM((fold, rows, width), bf16),
            pltpu.VMEM((width, width), bf16),
            pltpu.VMEM((fold, width, width), bf16),
            pltpu.SemaphoreType.DMA(((1 + fold) * links.outer,)),
        ],
        name="lift",
        flops=2 * rows * width * (width + 2 * hidden),
        traffic=4 * rows * hidden + 10 * rows * width,
        exps=rows * hidden,
        after=after,
    )(tokens, cot, mixture, vectors, up_bias, *second)


def settle(links, residual, slopes, cot, inverse, mixture, normed2, vectors, second, third, hidden, after=()):
    rows, width = residual.shape
    fold = hidden // width
    line_rows = width // links.outer
    step = 256
    steps = rows // step

    def kernel(res_ref, slope_ref, cot_ref, inv_ref, mix_ref, n_ref, vec_ref, *refs):
        parts, refs = refs[: links.outer], refs[links.outer :]
        lasts, refs = refs[: links.outer], refs[links.outer :]
        ag_ref, mg_ref, sums_ref, ub_ref, send_ref, keep_ref = refs[:6]
        ups, ags, out_w, up_w, down_w, sems = refs[6:]
        at = pl.program_id(0)

        @pl.when(at < steps)
        def _():
            @pl.when(at == 0)
            def _():
                copies = links.load(lasts, fold * line_rows, 0, down_w, sems, (1 + fold) * links.outer)
                copies += tops(links, parts, line_rows, out_w, up_w, sems)
                for copy in copies:
                    copy.wait()
                sums_ref[...] = jnp.zeros_like(sums_ref)
                ub_ref[...] = jnp.zeros_like(ub_ref)

            residual = res_ref[...]
            cot = cot_ref[...]
            cot_f = cot.astype(f32)
            into = jnp.zeros((step, width), f32)
            here = pl.ds(pl.multiple_of(at * step, step), step)
            for j in range(fold):
                cols = slice(j * width, (j + 1) * width)
                grad = dot_right(cot, down_w[cols, :]) * slope_ref[:, cols].astype(f32)
                low = grad.astype(bf16)
                ups[j, here] = low
                ub_ref[0:1, cols] += jnp.sum(grad, axis=0, keepdims=True)
                into += dot_right(low, up_w[j])
            unit, scale = standardize(residual)
            residual_grad = cot_f + norm_back(into, vec_ref[5:6], unit, scale)
            low = residual_grad.astype(bf16)
            ag_ref[...] = low
            ags[here] = low
            mg_ref[...] = (dot_right(low, out_w[...]) * inv_ref[...]).astype(bf16)
            total = lambda v: jnp.sum(v, axis=0, keepdims=True)
            sums_ref[4:5] += total(residual_grad)
            sums_ref[5:6] += total(into * unit)
            sums_ref[6:7] += total(into)
            sums_ref[7:8] += total(cot_f)

        for j in range(fold):

            @pl.when(at == steps + j)
            def _(j=j):
                split_rows(dot_left(n_ref[...], ups[j]), send_ref, keep_ref)

        @pl.when(at == steps + fold)
        def _():
            split_rows(dot_left(mix_ref[...], ags[...]), send_ref, keep_ref)

    early = lambda w: spec((step, w), lambda i: (jnp.minimum(i, steps - 1), 0))
    late = spec((links.across, line_rows, width), lambda i: (0, 0, jnp.maximum(i - steps, 0)))
    return call(
        kernel,
        (shape((rows, width), bf16),) * 2
        + (shape((8, width), f32), shape((8, hidden), f32))
        + (shape((links.across, line_rows, width + hidden), bf16),) * 2,
        grid=(steps + fold + 1,),
        in_specs=[
            early(width),
            early(hidden),
            early(width),
            early(width),
            fixed((rows, width)),
            fixed((rows, width)),
            fixed(vectors.shape),
        ]
        + [hbm()] * (2 * links.outer),
        out_specs=(early(width),) * 2 + (fixed((8, width)), fixed((8, hidden)), late, late),
        scratch=[
            pltpu.VMEM((fold, rows, width), bf16),
            pltpu.VMEM((rows, width), bf16),
            pltpu.VMEM((width, width), bf16),
            pltpu.VMEM((fold, width, width), bf16),
            pltpu.VMEM((hidden, width), bf16),
            pltpu.SemaphoreType.DMA(((2 + fold) * links.outer,)),
        ],
        name="settle",
        flops=2 * rows * width * (2 * width + 3 * hidden),
        traffic=2 * rows * hidden + 14 * rows * width,
        after=after,
    )(residual, slopes, cot, inverse, mixture, normed2, vectors, *second, *third)


def emit(links, residual, activated, vectors, third, after=()):
    rows, width = residual.shape
    hidden = activated.shape[1]
    line_rows = hidden // links.outer
    step = 256

    def kernel(res_ref, act_ref, vec_ref, *refs):
        parts, (y_ref, down_w, sems) = refs[: links.outer], refs[links.outer :]

        @pl.when(pl.program_id(0) == 0)
        def _():
            for copy in links.load(parts, line_rows, 0, down_w, sems):
                copy.wait()

        y_ref[...] = (res_ref[...] + dot(act_ref[...], down_w[...]) + vec_ref[7:8]).astype(bf16)

    one = lambda w: spec((step, w), lambda i: (i, 0))
    return call(
        kernel,
        shape((rows, width), bf16),
        grid=(rows // step,),
        in_specs=[one(width), one(hidden), fixed(vectors.shape)] + [hbm()] * links.outer,
        out_specs=one(width),
        scratch=[pltpu.VMEM((hidden, width), bf16), pltpu.SemaphoreType.DMA((links.outer,))],
        name="emit",
        flops=2 * rows * width * hidden,
        traffic=2 * rows * hidden + 6 * rows * width,
        after=after,
    )(residual, activated, vectors, *third)


def finish(links, tokens, attn_grad, groups, vectors, first, after=()):
    batch, rows, width = tokens.shape
    line_rows = width // links.outer
    wide = width // BACK
    step = rows // 2

    def kernel(x_ref, ag_ref, vec_ref, *refs):
        grads, refs = refs[: 3 * BACK], refs[3 * BACK :]
        parts, refs = refs[: links.outer], refs[links.outer :]
        tg_ref, weight, sems = refs

        @pl.when((pl.program_id(0) == 0) & (pl.program_id(1) == 0))
        def _():
            for copy in links.load(parts, line_rows, 0, weight, sems):
                copy.wait()

        grad = jnp.zeros((step, width), f32)
        for g in range(BACK):
            for kind in range(3):
                at = kind * width + g * wide
                grad += dot_right(grads[3 * g + kind][0], weight[:, at : at + wide])
        unit, scale = standardize(x_ref[0].astype(f32))
        tokens_grad = ag_ref[0].astype(f32) + norm_back(grad, vec_ref[0:1], unit, scale)
        tg_ref[0] = tokens_grad.astype(bf16)

    one = lambda w: spec((1, step, w), lambda m, i: (m, i, 0))
    return call(
        kernel,
        shape((batch, rows, width), bf16),
        grid=(batch, rows // step),
        in_specs=[one(width), one(width), fixed(vectors.shape)]
        + [one(wide)] * (3 * BACK)
        + [hbm()] * (links.outer),
        out_specs=one(width),
        scratch=[
            pltpu.VMEM((width, 3 * width), bf16),
            pltpu.SemaphoreType.DMA((links.outer,)),
        ],
        name="finish",
        flops=6 * batch * rows * width * width,
        traffic=12 * batch * rows * width,
        after=after,
    )(
        tokens,
        attn_grad,
        vectors,
        *[v for group in groups for v in group],
        *first,
    )


def split_rows(value, send_ref, keep_ref):
    core = lax.axis_index("dp") % 2
    groups, block, _ = send_ref.shape
    for a in range(groups):
        low = value[2 * a * block : (2 * a + 1) * block]
        high = value[(2 * a + 1) * block : (2 * a + 2) * block]
        send_ref[a] = jnp.where(core == 0, high, low).astype(bf16)
        keep_ref[a] = jnp.where(core == 0, low, high).astype(bf16)


def qkv_grads(links, units, memory_low, groups, first, columns, sums, after=()):
    batch, rows, width = units.shape
    total = groups[0][1].shape[1]
    wide = width // BACK
    block = width // links.outer
    basis = memory_low.shape[1]

    def kernel(u_ref, mem_ref, col_ref, sum_ref, *refs):
        grads, refs = refs[: 3 * BACK], refs[3 * BACK :]
        parts, refs = refs[: links.outer], refs[links.outer :]
        send_ref, keep_ref, send_more, keep_more, weight, ends, lines, sems = refs
        step = pl.program_id(0)
        lane = lax.broadcasted_iota(jnp.int32, (1, 128), 1)
        across = lambda v: jnp.sum(v, axis=1, keepdims=True)
        down = lambda v: jnp.sum(v.astype(f32), axis=0, keepdims=True)
        for at in range(3 * BACK):
            kind, g = at // BACK, at % BACK
            mine = slice(g * wide, (g + 1) * wide)

            @pl.when(step == at)
            def _(at=at, kind=kind, g=g, mine=mine):
                if at == 0:
                    copies = links.load(parts, block, 0, weight, sems)
                    lines[...] = jnp.zeros_like(lines)
                    lines[0:16] = sum_ref[...]
                    ends[...] = jnp.zeros_like(ends)
                ref = grads[3 * g + kind]
                value = sum(dot_left(u_ref[m], ref[m, :rows]) for m in range(batch))
                line = sum(down(ref[m, :rows]) for m in range(batch))
                if at == 0:
                    for copy in copies:
                        copy.wait()
                w = weight[:, kind * width + g * wide : kind * width + (g + 1) * wide].astype(f32)
                ends[...] += jnp.where(
                    lane == 0, across(w * value), jnp.where(lane == 1, across(w * line), 0.0)
                )
                value = col_ref[:, 0:1] * value + col_ref[:, 1:2] * line
                if kind:
                    value += sum(dot_left(mem_ref[m], ref[m, rows:]) for m in range(batch))
                if kind == 0:
                    lines[2:3, mine] = line
                if kind == 2:
                    lines[3:4, mine] = line + sum(down(ref[m, rows:]) for m in range(batch))
                split_rows(value, send_ref, keep_ref)

        @pl.when(step == 3 * BACK)
        def _():
            split_rows(lines[...].T + ends[...], send_more, keep_more)

    out = spec((links.across, block, wide), lambda i: (0, 0, jnp.minimum(i, 3 * BACK - 1)))
    more = fixed((links.across, block, 128))
    return call(
        kernel,
        (shape((links.across, block, 3 * width), bf16),) * 2
        + (shape((links.across, block, 128), bf16),) * 2,
        grid=(3 * BACK + 1,),
        in_specs=[
            fixed((batch, rows, width)),
            fixed((batch, basis, width)),
            fixed(columns.shape),
            fixed(sums.shape),
        ]
        + [fixed((batch, rows, wide)), fixed((batch, total, wide)), fixed((batch, total, wide))] * BACK
        + [hbm()] * (links.outer),
        out_specs=(out, out, more, more),
        scratch=[
            pltpu.VMEM((width, 3 * width), bf16),
            pltpu.VMEM((width, 128), f32),
            pltpu.VMEM((128, width), f32),
            pltpu.SemaphoreType.DMA((links.outer,)),
        ],
        name="qkv_grads",
        flops=2 * batch * width * width * (3 * rows + 2 * basis),
        traffic=2 * batch * width * 7 * rows,
        after=after,
    )(
        units,
        memory_low,
        columns,
        sums,
        *[v for group in groups for v in group],
        *first,
    )


def body(links, tokens, cotangent, doc_start, memory_init, *shards):
    (
        norm1_gain,
        norm1_bias,
        qkv_weight,
        query_bias,
        value_bias,
        out_weight,
        out_bias,
        norm2_gain,
        norm2_bias,
        up_weight,
        up_bias,
        down_weight,
        down_bias,
    ) = shards
    own, width = out_weight.shape
    hidden = up_weight.shape[1]
    fold = hidden // width
    n = links.count
    tokens, cotangent, doc_start, memory_init = (
        tokens[:, 0],
        cotangent[:, 0],
        doc_start[:, 0],
        memory_init[0],
    )
    batch, rows, _ = tokens.shape

    small = (norm1_gain, norm1_bias, query_bias, value_bias, out_bias, norm2_gain, norm2_bias, down_bias)
    small = jnp.concatenate([jnp.stack(small).T, up_bias.reshape(own, fold)], axis=1)
    small = jnp.pad(small, ((0, 0), (0, 128 - small.shape[1])))
    wide = width // GROUPS
    positions = jnp.arange(rows)
    before = positions[None, :] <= positions[:, None]
    documents = jnp.sum(jnp.where(before, doc_start[:, None, :], 0), axis=2)
    documents = (documents[:, :, None], documents[:, None, :])

    carry_table, fresh_table = rbf_tables(rows, memory_init.shape[0])
    high = functools.partial(jnp.dot, precision=lax.Precision.HIGH)
    memories = [(memory_init,)]
    carried, gained, biased = memory_init, None, None
    for m in range(batch - 1):
        keep_share = jnp.where(documents[0][m, -1, 0] == 0, 1.0, 0.0)
        unit, _ = standardize(tokens[m].astype(f32))
        table = keep_share * carry_table
        carried = high(table, carried)
        new_gained = high(fresh_table, unit)
        new_biased = jnp.sum(fresh_table, axis=1, keepdims=True)
        if m:
            new_gained += high(table, gained)
            new_biased += high(table, biased)
        gained, biased = new_gained, new_biased
        memories.append((carried, gained, biased))

    flat = lambda v: v.reshape(batch * rows, v.shape[-1])
    full = lambda v: v.reshape(batch, rows, v.shape[-1])
    line = links.line(jnp.concatenate([qkv_weight, small], axis=1), [own])
    early = [v for memory in memories[1:] for v in memory] + list(documents)
    first = links.spread(line, early)
    unit = width // 2
    least = -(-(2**20) // (2 * links.deep * unit))
    packed = pack([out_weight, up_weight, down_weight], unit, -(-least // 16) * 16, after=[line])
    packed = lax.all_gather(packed, "fsdp", axis=0, tiled=True)
    vectors, columns = unpack(links, first, width)
    made = project(links, tokens, memories, None, vectors, 0, first)
    queries, keys, values, units, memory_low = made
    line = regroup(links.deep, packed, 0, own, 2, 1 + fold, after=made[:1])
    mixture, inverse, exps = attend(queries, keys, values, *documents, after=[line])
    second = links.spread(line, [mixture])
    line = regroup(links.deep, packed, 2 * own * (1 + fold), fold * own, 2, 1, after=second)
    up_bias_full = columns[:, 8 : 8 + fold].reshape(1, hidden)
    cot = flat(cotangent)
    made = lift(
        links, flat(tokens), cot, flat(mixture), vectors, up_bias_full, second, hidden, after=[line]
    )
    residual, normed2, activated, slopes = made[:4]
    down_parts = made[4:]
    third = links.spread(line, made[:1])
    made = settle(
        links,
        residual,
        slopes,
        cot,
        flat(inverse),
        flat(mixture),
        normed2,
        vectors,
        second,
        third,
        hidden,
    )
    attn_grad, scaled, sums, up_sums = made[:4]
    up_parts = made[4:]
    down_parts = links.merge_core(*down_parts, after=[attn_grad])
    sums = jnp.concatenate(
        [sums, up_sums[0].reshape(width, fold).T, jnp.zeros((8 - fold, width), f32)], axis=0
    )
    groups = []
    hold = list(down_parts[:1])
    pairs = width // PAIR // BACK
    for g in range(BACK):
        groups.append(
            attend_back(
                queries, keys, values, exps, mixture, full(scaled), g * pairs, pairs, after=hold
            )
        )
        hold = list(groups[-1][:1])
        if g == 0:
            down_total = links.merge_columns(*down_parts, after=hold)
            up_parts = links.merge_core(*up_parts, after=[down_total])
            hold = [up_parts[0]]
    down_grad = links.merge_deep(down_total)
    qkv_parts = qkv_grads(links, units, memory_low, groups, first, columns, sums)
    up_total = links.merge_columns(*up_parts, after=qkv_parts[:1])
    up_grad = links.merge_deep(up_total)
    qkv_parts = links.merge_core(*qkv_parts, after=[up_total, down_grad])
    output = emit(links, residual, activated, vectors, third, after=qkv_parts[:1])
    tokens_grad = finish(links, tokens, full(attn_grad), groups, vectors, first, after=[output])
    qkv_parts = links.merge_line(*qkv_parts, after=[tokens_grad, up_grad])
    qkv_grad = links.merge_depth(*qkv_parts)
    vec = [qkv_grad[:, 3 * width + k] for k in range(8)]
    lead = lambda v: v[:, None]
    return (
        lead(full(output)),
        lead(tokens_grad),
        vec[0],
        vec[1],
        qkv_grad[:, : 3 * width],
        vec[2],
        vec[3],
        up_grad[:, hidden:],
        vec[4],
        vec[5],
        vec[6],
        up_grad[:, :hidden],
        qkv_grad[:, 3 * width + 8 : 3 * width + 8 + fold].reshape(fold * own),
        down_grad,
        vec[7],
    )


def solution(mesh):
    both = ("dp", "fsdp")
    vector, matrix = P(both), P(both, None)
    params = (
        vector,
        vector,
        matrix,
        vector,
        vector,
        matrix,
        vector,
        vector,
        vector,
        matrix,
        vector,
        matrix,
        vector,
    )
    stream = P(None, both, None, None)
    return jax.shard_map(
        functools.partial(body, Links(mesh)),
        mesh=mesh,
        in_specs=(stream, stream, P(None, both, None), P(both, None, None)) + params,
        out_specs=(stream, stream) + params,
        check_vma=False,
    )
```

```python
import functools

import jax
import jax.numpy as jnp
from jax import lax
from jax.experimental import pallas as pl
from jax.experimental.pallas import tpu as pltpu
from jax.sharding import PartitionSpec as P

HD = 64
PAIR = 2 * HD
GROUPS = 1
BACK = 2
epsilon = 1e-05
hidden_score = -1e30
bf16 = jnp.bfloat16
f32 = jnp.float32
VMEM = 60 * 2**20


def dot(left, right):
    return jnp.dot(left, right, preferred_element_type=f32)


def dot_right(left, right):
    return lax.dot_general(left, right, (((1,), (1,)), ((), ())), preferred_element_type=f32)


def dot_left(left, right):
    return lax.dot_general(left, right, (((0,), (0,)), ((), ())), preferred_element_type=f32)


def call(
    kernel,
    out_shape,
    *,
    grid=(1,),
    in_specs,
    out_specs,
    scratch=(),
    name,
    flops,
    traffic,
    exps=0,
    after=(),
):
    count = len(in_specs)

    def run(*refs):
        return kernel(*refs[:count], *refs[count + len(after) :])

    made = pl.pallas_call(
        run,
        out_shape=out_shape,
        grid=grid,
        in_specs=list(in_specs) + [hbm()] * len(after),
        out_specs=out_specs,
        scratch_shapes=list(scratch),
        compiler_params=pltpu.CompilerParams(vmem_limit_bytes=VMEM),
        cost_estimate=pl.CostEstimate(flops=flops, bytes_accessed=traffic, transcendentals=exps),
        name=name,
    )
    return lambda *operands: made(*operands, *after)


def shape(dims, dtype):
    return jax.ShapeDtypeStruct(dims, dtype)


def hbm():
    return pl.BlockSpec(memory_space=pl.ANY)


def spec(block, index):
    return pl.BlockSpec(block, index)


def fixed(dims):
    return pl.BlockSpec(dims, lambda *_: (0,) * len(dims))


class Links:
    def __init__(self, mesh):
        self.outer = mesh.shape["dp"]
        self.across = self.outer // 2
        self.deep = mesh.shape["fsdp"]
        self.count = self.outer * self.deep

    def place(self):
        outer = lax.axis_index("dp")
        return (outer // 2, outer % 2, lax.axis_index("fsdp"))

    def swap(self, value, column=0, core=0, depth=0):
        pairs = []
        for device in range(self.count):
            outer, inner = divmod(device, self.deep)
            target = (((outer // 2) ^ column) * 2 + ((outer % 2) ^ core)) * self.deep + (
                inner ^ depth
            )
            pairs.append((device, target))
        return lax.ppermute(value, ("dp", "fsdp"), pairs)

    def line(self, shard, segments, after=()):
        pieces = [shard] + [self.swap(shard, depth=s) for s in range(1, self.deep)]
        rows, width = shard.shape

        def kernel(*refs):
            target = refs[self.deep]
            depth = lax.axis_index("fsdp")
            values = [ref[...].astype(f32) for ref in refs[: self.deep]]
            turned = []
            for j in range(self.deep):
                value = values[0]
                for s in range(1, self.deep):
                    value = jnp.where(depth == s ^ j, values[s], value)
                turned.append(value)
            out = []
            at = 0
            for count in segments:
                out += [value[at : at + count] for value in turned]
                at += count
            target[...] = jnp.concatenate(out, axis=0).astype(bf16)

        return call(
            kernel,
            shape((self.deep * rows, width), bf16),
            in_specs=[fixed((rows, width))] * self.deep,
            out_specs=fixed((self.deep * rows, width)),
            name="line",
            flops=self.deep**2 * rows * width,
            traffic=4 * self.deep * rows * width,
            after=after,
        )(*pieces)

    def spread(self, line, after=(), along=()):
        lines = [line] + [self.swap(line, column=s) for s in range(1, self.across)]
        extra = []
        if after:
            lines = gate(lines + list(along), after)
            lines, extra = lines[: self.across], lines[self.across :]
        out = []
        for part in lines:
            out += [part, self.swap(part, core=1)]
        return (out, extra) if along else out

    def merge_core(self, send, keep, used=None, after=()):
        across, rows, width = send.shape
        came = self.swap(send, core=1)
        if used is None:
            units = width // 128
            used, tile = width, 128 * max(k for k in range(1, 7) if units % k == 0)
        else:
            tile = used

        def kernel(keep_ref, came_ref, *outs):
            column = lax.axis_index("dp") // 2
            for s in range(across):
                value = keep_ref[column ^ s, :, :tile].astype(f32)
                value = value + came_ref[column ^ s, :, :tile].astype(f32)
                outs[s][...] = value.astype(outs[s].dtype)

        whole = pl.BlockSpec((across, rows, tile if tile < used else width), lambda i: (0, 0, i))
        part = pl.BlockSpec((rows, tile), lambda i: (0, i))
        return call(
            kernel,
            (shape((rows, used), f32),) + (shape((rows, used), bf16),) * (across - 1),
            grid=(used // tile,),
            in_specs=[whole, whole],
            out_specs=(part,) * across,
            name="merge_core",
            flops=across * rows * width,
            traffic=6 * across * rows * width,
            after=after,
        )(keep, came)

    def merge_columns(self, own, *sends, after=()):
        came = [self.swap(sends[s - 1], column=s) for s in range(1, self.across)]
        rows, width = own.shape
        tile = 768 if width % 768 == 0 else 128

        def kernel(own_ref, *refs):
            total = own_ref[...]
            for ref in refs[:-1]:
                total = total + ref[...].astype(f32)
            refs[-1][...] = total

        part = pl.BlockSpec((rows, tile), lambda i: (0, i))
        return call(
            kernel,
            shape((rows, width), f32),
            grid=(width // tile,),
            in_specs=[part] * self.across,
            out_specs=part,
            name="merge_columns",
            flops=self.across * rows * width,
            traffic=14 * rows * width,
            after=after,
        )(own, *came)

    def merge_deep(self, total):
        return lax.psum_scatter(total, "fsdp", scatter_dimension=0, tiled=True)

    def merge_line(self, own, *sends, after=()):
        came = [self.swap(sends[s - 1], column=s) for s in range(1, self.across)]
        rows, width = own.shape
        main = rows // self.deep

        def kernel(own_ref, *refs):
            total = own_ref[...]
            for ref in refs[: self.across - 1]:
                total = total + ref[...].astype(f32)
            outs = refs[self.across - 1 :]
            parts = [total[j * main : (j + 1) * main] for j in range(self.deep)]
            depth = lax.axis_index("fsdp")
            for s in range(self.deep):
                value = parts[0]
                for j in range(1, self.deep):
                    value = jnp.where(depth == s ^ j, parts[j], value)
                outs[s][...] = value.astype(outs[s].dtype)

        return call(
            kernel,
            (shape((main, width), f32),) + (shape((main, width), bf16),) * (self.deep - 1),
            in_specs=[fixed((rows, width))] * self.across,
            out_specs=(fixed((main, width)),) * self.deep,
            name="merge_line",
            flops=(self.across + self.deep) * rows * width,
            traffic=14 * rows * width,
            after=after,
        )(own, *came)

    def merge_depth(self, own, *sends):
        came = [self.swap(sends[s - 1], depth=s) for s in range(1, self.deep)]
        return sum((part.astype(f32) for part in came), own)

    def load(self, parts, rows, at, target, sems, base=0):
        outer = lax.axis_index("dp")
        copies = []
        for k, part in enumerate(parts):
            spot = pl.multiple_of((outer ^ k) * rows, 16)
            copies.append(
                pltpu.make_async_copy(
                    part.at[pl.ds(at, rows), pl.ds(0, target.shape[1])],
                    target.at[pl.ds(spot, rows)],
                    sems.at[base + k],
                )
            )
        for copy in copies:
            copy.start()
        return copies


def rbf_tables(seg_rows, basis):
    centers = (jnp.arange(basis, dtype=f32) + 0.5) / basis

    def bumps(points):
        return jnp.exp(-0.5 * jnp.square((centers[:, None] - points[None, :]) * basis))

    old_points = 0.75 * centers
    new_points = 0.75 + 0.25 * (jnp.arange(seg_rows, dtype=f32) + 0.5) / seg_rows
    phi_old = bumps(old_points)
    phi_new = bumps(new_points)
    totals = jnp.sum(phi_old, axis=1) + jnp.sum(phi_new, axis=1)
    recon = bumps(centers)
    recon = recon / jnp.sum(recon, axis=0, keepdims=True)
    carry_table = jnp.dot(phi_old, recon.T, precision=lax.Precision.HIGH) / totals[:, None]
    fresh_table = phi_new / totals[:, None]
    return (carry_table, fresh_table)


def standardize(values):
    center = values - jnp.mean(values, axis=-1, keepdims=True)
    spread = jnp.mean(center * center, axis=-1, keepdims=True)
    scale = lax.rsqrt(spread + epsilon)
    return (center * scale, scale)


def norm_back(grad, gain, unit, scale):
    inner = grad * gain
    shift = jnp.mean(inner, axis=-1, keepdims=True)
    slope = jnp.mean(inner * unit, axis=-1, keepdims=True)
    return (inner - shift - unit * slope) * scale


def gate(values, after):
    count = len(values)

    def kernel(*refs):
        pass

    return pl.pallas_call(
        kernel,
        out_shape=[shape(v.shape, v.dtype) for v in values],
        in_specs=[hbm()] * (count + len(after)),
        out_specs=[hbm()] * count,
        input_output_aliases={k: k for k in range(count)},
        name="gate",
    )(*values, *after)


def pack(pieces, width, least, after=()):
    rows = max(sum(v.size for v in pieces) // width, least)

    def kernel(*refs):
        value = [ref[...].astype(f32) for ref in refs[:-1]]
        value = [
            v[:, k * width : (k + 1) * width] for v in value for k in range(v.shape[1] // width)
        ]
        value = jnp.concatenate(value, axis=0).astype(bf16)
        refs[-1][: value.shape[0]] = value
        if value.shape[0] < rows:
            refs[-1][value.shape[0] :] = jnp.zeros((rows - value.shape[0], width), bf16)

    return call(
        kernel,
        shape((rows, width), bf16),
        in_specs=[fixed(v.shape) for v in pieces],
        out_specs=fixed((rows, width)),
        name="pack",
        flops=rows * width,
        traffic=4 * rows * width,
        after=after,
    )(*pieces)


def regroup(deep, packed, first, height, blocks, segments, after=()):
    step, unit = packed.shape[0] // deep, packed.shape[1]
    rows, width = segments * deep * height, blocks * unit

    def kernel(packed_ref, target_ref):
        out = []
        for segment in range(segments):
            for z in range(deep):
                at = z * step + first + segment * blocks * height
                row = [
                    packed_ref[at + k * height : at + (k + 1) * height].astype(f32)
                    for k in range(blocks)
                ]
                out.append(jnp.concatenate(row, axis=1))
        target_ref[...] = jnp.concatenate(out, axis=0).astype(bf16)

    return call(
        kernel,
        shape((rows, width), bf16),
        in_specs=[fixed(packed.shape)],
        out_specs=fixed((rows, width)),
        name="regroup",
        flops=rows * width,
        traffic=4 * rows * width,
        after=after,
    )(packed)


def unpack(links, parts, width):
    line_rows = width // links.outer
    at = parts[0].shape[1] // 128 - 1

    def kernel(*refs):
        parts, (rows_ref, cols_ref) = refs[: links.outer], refs[links.outer :]
        outer = lax.axis_index("dp")
        for k, part in enumerate(parts):
            spot = pl.multiple_of((outer ^ k) * line_rows, 8)
            cols_ref[pl.ds(spot, line_rows)] = part[...].astype(f32)
        rows_ref[...] = cols_ref[...].T[:16]

    return call(
        kernel,
        (shape((16, width), f32), shape((width, 128), f32)),
        in_specs=[spec((line_rows, 128), lambda i: (0, at))] * links.outer,
        out_specs=(fixed((16, width)), fixed((width, 128))),
        name="unpack",
        flops=width * 128,
        traffic=8 * width * 128,
    )(*parts)


def project(links, tokens, memories, memory_low, vectors, group, parts, after=()):
    batch, rows, width = tokens.shape
    line_rows = width // links.outer
    wide = width // GROUPS
    leads = [v for memory in memories for v in memory] if memory_low is None else [memory_low]
    basis = leads[0].shape[-2]
    mine = slice(group * wide, (group + 1) * wide)

    def kernel(tokens_ref, vec_ref, *refs):
        lead, refs = refs[: len(leads)], refs[len(leads) :]
        parts, refs = refs[: links.outer], refs[links.outer :]
        q_ref, k_ref, v_ref = refs[:3]
        weight, sems = refs[-2:]
        step = pl.program_id(0)

        @pl.when(step == 0)
        def _():
            for copy in links.load(parts, line_rows, 0, weight, sems):
                copy.wait()

        vec = vec_ref[...]
        if memory_low is None:
            unit_ref, low_ref = refs[3:5]
            at = 0
            for m, memory in enumerate(memories):

                @pl.when(step == m)
                def _(at=at, memory=memory):
                    value = lead[at][...]
                    if len(memory) > 1:
                        value = value + lead[at + 1][...] * vec[0:1] + lead[at + 2][...] * vec[1:2]
                    low_ref[0] = value.astype(bf16)

                at += len(memory)
        else:
            low_ref = lead[0]
        unit, _ = standardize(tokens_ref[0].astype(f32))
        normed = (unit * vec[0:1] + vec[1:2]).astype(bf16)
        if memory_low is None:
            unit_ref[0] = unit.astype(bf16)
        memory = low_ref[0]
        q_ref[0] = ((dot(normed, weight[:, :wide]) + vec[2:3, mine]) * 0.125).astype(bf16)
        k_ref[0, :rows] = dot(normed, weight[:, wide : 2 * wide]).astype(bf16)
        v_ref[0, :rows] = (dot(normed, weight[:, 2 * wide :]) + vec[3:4, mine]).astype(bf16)
        k_ref[0, rows:] = dot(memory, weight[:, wide : 2 * wide]).astype(bf16)
        v_ref[0, rows:] = (dot(memory, weight[:, 2 * wide :]) + vec[3:4, mine]).astype(bf16)

    keys = rows + basis
    one = lambda r, w: spec((1, r, w), lambda m: (m, 0, 0))
    kinds = [(rows, wide), (keys, wide), (keys, wide)]
    if memory_low is None:
        kinds += [(rows, width), (basis, width)]
        lead_specs = [fixed(v.shape) for v in leads]
    else:
        lead_specs = [one(basis, width)]
    return call(
        kernel,
        tuple(shape((batch, r, w), bf16) for r, w in kinds),
        grid=(batch,),
        in_specs=[one(rows, width), fixed(vectors.shape)] + lead_specs + [hbm()] * links.outer,
        out_specs=tuple(one(r, w) for r, w in kinds),
        scratch=[pltpu.VMEM((width, 3 * wide), bf16), pltpu.SemaphoreType.DMA((links.outer,))],
        name="project",
        flops=2 * batch * width * wide * (3 * rows + 2 * basis),
        traffic=2 * (batch * width * 8 * rows + 3 * width * wide),
        after=after,
    )(tokens, vectors, *leads, *parts)


def lanes(head):
    lane = lax.broadcasted_iota(jnp.int32, (1, PAIR), 1)
    return (lane // HD == head, (lane == (1 - head) * HD))


def attend(queries, keys, values, starts_col, starts_row, after=()):
    batch, rows, width = queries.shape
    total = keys.shape[1]
    heads = width // HD
    half = rows // 2

    def kernel(q_ref, k_ref, v_ref, col_ref, row_ref, mix_ref, inv_ref, e_ref, mask):
        @pl.when(pl.program_id(1) == 0)
        def _():
            i = lax.broadcasted_iota(jnp.int32, (rows, rows), 0)
            j = lax.broadcasted_iota(jnp.int32, (rows, rows), 1)
            allowed = (j <= i) & (col_ref[0] == row_ref[0])
            mask[...] = jnp.where(allowed, 0.0, hidden_score)

        q, k, v = q_ref[0], k_ref[0], v_ref[0]
        memory_bias = jnp.where(col_ref[0] == 0, 0.0, hidden_score).astype(bf16)
        outs = []
        for head in range(2):
            inside, first = lanes(head)
            qh = jnp.where(inside, q, jnp.where(first, memory_bias, 0).astype(bf16))
            kl = jnp.where(inside, k[:rows], 0).astype(bf16)
            km = jnp.where(inside, k[rows:], jnp.where(first, 1, 0).astype(bf16))
            vh = jnp.where(inside, v, 1).astype(bf16)
            parts = []
            for block in range(2):
                top, wide = block * half, (block + 1) * half
                here = qh[top : top + half]
                sl = dot_right(here, kl[:wide]) + mask[top : top + half, :wide]
                sm = dot_right(here, km)
                peak = jnp.maximum(
                    jnp.max(sl, axis=-1, keepdims=True), jnp.max(sm, axis=-1, keepdims=True)
                )
                el = jnp.exp(sl - peak).astype(bf16)
                em = jnp.exp(sm - peak).astype(bf16)
                e_ref[0, head, top : top + half, :wide] = el
                e_ref[0, head, top : top + half, rows:] = em
                parts.append(dot(el, vh[:wide]) + dot(em, vh[rows:]))
            outs.append(jnp.concatenate(parts, axis=0))
        inside, _ = lanes(0)
        mixed = jnp.where(inside, outs[0], outs[1])
        inverse = 1.0 / pltpu.roll(jnp.where(inside, outs[1], outs[0]), HD, 1)
        mix_ref[0] = (mixed * inverse).astype(bf16)
        inv_ref[0] = inverse

    pair = lambda r: spec((1, r, PAIR), lambda m, p: (m, 0, p))
    return call(
        kernel,
        (
            shape((batch, rows, width), bf16),
            shape((batch, rows, width), f32),
            shape((batch, heads, rows, total), bf16),
        ),
        grid=(batch, heads // 2),
        in_specs=[
            pair(rows),
            pair(total),
            pair(total),
            spec((1, rows, 1), lambda m, p: (m, 0, 0)),
            spec((1, 1, rows), lambda m, p: (m, 0, 0)),
        ],
        out_specs=(
            pair(rows),
            pair(rows),
            spec((1, 2, rows, total), lambda m, p: (m, p, 0, 0)),
        ),
        scratch=[pltpu.VMEM((rows, rows), f32)],
        name="attend",
        flops=16 * batch * heads * rows * total * HD,
        traffic=2 * batch * heads * rows * total,
        exps=batch * heads * rows * total,
        after=after,
    )(queries, keys, values, starts_col, starts_row)


def attend_back(queries, keys, values, exps, mixture, scaled, base, count, after=()):
    batch, rows, width = queries.shape
    total = keys.shape[1]
    half = rows // 2

    def kernel(q_ref, k_ref, v_ref, e_ref, mix_ref, g_ref, dq_ref, dk_ref, dv_ref):
        q, k, v, g = q_ref[0], k_ref[0], v_ref[0], g_ref[0]
        product = -(g.astype(f32) * mix_ref[0].astype(f32))
        product = pltpu.roll(product, HD, 1).astype(bf16)
        dqs, dks, dvs = [], [], []
        for head in range(2):
            inside, _ = lanes(head)
            gh = jnp.where(inside, g, product)
            vh = jnp.where(inside, v, 1).astype(bf16)
            near = (e_ref[0, head, :, :half].astype(f32) * dot_right(gh, vh[:half])).astype(bf16)
            late = e_ref[0, head, half:, half:rows].astype(f32) * dot_right(gh[half:], vh[half:rows])
            late = late.astype(bf16)
            far = (e_ref[0, head, :, rows:].astype(f32) * dot_right(gh, vh[rows:])).astype(bf16)
            mixed = dot(near, k[:half]) + dot(far, k[rows:])
            dqs.append(
                jnp.concatenate([mixed[:half], mixed[half:] + dot(late, k[half:rows])], axis=0)
            )
            e = e_ref[0, head]
            dks.append(
                [
                    dot_left(near, q),
                    dot_left(late, q[half:]),
                    dot_left(far, q),
                ]
            )
            dvs.append(
                [
                    dot_left(e[:, :half], g),
                    dot_left(e[half:, half:rows], g[half:]),
                    dot_left(e[:, rows:], g),
                ]
            )
        inside, _ = lanes(0)
        dq_ref[0] = (jnp.where(inside, dqs[0], dqs[1]) * 0.125).astype(bf16)
        for ref, pieces in ((dk_ref, dks), (dv_ref, dvs)):
            for i, (lo, hi) in enumerate(((0, half), (half, rows), (rows, total))):
                ref[0, lo:hi] = jnp.where(inside, pieces[0][i], pieces[1][i]).astype(bf16)

    pair = lambda r: spec((1, r, PAIR), lambda m, p: (m, 0, p + base))
    out = lambda r: spec((1, r, PAIR), lambda m, p: (m, 0, p))
    return call(
        kernel,
        (
            shape((batch, rows, count * PAIR), bf16),
            shape((batch, total, count * PAIR), bf16),
            shape((batch, total, count * PAIR), bf16),
        ),
        grid=(batch, count),
        in_specs=[
            pair(rows),
            pair(total),
            pair(total),
            spec((1, 2, rows, total), lambda m, p: (m, p + base, 0, 0)),
            pair(rows),
            pair(rows),
        ],
        out_specs=(out(rows), out(total), out(total)),
        name="attend_back",
        flops=64 * batch * count * rows * total * HD,
        traffic=4 * batch * count * rows * total,
        after=after,
    )(queries, keys, values, exps, mixture, scaled)


def tops(links, parts, rows, out_w, up_w, sems):
    copies = links.load(parts, rows, 0, out_w, sems)
    for j in range(up_w.shape[0]):
        copies += links.load(parts, rows, (1 + j) * rows, up_w.at[j], sems, (1 + j) * links.outer)
    return copies


def wait(copies):
    for copy in copies:
        copy.wait()


def lift(links, tokens, cot, mixture, vectors, up_bias, second, hidden, after=()):
    rows, width = tokens.shape
    fold = hidden // width
    line_rows = width // links.outer
    block = hidden // links.outer
    step = 256
    steps = rows // step

    def kernel(x_ref, cot_ref, mix_ref, vec_ref, bias_ref, *refs):
        parts, refs = refs[: links.outer], refs[links.outer :]
        res_ref, n_ref, act_ref, slope_ref, send_ref, keep_ref, acts, out_w, up_w, sems = refs
        at = pl.program_id(0)

        @pl.when(at < steps)
        def _():
            @pl.when(at == 0)
            def _():
                wait(tops(links, parts, line_rows, out_w, up_w, sems))

            residual = x_ref[...].astype(f32) + vec_ref[4:5] + dot(mix_ref[...], out_w[...])
            res_ref[...] = residual
            unit, _ = standardize(residual)
            normed = (unit * vec_ref[5:6] + vec_ref[6:7]).astype(bf16)
            n_ref[...] = normed
            here = pl.ds(pl.multiple_of(at * step, step), step)
            for j in range(fold):
                cols = slice(j * width, (j + 1) * width)
                u = dot(normed, up_w[j]) + bias_ref[:, cols]
                c0 = 0.7978845608028654
                square = u * u
                t = jnp.tanh(u * (c0 + (c0 * 0.044715) * square))
                half_up = 0.5 + 0.5 * t
                low = (u * half_up).astype(bf16)
                act_ref[:, cols] = low
                acts[j, here] = low
                slope = half_up + (u * (c0 + (3 * c0 * 0.044715) * square)) * (half_up * (1.0 - t))
                slope_ref[:, cols] = slope.astype(bf16)

        for j in range(fold):

            @pl.when(at == steps + j)
            def _(j=j):
                split_rows(dot_left(acts[j], cot_ref[...]), send_ref, keep_ref)

    early = lambda w: spec((step, w), lambda i: (jnp.minimum(i, steps - 1), 0))
    late = spec((width // (2 * block), block, width), lambda i: (jnp.maximum(i - steps, 0), 0, 0))
    return call(
        kernel,
        (
            shape((rows, width), f32),
            shape((rows, width), bf16),
            shape((rows, hidden), bf16),
            shape((rows, hidden), bf16),
        )
        + (shape((links.across, block, width), bf16),) * 2,
        grid=(steps + fold,),
        in_specs=[
            early(width),
            fixed((rows, width)),
            early(width),
            fixed(vectors.shape),
            fixed(up_bias.shape),
        ]
        + [hbm()] * links.outer,
        out_specs=(early(width), early(width), early(hidden), early(hidden), late, late),
        scratch=[
            pltpu.VMEM((fold, rows, width), bf16),
            pltpu.VMEM((width, width), bf16),
            pltpu.VMEM((fold, width, width), bf16),
            pltpu.SemaphoreType.DMA(((1 + fold) * links.outer,)),
        ],
        name="lift",
        flops=2 * rows * width * (width + 2 * hidden),
        traffic=4 * rows * hidden + 10 * rows * width,
        exps=rows * hidden,
        after=after,
    )(tokens, cot, mixture, vectors, up_bias, *second)


def settle(links, residual, slopes, cot, inverse, mixture, normed2, vectors, second, third, hidden, after=()):
    rows, width = residual.shape
    fold = hidden // width
    line_rows = width // links.outer
    step = 256
    steps = rows // step

    def kernel(res_ref, slope_ref, cot_ref, inv_ref, mix_ref, n_ref, vec_ref, *refs):
        parts, refs = refs[: links.outer], refs[links.outer :]
        lasts, refs = refs[: links.outer], refs[links.outer :]
        ag_ref, mg_ref, sums_ref, ub_ref, send_ref, keep_ref = refs[:6]
        ups, ags, out_w, up_w, down_w, sems = refs[6:]
        at = pl.program_id(0)

        @pl.when(at < steps)
        def _():
            @pl.when(at == 0)
            def _():
                copies = links.load(lasts, fold * line_rows, 0, down_w, sems, (1 + fold) * links.outer)
                wait(copies + tops(links, parts, line_rows, out_w, up_w, sems))
                sums_ref[...] = jnp.zeros_like(sums_ref)
                ub_ref[...] = jnp.zeros_like(ub_ref)

            residual = res_ref[...]
            cot = cot_ref[...]
            cot_f = cot.astype(f32)
            into = jnp.zeros((step, width), f32)
            here = pl.ds(pl.multiple_of(at * step, step), step)
            for j in range(fold):
                cols = slice(j * width, (j + 1) * width)
                grad = dot_right(cot, down_w[cols, :]) * slope_ref[:, cols].astype(f32)
                low = grad.astype(bf16)
                ups[j, here] = low
                ub_ref[0:1, cols] += jnp.sum(grad, axis=0, keepdims=True)
                into += dot_right(low, up_w[j])

            unit, scale = standardize(residual)
            residual_grad = cot_f + norm_back(into, vec_ref[5:6], unit, scale)
            low = residual_grad.astype(bf16)
            ag_ref[...] = low
            ags[here] = low
            mg_ref[...] = (dot_right(low, out_w[...]) * inv_ref[...]).astype(bf16)
            total = lambda v: jnp.sum(v, axis=0, keepdims=True)
            sums_ref[4:5] += total(residual_grad)
            sums_ref[5:6] += total(into * unit)
            sums_ref[6:7] += total(into)
            sums_ref[7:8] += total(cot_f)

        for j in range(fold):

            @pl.when(at == steps + j)
            def _(j=j):
                split_rows(dot_left(n_ref[...], ups[j]), send_ref, keep_ref)

        @pl.when(at == steps + fold)
        def _():
            split_rows(dot_left(mix_ref[...], ags[...]), send_ref, keep_ref)

    early = lambda w: spec((step, w), lambda i: (jnp.minimum(i, steps - 1), 0))
    late = spec((links.across, line_rows, width), lambda i: (0, 0, jnp.maximum(i - steps, 0)))
    return call(
        kernel,
        (shape((rows, width), bf16),) * 2
        + (shape((8, width), f32), shape((8, hidden), f32))
        + (shape((links.across, line_rows, width + hidden), bf16),) * 2,
        grid=(steps + fold + 1,),
        in_specs=[
            early(width),
            early(hidden),
            early(width),
            early(width),
            fixed((rows, width)),
            fixed((rows, width)),
            fixed(vectors.shape),
        ]
        + [hbm()] * (2 * links.outer),
        out_specs=(early(width),) * 2 + (fixed((8, width)), fixed((8, hidden)), late, late),
        scratch=[
            pltpu.VMEM((fold, rows, width), bf16),
            pltpu.VMEM((rows, width), bf16),
            pltpu.VMEM((width, width), bf16),
            pltpu.VMEM((fold, width, width), bf16),
            pltpu.VMEM((hidden, width), bf16),
            pltpu.SemaphoreType.DMA(((2 + fold) * links.outer,)),
        ],
        name="settle",
        flops=2 * rows * width * (2 * width + 3 * hidden),
        traffic=2 * rows * hidden + 14 * rows * width,
        after=after,
    )(residual, slopes, cot, inverse, mixture, normed2, vectors, *second, *third)


def emit(links, residual, activated, vectors, third, after=()):
    rows, width = residual.shape
    hidden = activated.shape[1]
    line_rows = hidden // links.outer
    step = 256

    def kernel(res_ref, act_ref, vec_ref, *refs):
        parts, (y_ref, down_w, sems) = refs[: links.outer], refs[links.outer :]

        @pl.when(pl.program_id(0) == 0)
        def _():
            for copy in links.load(parts, line_rows, 0, down_w, sems):
                copy.wait()

        y_ref[...] = (res_ref[...] + dot(act_ref[...], down_w[...]) + vec_ref[7:8]).astype(bf16)

    one = lambda w: spec((step, w), lambda i: (i, 0))
    return call(
        kernel,
        shape((rows, width), bf16),
        grid=(rows // step,),
        in_specs=[one(width), one(hidden), fixed(vectors.shape)] + [hbm()] * links.outer,
        out_specs=one(width),
        scratch=[pltpu.VMEM((hidden, width), bf16), pltpu.SemaphoreType.DMA((links.outer,))],
        name="emit",
        flops=2 * rows * width * hidden,
        traffic=2 * rows * hidden + 6 * rows * width,
        after=after,
    )(residual, activated, vectors, *third)


def finish(links, tokens, attn_grad, groups, vectors, first, after=()):
    batch, rows, width = tokens.shape
    line_rows = width // links.outer
    wide = width // BACK
    step = rows // 2

    def kernel(x_ref, ag_ref, vec_ref, *refs):
        grads, refs = refs[: 3 * BACK], refs[3 * BACK :]
        parts, refs = refs[: links.outer], refs[links.outer :]
        tg_ref, weight, sems = refs

        @pl.when((pl.program_id(0) == 0) & (pl.program_id(1) == 0))
        def _():
            for copy in links.load(parts, line_rows, 0, weight, sems):
                copy.wait()

        grad = jnp.zeros((step, width), f32)
        for g in range(BACK):
            for kind in range(3):
                at = kind * width + g * wide
                grad += dot_right(grads[3 * g + kind][0], weight[:, at : at + wide])
        unit, scale = standardize(x_ref[0].astype(f32))
        tokens_grad = ag_ref[0].astype(f32) + norm_back(grad, vec_ref[0:1], unit, scale)
        tg_ref[0] = tokens_grad.astype(bf16)

    one = lambda w: spec((1, step, w), lambda m, i: (m, i, 0))
    return call(
        kernel,
        shape((batch, rows, width), bf16),
        grid=(batch, rows // step),
        in_specs=[one(width), one(width), fixed(vectors.shape)]
        + [one(wide)] * (3 * BACK)
        + [hbm()] * (links.outer),
        out_specs=one(width),
        scratch=[
            pltpu.VMEM((width, 3 * width), bf16),
            pltpu.SemaphoreType.DMA((links.outer,)),
        ],
        name="finish",
        flops=6 * batch * rows * width * width,
        traffic=12 * batch * rows * width,
        after=after,
    )(
        tokens,
        attn_grad,
        vectors,
        *[v for group in groups for v in group],
        *first,
    )


def split_rows(value, send_ref, keep_ref):
    core = lax.axis_index("dp") % 2
    groups, block, _ = send_ref.shape
    for a in range(groups):
        low = value[2 * a * block : (2 * a + 1) * block]
        high = value[(2 * a + 1) * block : (2 * a + 2) * block]
        send_ref[a] = jnp.where(core == 0, high, low).astype(bf16)
        keep_ref[a] = jnp.where(core == 0, low, high).astype(bf16)


def qkv_grads(links, units, memory_low, groups, first, columns, sums, after=()):
    batch, rows, width = units.shape
    total = groups[0][1].shape[1]
    wide = width // BACK
    block = width // links.outer
    basis = memory_low.shape[1]
    count = 3 * BACK

    def kernel(u_ref, mem_ref, col_ref, sum_ref, *refs):
        sources, refs = refs[:count], refs[count:]
        parts, refs = refs[: links.outer], refs[links.outer :]
        send_ref, keep_ref, weight, ends, lines, *grads, sems, more_sems = refs
        step = pl.program_id(0)
        lane = lax.broadcasted_iota(jnp.int32, (1, 128), 1)
        across = lambda v: jnp.sum(v, axis=1, keepdims=True)
        down = lambda v: jnp.sum(v.astype(f32), axis=0, keepdims=True)
        fetch = lambda at: pltpu.make_async_copy(sources[at], grads[at], more_sems.at[at])
        for at in range(count):
            kind, g = at // BACK, at % BACK
            mine = slice(g * wide, (g + 1) * wide)

            @pl.when(step == at)
            def _(at=at, kind=kind, g=g, mine=mine):
                if at == 0:
                    fetch(0).start()
                    copies = links.load(parts, block, 0, weight, sems)
                    for later in range(1, count):
                        fetch(later).start()
                    lines[...] = jnp.zeros_like(lines)
                    lines[0:16] = sum_ref[...]
                    ends[...] = jnp.zeros_like(ends)
                fetch(at).wait()
                ref = grads[at]
                value = sum(dot_left(u_ref[m], ref[m, :rows]) for m in range(batch))
                line = sum(down(ref[m, :rows]) for m in range(batch))
                if at == 0:
                    wait(copies)
                w = weight[:, kind * width + g * wide : kind * width + (g + 1) * wide].astype(f32)
                ends[...] += jnp.where(
                    lane == 0, across(w * value), jnp.where(lane == 1, across(w * line), 0.0)
                )
                value = col_ref[:, 0:1] * value + col_ref[:, 1:2] * line
                if kind:
                    value += sum(dot_left(mem_ref[m], ref[m, rows:]) for m in range(batch))
                if kind == 0:
                    lines[2:3, mine] = line
                if kind == 2:
                    lines[3:4, mine] = line + sum(down(ref[m, rows:]) for m in range(batch))
                split_rows(value, send_ref, keep_ref)

        @pl.when(step == count)
        def _():
            value = lines[...].T + ends[...]
            split_rows(value, send_ref.at[:, :, 0:128], keep_ref.at[:, :, 0:128])

    out = spec((links.across, block, wide), lambda i: (0, 0, i))
    kinds = [(batch, rows, wide)] * BACK + [(batch, total, wide)] * (2 * BACK)
    return call(
        kernel,
        (shape((links.across, block, 3 * width + wide), bf16),) * 2,
        grid=(count + 1,),
        in_specs=[
            fixed((batch, rows, width)),
            fixed((batch, basis, width)),
            fixed(columns.shape),
            fixed(sums.shape),
        ]
        + [hbm()] * (count + links.outer),
        out_specs=(out, out),
        scratch=[
            pltpu.VMEM((width, 3 * width), bf16),
            pltpu.VMEM((width, 128), f32),
            pltpu.VMEM((128, width), f32),
        ]
        + [pltpu.VMEM(kind, bf16) for kind in kinds]
        + [pltpu.SemaphoreType.DMA((links.outer,)), pltpu.SemaphoreType.DMA((count,))],
        name="qkv_grads",
        flops=2 * batch * width * width * (3 * rows + 2 * basis),
        traffic=2 * batch * width * 7 * rows,
        after=after,
    )(
        units,
        memory_low,
        columns,
        sums,
        *[group[kind] for kind in range(3) for group in groups],
        *first,
    )


def body(links, tokens, cotangent, doc_start, memory_init, *shards):
    (
        norm1_gain,
        norm1_bias,
        qkv_weight,
        query_bias,
        value_bias,
        out_weight,
        out_bias,
        norm2_gain,
        norm2_bias,
        up_weight,
        up_bias,
        down_weight,
        down_bias,
    ) = shards
    own, width = out_weight.shape
    hidden = up_weight.shape[1]
    fold = hidden // width
    n = links.count
    tokens, cotangent, doc_start, memory_init = (
        tokens[:, 0],
        cotangent[:, 0],
        doc_start[:, 0],
        memory_init[0],
    )
    batch, rows, _ = tokens.shape

    small = (norm1_gain, norm1_bias, query_bias, value_bias, out_bias, norm2_gain, norm2_bias, down_bias)
    small = jnp.concatenate([jnp.stack(small).T, up_bias.reshape(own, fold)], axis=1)
    small = jnp.pad(small, ((0, 0), (0, 128 - small.shape[1])))
    wide = width // GROUPS
    positions = jnp.arange(rows)
    before = positions[None, :] <= positions[:, None]
    documents = jnp.sum(jnp.where(before, doc_start[:, None, :], 0), axis=2)
    documents = (documents[:, :, None], documents[:, None, :])

    carry_table, fresh_table = rbf_tables(rows, memory_init.shape[0])
    high = functools.partial(jnp.dot, precision=lax.Precision.HIGH)
    memories = [(memory_init,)]
    carried, gained, biased = memory_init, None, None
    for m in range(batch - 1):
        keep_share = jnp.where(documents[0][m, -1, 0] == 0, 1.0, 0.0)
        unit, _ = standardize(tokens[m].astype(f32))
        table = keep_share * carry_table
        carried = high(table, carried)
        new_gained = high(fresh_table, unit)
        new_biased = jnp.sum(fresh_table, axis=1, keepdims=True)
        if m:
            new_gained += high(table, gained)
            new_biased += high(table, biased)
        gained, biased = new_gained, new_biased
        memories.append((carried, gained, biased))

    flat = lambda v: v.reshape(batch * rows, v.shape[-1])
    full = lambda v: v.reshape(batch, rows, v.shape[-1])
    line = links.line(jnp.concatenate([qkv_weight, small], axis=1), [own], after=[carry_table])
    early = [v for memory in memories[1:] for v in memory] + list(documents)
    first = links.spread(line, early)
    unit = width // 2
    least = -(-(2**20) // (2 * links.deep * unit))
    packed = pack([out_weight, up_weight, down_weight], unit, -(-least // 16) * 16)
    packed = lax.all_gather(packed, "fsdp", axis=0, tiled=True)
    vectors, columns = unpack(links, first, width)
    made = project(links, tokens, memories, None, vectors, 0, first)
    queries, keys, values, units, memory_low = made
    line = regroup(links.deep, packed, 0, own, 2, 1 + fold, after=made[:1])
    mixture, inverse, exps = attend(queries, keys, values, *documents, after=[line])
    second = links.spread(line, [mixture])
    line = regroup(links.deep, packed, 2 * own * (1 + fold), fold * own, 2, 1, after=second)
    up_bias_full = columns[:, 8 : 8 + fold].reshape(1, hidden)
    cot = flat(cotangent)
    made = lift(
        links, flat(tokens), cot, flat(mixture), vectors, up_bias_full, second, hidden, after=[line]
    )
    residual, normed2, activated, slopes = made[:4]
    down_parts = made[4:]
    third, down_parts = links.spread(line, made[:1], down_parts)
    down_parts = links.merge_core(*down_parts, after=third[-1:])
    made = settle(
        links,
        residual,
        slopes,
        cot,
        flat(inverse),
        flat(mixture),
        normed2,
        vectors,
        second,
        third,
        hidden,
        after=down_parts[:1],
    )
    attn_grad, scaled, sums, up_sums = made[:4]
    up_parts = made[4:]
    sums = jnp.concatenate(
        [sums, up_sums[0].reshape(width, fold).T, jnp.zeros((8 - fold, width), f32)], axis=0
    )
    groups = []
    down_total = links.merge_columns(*down_parts, after=[attn_grad])
    up_parts = gate(up_parts, [down_total])
    hold = [down_total]
    pairs = width // PAIR // BACK
    for g in range(BACK):
        groups.append(
            attend_back(
                queries, keys, values, exps, mixture, full(scaled), g * pairs, pairs, after=hold
            )
        )
        hold = list(groups[-1][:1])
        if g == 0:
            up_parts = links.merge_core(*up_parts, after=hold)
            hold = [up_parts[0]]
    down_grad = links.merge_deep(down_total)
    qkv_parts = qkv_grads(links, units, memory_low, groups, first, columns, sums)
    up_total = links.merge_columns(*up_parts, after=qkv_parts[:1])
    up_grad = links.merge_deep(up_total)
    qkv_parts = links.merge_core(*qkv_parts, 3 * width + 128, after=[up_total, down_grad])
    output = emit(links, residual, activated, vectors, third, after=qkv_parts[:1])
    tokens_grad = finish(links, tokens, full(attn_grad), groups, vectors, first, after=[output])
    qkv_parts = links.merge_line(*qkv_parts, after=[tokens_grad, up_grad])
    qkv_grad = links.merge_depth(*qkv_parts)
    vec = [qkv_grad[:, 3 * width + k] for k in range(8)]
    lead = lambda v: v[:, None]
    return (
        lead(full(output)),
        lead(tokens_grad),
        vec[0],
        vec[1],
        qkv_grad[:, : 3 * width],
        vec[2],
        vec[3],
        up_grad[:, hidden:],
        vec[4],
        vec[5],
        vec[6],
        up_grad[:, :hidden],
        qkv_grad[:, 3 * width + 8 : 3 * width + 8 + fold].reshape(fold * own),
        down_grad,
        vec[7],
    )


def solution(mesh):
    both = ("dp", "fsdp")
    vector, matrix = P(both), P(both, None)
    params = (
        vector,
        vector,
        matrix,
        vector,
        vector,
        matrix,
        vector,
        vector,
        vector,
        matrix,
        vector,
        matrix,
        vector,
    )
    stream = P(None, both, None, None)
    return jax.shard_map(
        functools.partial(body, Links(mesh)),
        mesh=mesh,
        in_specs=(stream, stream, P(None, both, None), P(both, None, None)) + params,
        out_specs=(stream, stream) + params,
        check_vma=False,
    )
```

```python
import functools

import jax
import jax.numpy as jnp
from jax import lax
from jax.experimental import pallas as pl
from jax.experimental.pallas import tpu as pltpu
from jax.sharding import PartitionSpec as P

HD = 64
PAIR = 2 * HD
GROUPS = 1
BACK = 2
epsilon = 1e-05
hidden_score = -1e30
bf16 = jnp.bfloat16
f32 = jnp.float32
VMEM = 64 * 2**20


def dot(left, right):
    return jnp.dot(left, right, preferred_element_type=f32)


def dot_right(left, right):
    return lax.dot_general(left, right, (((1,), (1,)), ((), ())), preferred_element_type=f32)


def dot_left(left, right):
    return lax.dot_general(left, right, (((0,), (0,)), ((), ())), preferred_element_type=f32)


def call(
    kernel,
    out_shape,
    *,
    grid=(1,),
    in_specs,
    out_specs,
    scratch=(),
    name,
    flops,
    traffic,
    exps=0,
    after=(),
):
    count = len(in_specs)

    def run(*refs):
        return kernel(*refs[:count], *refs[count + len(after) :])

    made = pl.pallas_call(
        run,
        out_shape=out_shape,
        grid=grid,
        in_specs=list(in_specs) + [hbm()] * len(after),
        out_specs=out_specs,
        scratch_shapes=list(scratch),
        compiler_params=pltpu.CompilerParams(vmem_limit_bytes=VMEM),
        cost_estimate=pl.CostEstimate(flops=flops, bytes_accessed=traffic, transcendentals=exps),
        name=name,
    )
    return lambda *operands: made(*operands, *after)


def shape(dims, dtype):
    return jax.ShapeDtypeStruct(dims, dtype)


def hbm():
    return pl.BlockSpec(memory_space=pl.ANY)


def spec(block, index):
    return pl.BlockSpec(block, index)


def fixed(dims):
    return pl.BlockSpec(dims, lambda *_: (0,) * len(dims))


class Links:
    def __init__(self, mesh):
        self.outer = mesh.shape["dp"]
        self.across = self.outer // 2
        self.deep = mesh.shape["fsdp"]
        self.count = self.outer * self.deep

    def place(self):
        outer = lax.axis_index("dp")
        return (outer // 2, outer % 2, lax.axis_index("fsdp"))

    def swap(self, value, column=0, core=0, depth=0):
        pairs = []
        for device in range(self.count):
            outer, inner = divmod(device, self.deep)
            target = (((outer // 2) ^ column) * 2 + ((outer % 2) ^ core)) * self.deep + (
                inner ^ depth
            )
            pairs.append((device, target))
        return lax.ppermute(value, ("dp", "fsdp"), pairs)

    def line(self, shard, segments, after=()):
        pieces = [shard] + [self.swap(shard, depth=s) for s in range(1, self.deep)]
        rows, width = shard.shape

        def kernel(*refs):
            target = refs[self.deep]
            depth = lax.axis_index("fsdp")
            values = [ref[...].astype(f32) for ref in refs[: self.deep]]
            turned = []
            for j in range(self.deep):
                value = values[0]
                for s in range(1, self.deep):
                    value = jnp.where(depth == s ^ j, values[s], value)
                turned.append(value)
            out = []
            at = 0
            for count in segments:
                out += [value[at : at + count] for value in turned]
                at += count
            target[...] = jnp.concatenate(out, axis=0).astype(bf16)

        return call(
            kernel,
            shape((self.deep * rows, width), bf16),
            in_specs=[fixed((rows, width))] * self.deep,
            out_specs=fixed((self.deep * rows, width)),
            name="line",
            flops=self.deep**2 * rows * width,
            traffic=4 * self.deep * rows * width,
            after=after,
        )(*pieces)

    def spread(self, line, after=(), along=()):
        lines = [line] + [self.swap(line, column=s) for s in range(1, self.across)]
        extra = []
        if after:
            lines = gate(lines + list(along), after)
            lines, extra = lines[: self.across], lines[self.across :]
        out = []
        for part in lines:
            out += [part, self.swap(part, core=1)]
        return (out, extra) if along else out

    def merge_core(self, send, keep, used=None, after=()):
        across, rows, width = send.shape
        came = self.swap(send, core=1)
        if used is None:
            units = width // 128
            used, tile = width, 128 * max(k for k in range(1, 7) if units % k == 0)
        else:
            tile = used

        def kernel(keep_ref, came_ref, *outs):
            column = lax.axis_index("dp") // 2
            for s in range(across):
                value = keep_ref[column ^ s, :, :tile].astype(f32)
                value = value + came_ref[column ^ s, :, :tile].astype(f32)
                outs[s][...] = value.astype(outs[s].dtype)

        whole = pl.BlockSpec((across, rows, tile if tile < used else width), lambda i: (0, 0, i))
        part = pl.BlockSpec((rows, tile), lambda i: (0, i))
        return call(
            kernel,
            (shape((rows, used), f32),) + (shape((rows, used), bf16),) * (across - 1),
            grid=(used // tile,),
            in_specs=[whole, whole],
            out_specs=(part,) * across,
            name="merge_core",
            flops=across * rows * width,
            traffic=6 * across * rows * width,
            after=after,
        )(keep, came)

    def merge_columns(self, own, *sends, after=()):
        came = [self.swap(sends[s - 1], column=s) for s in range(1, self.across)]
        rows, width = own.shape
        tile = 768 if width % 768 == 0 else 128

        def kernel(own_ref, *refs):
            total = own_ref[...]
            for ref in refs[:-1]:
                total = total + ref[...].astype(f32)
            refs[-1][...] = total

        part = pl.BlockSpec((rows, tile), lambda i: (0, i))
        return call(
            kernel,
            shape((rows, width), f32),
            grid=(width // tile,),
            in_specs=[part] * self.across,
            out_specs=part,
            name="merge_columns",
            flops=self.across * rows * width,
            traffic=14 * rows * width,
            after=after,
        )(own, *came)

    def merge_deep(self, total):
        return lax.psum_scatter(total, "fsdp", scatter_dimension=0, tiled=True)

    def merge_line(self, own, *sends, after=()):
        came = [self.swap(sends[s - 1], column=s) for s in range(1, self.across)]
        rows, width = own.shape
        main = rows // self.deep

        def kernel(own_ref, *refs):
            total = own_ref[...]
            for ref in refs[: self.across - 1]:
                total = total + ref[...].astype(f32)
            outs = refs[self.across - 1 :]
            parts = [total[j * main : (j + 1) * main] for j in range(self.deep)]
            depth = lax.axis_index("fsdp")
            for s in range(self.deep):
                value = parts[0]
                for j in range(1, self.deep):
                    value = jnp.where(depth == s ^ j, parts[j], value)
                outs[s][...] = value.astype(outs[s].dtype)

        return call(
            kernel,
            (shape((main, width), f32),) + (shape((main, width), bf16),) * (self.deep - 1),
            in_specs=[fixed((rows, width))] * self.across,
            out_specs=(fixed((main, width)),) * self.deep,
            name="merge_line",
            flops=(self.across + self.deep) * rows * width,
            traffic=14 * rows * width,
            after=after,
        )(own, *came)

    def merge_depth(self, own, *sends):
        came = [self.swap(sends[s - 1], depth=s) for s in range(1, self.deep)]
        return sum((part.astype(f32) for part in came), own)

    def load(self, parts, rows, at, target, sems, base=0):
        outer = lax.axis_index("dp")
        copies = []
        for k, part in enumerate(parts):
            spot = pl.multiple_of((outer ^ k) * rows, 16)
            copies.append(
                pltpu.make_async_copy(
                    part.at[pl.ds(at, rows), pl.ds(0, target.shape[1])],
                    target.at[pl.ds(spot, rows)],
                    sems.at[base + k],
                )
            )
        for copy in copies:
            copy.start()
        return copies


def rbf_tables(seg_rows, basis):
    centers = (jnp.arange(basis, dtype=f32) + 0.5) / basis

    def bumps(points):
        return jnp.exp(-0.5 * jnp.square((centers[:, None] - points[None, :]) * basis))

    old_points = 0.75 * centers
    new_points = 0.75 + 0.25 * (jnp.arange(seg_rows, dtype=f32) + 0.5) / seg_rows
    phi_old = bumps(old_points)
    phi_new = bumps(new_points)
    totals = jnp.sum(phi_old, axis=1) + jnp.sum(phi_new, axis=1)
    recon = bumps(centers)
    recon = recon / jnp.sum(recon, axis=0, keepdims=True)
    carry_table = jnp.dot(phi_old, recon.T, precision=lax.Precision.HIGH) / totals[:, None]
    fresh_table = phi_new / totals[:, None]
    return (carry_table, fresh_table)


def standardize(values):
    center = values - jnp.mean(values, axis=-1, keepdims=True)
    spread = jnp.mean(center * center, axis=-1, keepdims=True)
    scale = lax.rsqrt(spread + epsilon)
    return (center * scale, scale)


def norm_back(grad, gain, unit, scale):
    inner = grad * gain
    shift = jnp.mean(inner, axis=-1, keepdims=True)
    slope = jnp.mean(inner * unit, axis=-1, keepdims=True)
    return (inner - shift - unit * slope) * scale


def gate(values, after):
    count = len(values)

    def kernel(*refs):
        pass

    return pl.pallas_call(
        kernel,
        out_shape=[shape(v.shape, v.dtype) for v in values],
        in_specs=[hbm()] * (count + len(after)),
        out_specs=[hbm()] * count,
        input_output_aliases={k: k for k in range(count)},
        name="gate",
    )(*values, *after)


def pack(pieces, width, least, after=()):
    rows = max(sum(v.size for v in pieces) // width, least)

    def kernel(*refs):
        value = [ref[...].astype(f32) for ref in refs[:-1]]
        value = [
            v[:, k * width : (k + 1) * width] for v in value for k in range(v.shape[1] // width)
        ]
        value = jnp.concatenate(value, axis=0).astype(bf16)
        refs[-1][: value.shape[0]] = value
        if value.shape[0] < rows:
            refs[-1][value.shape[0] :] = jnp.zeros((rows - value.shape[0], width), bf16)

    return call(
        kernel,
        shape((rows, width), bf16),
        in_specs=[fixed(v.shape) for v in pieces],
        out_specs=fixed((rows, width)),
        name="pack",
        flops=rows * width,
        traffic=4 * rows * width,
        after=after,
    )(*pieces)


def regroup(deep, packed, first, height, blocks, segments, after=()):
    step, unit = packed.shape[0] // deep, packed.shape[1]
    rows, width = segments * deep * height, blocks * unit

    def kernel(packed_ref, target_ref):
        out = []
        for segment in range(segments):
            for z in range(deep):
                at = z * step + first + segment * blocks * height
                row = [
                    packed_ref[at + k * height : at + (k + 1) * height].astype(f32)
                    for k in range(blocks)
                ]
                out.append(jnp.concatenate(row, axis=1))
        target_ref[...] = jnp.concatenate(out, axis=0).astype(bf16)

    return call(
        kernel,
        shape((rows, width), bf16),
        in_specs=[fixed(packed.shape)],
        out_specs=fixed((rows, width)),
        name="regroup",
        flops=rows * width,
        traffic=4 * rows * width,
        after=after,
    )(packed)


def unpack(links, parts, width):
    line_rows = width // links.outer
    at = parts[0].shape[1] // 128 - 1

    def kernel(*refs):
        parts, (rows_ref, cols_ref) = refs[: links.outer], refs[links.outer :]
        outer = lax.axis_index("dp")
        for k, part in enumerate(parts):
            spot = pl.multiple_of((outer ^ k) * line_rows, 8)
            cols_ref[pl.ds(spot, line_rows)] = part[...].astype(f32)
        rows_ref[...] = cols_ref[...].T[:16]

    return call(
        kernel,
        (shape((16, width), f32), shape((width, 128), f32)),
        in_specs=[spec((line_rows, 128), lambda i: (0, at))] * links.outer,
        out_specs=(fixed((16, width)), fixed((width, 128))),
        name="unpack",
        flops=width * 128,
        traffic=8 * width * 128,
    )(*parts)


def project(links, tokens, memories, memory_low, vectors, group, parts, after=()):
    batch, rows, width = tokens.shape
    line_rows = width // links.outer
    wide = width // GROUPS
    leads = [v for memory in memories for v in memory] if memory_low is None else [memory_low]
    basis = leads[0].shape[-2]
    mine = slice(group * wide, (group + 1) * wide)

    def kernel(tokens_ref, vec_ref, *refs):
        lead, refs = refs[: len(leads)], refs[len(leads) :]
        parts, refs = refs[: links.outer], refs[links.outer :]
        q_ref, k_ref, v_ref = refs[:3]
        weight, sems = refs[-2:]
        step = pl.program_id(0)

        @pl.when(step == 0)
        def _():
            for copy in links.load(parts, line_rows, 0, weight, sems):
                copy.wait()

        vec = vec_ref[...]
        if memory_low is None:
            unit_ref, low_ref = refs[3:5]
            at = 0
            for m, memory in enumerate(memories):

                @pl.when(step == m)
                def _(at=at, memory=memory):
                    value = lead[at][...]
                    if len(memory) > 1:
                        value = value + lead[at + 1][...] * vec[0:1] + lead[at + 2][...] * vec[1:2]
                    low_ref[0] = value.astype(bf16)

                at += len(memory)
        else:
            low_ref = lead[0]
        unit, _ = standardize(tokens_ref[0].astype(f32))
        normed = (unit * vec[0:1] + vec[1:2]).astype(bf16)
        if memory_low is None:
            unit_ref[0] = unit.astype(bf16)
        memory = low_ref[0]
        q_ref[0] = ((dot(normed, weight[:, :wide]) + vec[2:3, mine]) * 0.125).astype(bf16)
        k_ref[0, :rows] = dot(normed, weight[:, wide : 2 * wide]).astype(bf16)
        v_ref[0, :rows] = (dot(normed, weight[:, 2 * wide :]) + vec[3:4, mine]).astype(bf16)
        k_ref[0, rows:] = dot(memory, weight[:, wide : 2 * wide]).astype(bf16)
        v_ref[0, rows:] = (dot(memory, weight[:, 2 * wide :]) + vec[3:4, mine]).astype(bf16)

    keys = rows + basis
    one = lambda r, w: spec((1, r, w), lambda m: (m, 0, 0))
    kinds = [(rows, wide), (keys, wide), (keys, wide)]
    if memory_low is None:
        kinds += [(rows, width), (basis, width)]
        lead_specs = [fixed(v.shape) for v in leads]
    else:
        lead_specs = [one(basis, width)]
    return call(
        kernel,
        tuple(shape((batch, r, w), bf16) for r, w in kinds),
        grid=(batch,),
        in_specs=[one(rows, width), fixed(vectors.shape)] + lead_specs + [hbm()] * links.outer,
        out_specs=tuple(one(r, w) for r, w in kinds),
        scratch=[pltpu.VMEM((width, 3 * wide), bf16), pltpu.SemaphoreType.DMA((links.outer,))],
        name="project",
        flops=2 * batch * width * wide * (3 * rows + 2 * basis),
        traffic=2 * (batch * width * 8 * rows + 3 * width * wide),
        after=after,
    )(tokens, vectors, *leads, *parts)


def lanes(head):
    lane = lax.broadcasted_iota(jnp.int32, (1, PAIR), 1)
    return (lane // HD == head, (lane == (1 - head) * HD))


def attend(queries, keys, values, starts_col, starts_row, after=()):
    batch, rows, width = queries.shape
    total = keys.shape[1]
    heads = width // HD
    half = rows // 2

    def kernel(q_ref, k_ref, v_ref, col_ref, row_ref, mix_ref, inv_ref, e_ref, mask):
        @pl.when(pl.program_id(1) == 0)
        def _():
            i = lax.broadcasted_iota(jnp.int32, (rows, rows), 0)
            j = lax.broadcasted_iota(jnp.int32, (rows, rows), 1)
            allowed = (j <= i) & (col_ref[0] == row_ref[0])
            mask[...] = jnp.where(allowed, 0.0, hidden_score)

        q, k, v = q_ref[0], k_ref[0], v_ref[0]
        memory_bias = jnp.where(col_ref[0] == 0, 0.0, hidden_score).astype(bf16)
        outs = []
        for head in range(2):
            inside, first = lanes(head)
            qh = jnp.where(inside, q, jnp.where(first, memory_bias, 0).astype(bf16))
            kl = jnp.where(inside, k[:rows], 0).astype(bf16)
            km = jnp.where(inside, k[rows:], jnp.where(first, 1, 0).astype(bf16))
            vh = jnp.where(inside, v, 1).astype(bf16)
            parts = []
            for block in range(2):
                top, wide = block * half, (block + 1) * half
                here = qh[top : top + half]
                sl = dot_right(here, kl[:wide]) + mask[top : top + half, :wide]
                sm = dot_right(here, km)
                peak = jnp.maximum(
                    jnp.max(sl, axis=-1, keepdims=True), jnp.max(sm, axis=-1, keepdims=True)
                )
                el = jnp.exp(sl - peak).astype(bf16)
                em = jnp.exp(sm - peak).astype(bf16)
                e_ref[0, head, top : top + half, :wide] = el
                e_ref[0, head, top : top + half, rows:] = em
                parts.append(dot(el, vh[:wide]) + dot(em, vh[rows:]))
            outs.append(jnp.concatenate(parts, axis=0))
        inside, _ = lanes(0)
        mixed = jnp.where(inside, outs[0], outs[1])
        inverse = 1.0 / pltpu.roll(jnp.where(inside, outs[1], outs[0]), HD, 1)
        mix_ref[0] = (mixed * inverse).astype(bf16)
        inv_ref[0] = inverse

    pair = lambda r: spec((1, r, PAIR), lambda m, p: (m, 0, p))
    return call(
        kernel,
        (
            shape((batch, rows, width), bf16),
            shape((batch, rows, width), f32),
            shape((batch, heads, rows, total), bf16),
        ),
        grid=(batch, heads // 2),
        in_specs=[
            pair(rows),
            pair(total),
            pair(total),
            spec((1, rows, 1), lambda m, p: (m, 0, 0)),
            spec((1, 1, rows), lambda m, p: (m, 0, 0)),
        ],
        out_specs=(
            pair(rows),
            pair(rows),
            spec((1, 2, rows, total), lambda m, p: (m, p, 0, 0)),
        ),
        scratch=[pltpu.VMEM((rows, rows), f32)],
        name="attend",
        flops=16 * batch * heads * rows * total * HD,
        traffic=2 * batch * heads * rows * total,
        exps=batch * heads * rows * total,
        after=after,
    )(queries, keys, values, starts_col, starts_row)


def attend_back(queries, keys, values, exps, mixture, scaled, base, count, after=()):
    batch, rows, width = queries.shape
    total = keys.shape[1]
    half = rows // 2

    def kernel(q_ref, k_ref, v_ref, e_ref, mix_ref, g_ref, dq_ref, dk_ref, dv_ref):
        q, k, v, g = q_ref[0], k_ref[0], v_ref[0], g_ref[0]
        product = -(g.astype(f32) * mix_ref[0].astype(f32))
        product = pltpu.roll(product, HD, 1).astype(bf16)
        dqs, dks, dvs = [], [], []
        for head in range(2):
            inside, _ = lanes(head)
            gh = jnp.where(inside, g, product)
            vh = jnp.where(inside, v, 1).astype(bf16)
            near = (e_ref[0, head, :, :half].astype(f32) * dot_right(gh, vh[:half])).astype(bf16)
            late = e_ref[0, head, half:, half:rows].astype(f32) * dot_right(gh[half:], vh[half:rows])
            late = late.astype(bf16)
            far = (e_ref[0, head, :, rows:].astype(f32) * dot_right(gh, vh[rows:])).astype(bf16)
            mixed = dot(near, k[:half]) + dot(far, k[rows:])
            dqs.append(
                jnp.concatenate([mixed[:half], mixed[half:] + dot(late, k[half:rows])], axis=0)
            )
            e = e_ref[0, head]
            dks.append(
                [
                    dot_left(near, q),
                    dot_left(late, q[half:]),
                    dot_left(far, q),
                ]
            )
            dvs.append(
                [
                    dot_left(e[:, :half], g),
                    dot_left(e[half:, half:rows], g[half:]),
                    dot_left(e[:, rows:], g),
                ]
            )
        inside, _ = lanes(0)
        dq_ref[0] = (jnp.where(inside, dqs[0], dqs[1]) * 0.125).astype(bf16)
        for ref, pieces in ((dk_ref, dks), (dv_ref, dvs)):
            for i, (lo, hi) in enumerate(((0, half), (half, rows), (rows, total))):
                ref[0, lo:hi] = jnp.where(inside, pieces[0][i], pieces[1][i]).astype(bf16)

    pair = lambda r: spec((1, r, PAIR), lambda m, p: (m, 0, p + base))
    out = lambda r: spec((1, r, PAIR), lambda m, p: (m, 0, p))
    return call(
        kernel,
        (
            shape((batch, rows, count * PAIR), bf16),
            shape((batch, total, count * PAIR), bf16),
            shape((batch, total, count * PAIR), bf16),
        ),
        grid=(batch, count),
        in_specs=[
            pair(rows),
            pair(total),
            pair(total),
            spec((1, 2, rows, total), lambda m, p: (m, p + base, 0, 0)),
            pair(rows),
            pair(rows),
        ],
        out_specs=(out(rows), out(total), out(total)),
        name="attend_back",
        flops=64 * batch * count * rows * total * HD,
        traffic=4 * batch * count * rows * total,
        after=after,
    )(queries, keys, values, exps, mixture, scaled)


def tops(links, parts, rows, out_w, up_w, sems):
    copies = links.load(parts, rows, 0, out_w, sems)
    for j in range(up_w.shape[0]):
        copies += links.load(parts, rows, (1 + j) * rows, up_w.at[j], sems, (1 + j) * links.outer)
    return copies


def wait(copies):
    for copy in copies:
        copy.wait()


def lift(links, tokens, cot, mixture, vectors, up_bias, second, hidden, after=()):
    rows, width = tokens.shape
    fold = hidden // width
    line_rows = width // links.outer
    block = hidden // links.outer
    step = 256
    steps = rows // step

    def kernel(x_ref, cot_ref, mix_ref, vec_ref, bias_ref, *refs):
        parts, refs = refs[: links.outer], refs[links.outer :]
        res_ref, n_ref, act_ref, slope_ref, send_ref, keep_ref, acts, out_w, up_w, sems = refs
        at = pl.program_id(0)

        @pl.when(at < steps)
        def _():
            @pl.when(at == 0)
            def _():
                wait(tops(links, parts, line_rows, out_w, up_w, sems))

            residual = x_ref[...].astype(f32) + vec_ref[4:5] + dot(mix_ref[...], out_w[...])
            res_ref[...] = residual
            unit, _ = standardize(residual)
            normed = (unit * vec_ref[5:6] + vec_ref[6:7]).astype(bf16)
            n_ref[...] = normed
            here = pl.ds(pl.multiple_of(at * step, step), step)
            for j in range(fold):
                cols = slice(j * width, (j + 1) * width)
                u = dot(normed, up_w[j]) + bias_ref[:, cols]
                c0 = 0.7978845608028654
                square = u * u
                t = jnp.tanh(u * (c0 + (c0 * 0.044715) * square))
                half_up = 0.5 + 0.5 * t
                low = (u * half_up).astype(bf16)
                act_ref[:, cols] = low
                acts[j, here] = low
                slope = half_up + (u * (c0 + (3 * c0 * 0.044715) * square)) * (half_up * (1.0 - t))
                slope_ref[:, cols] = slope.astype(bf16)

        for j in range(fold):

            @pl.when(at == steps + j)
            def _(j=j):
                split_rows(dot_left(acts[j], cot_ref[...]), send_ref, keep_ref)

    early = lambda w: spec((step, w), lambda i: (jnp.minimum(i, steps - 1), 0))
    late = spec((width // (2 * block), block, width), lambda i: (jnp.maximum(i - steps, 0), 0, 0))
    return call(
        kernel,
        (
            shape((rows, width), f32),
            shape((rows, width), bf16),
            shape((rows, hidden), bf16),
            shape((rows, hidden), bf16),
        )
        + (shape((links.across, block, width), bf16),) * 2,
        grid=(steps + fold,),
        in_specs=[
            early(width),
            fixed((rows, width)),
            early(width),
            fixed(vectors.shape),
            fixed(up_bias.shape),
        ]
        + [hbm()] * links.outer,
        out_specs=(early(width), early(width), early(hidden), early(hidden), late, late),
        scratch=[
            pltpu.VMEM((fold, rows, width), bf16),
            pltpu.VMEM((width, width), bf16),
            pltpu.VMEM((fold, width, width), bf16),
            pltpu.SemaphoreType.DMA(((1 + fold) * links.outer,)),
        ],
        name="lift",
        flops=2 * rows * width * (width + 2 * hidden),
        traffic=4 * rows * hidden + 10 * rows * width,
        exps=rows * hidden,
        after=after,
    )(tokens, cot, mixture, vectors, up_bias, *second)


def settle(links, residual, slopes, cot, inverse, mixture, normed2, vectors, second, third, hidden, after=()):
    rows, width = residual.shape
    fold = hidden // width
    line_rows = width // links.outer
    step = 256
    steps = rows // step

    def kernel(res_ref, slope_ref, cot_ref, inv_ref, mix_ref, n_ref, vec_ref, *refs):
        parts, refs = refs[: links.outer], refs[links.outer :]
        lasts, refs = refs[: links.outer], refs[links.outer :]
        ag_ref, mg_ref, sums_ref, ub_ref, send_ref, keep_ref = refs[:6]
        ups, ags, out_w, up_w, down_w, sems = refs[6:]
        at = pl.program_id(0)

        @pl.when(at < steps)
        def _():
            @pl.when(at == 0)
            def _():
                copies = links.load(lasts, fold * line_rows, 0, down_w, sems, (1 + fold) * links.outer)
                wait(copies + tops(links, parts, line_rows, out_w, up_w, sems))
                sums_ref[...] = jnp.zeros_like(sums_ref)
                ub_ref[...] = jnp.zeros_like(ub_ref)

            residual = res_ref[...]
            cot = cot_ref[...]
            cot_f = cot.astype(f32)
            into = jnp.zeros((step, width), f32)
            here = pl.ds(pl.multiple_of(at * step, step), step)
            for j in range(fold):
                cols = slice(j * width, (j + 1) * width)
                grad = dot_right(cot, down_w[cols, :]) * slope_ref[:, cols].astype(f32)
                low = grad.astype(bf16)
                ups[j, here] = low
                ub_ref[0:1, cols] += jnp.sum(grad, axis=0, keepdims=True)
                into += dot_right(low, up_w[j])

            unit, scale = standardize(residual)
            residual_grad = cot_f + norm_back(into, vec_ref[5:6], unit, scale)
            low = residual_grad.astype(bf16)
            ag_ref[...] = low
            ags[here] = low
            mg_ref[...] = (dot_right(low, out_w[...]) * inv_ref[...]).astype(bf16)
            total = lambda v: jnp.sum(v, axis=0, keepdims=True)
            sums_ref[4:5] += total(residual_grad)
            sums_ref[5:6] += total(into * unit)
            sums_ref[6:7] += total(into)
            sums_ref[7:8] += total(cot_f)

        for j in range(fold):

            @pl.when(at == steps + j)
            def _(j=j):
                split_rows(dot_left(n_ref[...], ups[j]), send_ref, keep_ref)

        @pl.when(at == steps + fold)
        def _():
            split_rows(dot_left(mix_ref[...], ags[...]), send_ref, keep_ref)

    early = lambda w: spec((step, w), lambda i: (jnp.minimum(i, steps - 1), 0))
    late = spec((links.across, line_rows, width), lambda i: (0, 0, jnp.maximum(i - steps, 0)))
    return call(
        kernel,
        (shape((rows, width), bf16),) * 2
        + (shape((8, width), f32), shape((8, hidden), f32))
        + (shape((links.across, line_rows, width + hidden), bf16),) * 2,
        grid=(steps + fold + 1,),
        in_specs=[
            early(width),
            early(hidden),
            early(width),
            early(width),
            fixed((rows, width)),
            fixed((rows, width)),
            fixed(vectors.shape),
        ]
        + [hbm()] * (2 * links.outer),
        out_specs=(early(width),) * 2 + (fixed((8, width)), fixed((8, hidden)), late, late),
        scratch=[
            pltpu.VMEM((fold, rows, width), bf16),
            pltpu.VMEM((rows, width), bf16),
            pltpu.VMEM((width, width), bf16),
            pltpu.VMEM((fold, width, width), bf16),
            pltpu.VMEM((hidden, width), bf16),
            pltpu.SemaphoreType.DMA(((2 + fold) * links.outer,)),
        ],
        name="settle",
        flops=2 * rows * width * (2 * width + 3 * hidden),
        traffic=2 * rows * hidden + 14 * rows * width,
        after=after,
    )(residual, slopes, cot, inverse, mixture, normed2, vectors, *second, *third)


def emit(links, residual, activated, vectors, third, after=()):
    rows, width = residual.shape
    hidden = activated.shape[1]
    line_rows = hidden // links.outer
    step = 256

    def kernel(res_ref, act_ref, vec_ref, *refs):
        parts, (y_ref, down_w, sems) = refs[: links.outer], refs[links.outer :]

        @pl.when(pl.program_id(0) == 0)
        def _():
            for copy in links.load(parts, line_rows, 0, down_w, sems):
                copy.wait()

        y_ref[...] = (res_ref[...] + dot(act_ref[...], down_w[...]) + vec_ref[7:8]).astype(bf16)

    one = lambda w: spec((step, w), lambda i: (i, 0))
    return call(
        kernel,
        shape((rows, width), bf16),
        grid=(rows // step,),
        in_specs=[one(width), one(hidden), fixed(vectors.shape)] + [hbm()] * links.outer,
        out_specs=one(width),
        scratch=[pltpu.VMEM((hidden, width), bf16), pltpu.SemaphoreType.DMA((links.outer,))],
        name="emit",
        flops=2 * rows * width * hidden,
        traffic=2 * rows * hidden + 6 * rows * width,
        after=after,
    )(residual, activated, vectors, *third)


def finish(links, tokens, attn_grad, groups, vectors, first, after=()):
    batch, rows, width = tokens.shape
    line_rows = width // links.outer
    wide = width // BACK
    step = rows // 2

    def kernel(x_ref, ag_ref, vec_ref, *refs):
        grads, refs = refs[: 3 * BACK], refs[3 * BACK :]
        parts, refs = refs[: links.outer], refs[links.outer :]
        tg_ref, weight, sems = refs

        @pl.when((pl.program_id(0) == 0) & (pl.program_id(1) == 0))
        def _():
            for copy in links.load(parts, line_rows, 0, weight, sems):
                copy.wait()

        grad = jnp.zeros((step, width), f32)
        for g in range(BACK):
            for kind in range(3):
                at = kind * width + g * wide
                grad += dot_right(grads[3 * g + kind][0], weight[:, at : at + wide])
        unit, scale = standardize(x_ref[0].astype(f32))
        tokens_grad = ag_ref[0].astype(f32) + norm_back(grad, vec_ref[0:1], unit, scale)
        tg_ref[0] = tokens_grad.astype(bf16)

    one = lambda w: spec((1, step, w), lambda m, i: (m, i, 0))
    return call(
        kernel,
        shape((batch, rows, width), bf16),
        grid=(batch, rows // step),
        in_specs=[one(width), one(width), fixed(vectors.shape)]
        + [one(wide)] * (3 * BACK)
        + [hbm()] * (links.outer),
        out_specs=one(width),
        scratch=[
            pltpu.VMEM((width, 3 * width), bf16),
            pltpu.SemaphoreType.DMA((links.outer,)),
        ],
        name="finish",
        flops=6 * batch * rows * width * width,
        traffic=12 * batch * rows * width,
        after=after,
    )(
        tokens,
        attn_grad,
        vectors,
        *[v for group in groups for v in group],
        *first,
    )


def split_rows(value, send_ref, keep_ref):
    core = lax.axis_index("dp") % 2
    groups, block, _ = send_ref.shape
    for a in range(groups):
        low = value[2 * a * block : (2 * a + 1) * block]
        high = value[(2 * a + 1) * block : (2 * a + 2) * block]
        send_ref[a] = jnp.where(core == 0, high, low).astype(bf16)
        keep_ref[a] = jnp.where(core == 0, low, high).astype(bf16)


def qkv_grads(links, units, memory_low, groups, first, columns, sums, after=()):
    batch, rows, width = units.shape
    total = groups[0][1].shape[1]
    wide = width // BACK
    block = width // links.outer
    basis = memory_low.shape[1]
    count = 3 * BACK

    def kernel(u_ref, mem_ref, col_ref, sum_ref, *refs):
        sources, refs = refs[:count], refs[count:]
        parts, refs = refs[: links.outer], refs[links.outer :]
        send_ref, keep_ref, weight, ends, lines, *grads, sems, more_sems = refs
        step = pl.program_id(0)
        lane = lax.broadcasted_iota(jnp.int32, (1, 128), 1)
        across = lambda v: jnp.sum(v, axis=1, keepdims=True)
        down = lambda v: jnp.sum(v.astype(f32), axis=0, keepdims=True)
        fetch = lambda at: pltpu.make_async_copy(sources[at], grads[at], more_sems.at[at])
        for at in range(count):
            kind, g = at // BACK, at % BACK
            mine = slice(g * wide, (g + 1) * wide)

            @pl.when(step == at)
            def _(at=at, kind=kind, g=g, mine=mine):
                if at == 0:
                    fetch(0).start()
                    copies = links.load(parts, block, 0, weight, sems)
                    for later in range(1, count):
                        fetch(later).start()
                    lines[...] = jnp.zeros_like(lines)
                    lines[0:16] = sum_ref[...]
                    ends[...] = jnp.zeros_like(ends)
                fetch(at).wait()
                ref = grads[at]
                value = sum(dot_left(u_ref[m], ref[m, :rows]) for m in range(batch))
                line = sum(down(ref[m, :rows]) for m in range(batch))
                if at == 0:
                    wait(copies)
                w = weight[:, kind * width + g * wide : kind * width + (g + 1) * wide].astype(f32)
                ends[...] += jnp.where(
                    lane == 0, across(w * value), jnp.where(lane == 1, across(w * line), 0.0)
                )
                value = col_ref[:, 0:1] * value + col_ref[:, 1:2] * line
                if kind:
                    value += sum(dot_left(mem_ref[m], ref[m, rows:]) for m in range(batch))
                if kind == 0:
                    lines[2:3, mine] = line
                if kind == 2:
                    lines[3:4, mine] = line + sum(down(ref[m, rows:]) for m in range(batch))
                split_rows(value, send_ref, keep_ref)

        @pl.when(step == count)
        def _():
            value = lines[...].T + ends[...]
            split_rows(value, send_ref.at[:, :, 0:128], keep_ref.at[:, :, 0:128])

    out = spec((links.across, block, wide), lambda i: (0, 0, i))
    kinds = [(batch, rows, wide)] * BACK + [(batch, total, wide)] * (2 * BACK)
    return call(
        kernel,
        (shape((links.across, block, 3 * width + wide), bf16),) * 2,
        grid=(count + 1,),
        in_specs=[
            fixed((batch, rows, width)),
            fixed((batch, basis, width)),
            fixed(columns.shape),
            fixed(sums.shape),
        ]
        + [hbm()] * (count + links.outer),
        out_specs=(out, out),
        scratch=[
            pltpu.VMEM((width, 3 * width), bf16),
            pltpu.VMEM((width, 128), f32),
            pltpu.VMEM((128, width), f32),
        ]
        + [pltpu.VMEM(kind, bf16) for kind in kinds]
        + [pltpu.SemaphoreType.DMA((links.outer,)), pltpu.SemaphoreType.DMA((count,))],
        name="qkv_grads",
        flops=2 * batch * width * width * (3 * rows + 2 * basis),
        traffic=2 * batch * width * 7 * rows,
        after=after,
    )(
        units,
        memory_low,
        columns,
        sums,
        *[group[kind] for kind in range(3) for group in groups],
        *first,
    )


def body(links, tokens, cotangent, doc_start, memory_init, *shards):
    (
        norm1_gain,
        norm1_bias,
        qkv_weight,
        query_bias,
        value_bias,
        out_weight,
        out_bias,
        norm2_gain,
        norm2_bias,
        up_weight,
        up_bias,
        down_weight,
        down_bias,
    ) = shards
    own, width = out_weight.shape
    hidden = up_weight.shape[1]
    fold = hidden // width
    n = links.count
    tokens, cotangent, doc_start, memory_init = (
        tokens[:, 0],
        cotangent[:, 0],
        doc_start[:, 0],
        memory_init[0],
    )
    batch, rows, _ = tokens.shape

    small = (norm1_gain, norm1_bias, query_bias, value_bias, out_bias, norm2_gain, norm2_bias, down_bias)
    small = jnp.concatenate([jnp.stack(small).T, up_bias.reshape(own, fold)], axis=1)
    small = jnp.pad(small, ((0, 0), (0, 128 - small.shape[1])))
    wide = width // GROUPS
    positions = jnp.arange(rows)
    before = positions[None, :] <= positions[:, None]
    documents = jnp.sum(jnp.where(before, doc_start[:, None, :], 0), axis=2)
    documents = (documents[:, :, None], documents[:, None, :])

    carry_table, fresh_table = rbf_tables(rows, memory_init.shape[0])
    high = functools.partial(jnp.dot, precision=lax.Precision.HIGH)
    memories = [(memory_init,)]
    carried, gained, biased = memory_init, None, None
    for m in range(batch - 1):
        keep_share = jnp.where(documents[0][m, -1, 0] == 0, 1.0, 0.0)
        unit, _ = standardize(tokens[m].astype(f32))
        table = keep_share * carry_table
        carried = high(table, carried)
        new_gained = high(fresh_table, unit)
        new_biased = jnp.sum(fresh_table, axis=1, keepdims=True)
        if m:
            new_gained += high(table, gained)
            new_biased += high(table, biased)
        gained, biased = new_gained, new_biased
        memories.append((carried, gained, biased))

    flat = lambda v: v.reshape(batch * rows, v.shape[-1])
    full = lambda v: v.reshape(batch, rows, v.shape[-1])
    line = links.line(jnp.concatenate([qkv_weight, small], axis=1), [own], after=[carry_table])
    early = [v for memory in memories[1:] for v in memory] + list(documents)
    first = links.spread(line, early)
    unit = width // 2
    least = -(-(2**20) // (2 * links.deep * unit))
    packed = pack([out_weight, up_weight, down_weight], unit, -(-least // 16) * 16)
    packed = lax.all_gather(packed, "fsdp", axis=0, tiled=True)
    vectors, columns = unpack(links, first, width)
    made = project(links, tokens, memories, None, vectors, 0, first)
    queries, keys, values, units, memory_low = made
    line = regroup(links.deep, packed, 0, own, 2, 1 + fold, after=made[:1])
    mixture, inverse, exps = attend(queries, keys, values, *documents, after=[line])
    second = links.spread(line, [mixture])
    line = regroup(links.deep, packed, 2 * own * (1 + fold), fold * own, 2, 1, after=second)
    up_bias_full = columns[:, 8 : 8 + fold].reshape(1, hidden)
    cot = flat(cotangent)
    made = lift(
        links, flat(tokens), cot, flat(mixture), vectors, up_bias_full, second, hidden, after=[line]
    )
    residual, normed2, activated, slopes = made[:4]
    down_parts = made[4:]
    third, down_parts = links.spread(line, made[:1], down_parts)
    down_parts = links.merge_core(*down_parts, after=third[-1:])
    made = settle(
        links,
        residual,
        slopes,
        cot,
        flat(inverse),
        flat(mixture),
        normed2,
        vectors,
        second,
        third,
        hidden,
        after=down_parts[:1],
    )
    attn_grad, scaled, sums, up_sums = made[:4]
    up_parts = made[4:]
    sums = jnp.concatenate(
        [sums, up_sums[0].reshape(width, fold).T, jnp.zeros((8 - fold, width), f32)], axis=0
    )
    groups = []
    down_total = links.merge_columns(*down_parts, after=[attn_grad])
    up_parts = gate(up_parts, [down_total])
    hold = [down_total]
    pairs = width // PAIR // BACK
    for g in range(BACK):
        groups.append(
            attend_back(
                queries, keys, values, exps, mixture, full(scaled), g * pairs, pairs, after=hold
            )
        )
        hold = list(groups[-1][:1])
        if g == 0:
            up_parts = links.merge_core(*up_parts, after=hold)
            hold = [up_parts[0]]
    down_grad = links.merge_deep(down_total)
    qkv_parts = qkv_grads(links, units, memory_low, groups, first, columns, sums)
    up_total = links.merge_columns(*up_parts, after=qkv_parts[:1])
    up_grad = links.merge_deep(up_total)
    qkv_parts = links.merge_core(*qkv_parts, 3 * width + 128, after=[up_total, down_grad])
    output = emit(links, residual, activated, vectors, third, after=qkv_parts[:1])
    tokens_grad = finish(links, tokens, full(attn_grad), groups, vectors, first, after=[output])
    qkv_parts = links.merge_line(*qkv_parts, after=[tokens_grad, up_grad])
    qkv_grad = links.merge_depth(*qkv_parts)
    vec = [qkv_grad[:, 3 * width + k] for k in range(8)]
    lead = lambda v: v[:, None]
    return (
        lead(full(output)),
        lead(tokens_grad),
        vec[0],
        vec[1],
        qkv_grad[:, : 3 * width],
        vec[2],
        vec[3],
        up_grad[:, hidden:],
        vec[4],
        vec[5],
        vec[6],
        up_grad[:, :hidden],
        qkv_grad[:, 3 * width + 8 : 3 * width + 8 + fold].reshape(fold * own),
        down_grad,
        vec[7],
    )


def solution(mesh):
    both = ("dp", "fsdp")
    vector, matrix = P(both), P(both, None)
    params = (
        vector,
        vector,
        matrix,
        vector,
        vector,
        matrix,
        vector,
        vector,
        vector,
        matrix,
        vector,
        matrix,
        vector,
    )
    stream = P(None, both, None, None)
    return jax.shard_map(
        functools.partial(body, Links(mesh)),
        mesh=mesh,
        in_specs=(stream, stream, P(None, both, None), P(both, None, None)) + params,
        out_specs=(stream, stream) + params,
        check_vma=False,
    )
```

```python
import functools

import jax
import jax.numpy as jnp
from jax import lax
from jax.experimental import pallas as pl
from jax.experimental.pallas import tpu as pltpu
from jax.sharding import PartitionSpec as P

HD = 64
PAIR = 2 * HD
GROUPS = 1
BACK = 2
STEP = 2
epsilon = 1e-05
hidden_score = -1e30
bf16 = jnp.bfloat16
f32 = jnp.float32
VMEM = 64 * 2**20


def dot(left, right):
    return jnp.dot(left, right, preferred_element_type=f32)


def dot_right(left, right):
    return lax.dot_general(left, right, (((1,), (1,)), ((), ())), preferred_element_type=f32)


def dot_left(left, right):
    return lax.dot_general(left, right, (((0,), (0,)), ((), ())), preferred_element_type=f32)


def call(
    kernel,
    out_shape,
    *,
    grid=(1,),
    in_specs,
    out_specs,
    scratch=(),
    name,
    flops,
    traffic,
    exps=0,
    after=(),
):
    count = len(in_specs)

    def run(*refs):
        return kernel(*refs[:count], *refs[count + len(after) :])

    made = pl.pallas_call(
        run,
        out_shape=out_shape,
        grid=grid,
        in_specs=list(in_specs) + [hbm()] * len(after),
        out_specs=out_specs,
        scratch_shapes=list(scratch),
        compiler_params=pltpu.CompilerParams(vmem_limit_bytes=VMEM),
        cost_estimate=pl.CostEstimate(flops=flops, bytes_accessed=traffic, transcendentals=exps),
        name=name,
    )
    return lambda *operands: made(*operands, *after)


def shape(dims, dtype):
    return jax.ShapeDtypeStruct(dims, dtype)


def hbm():
    return pl.BlockSpec(memory_space=pl.ANY)


def spec(block, index):
    return pl.BlockSpec(block, index)


def fixed(dims):
    return pl.BlockSpec(dims, lambda *_: (0,) * len(dims))


class Links:
    def __init__(self, mesh):
        self.outer = mesh.shape["dp"]
        self.across = self.outer // 2
        self.deep = mesh.shape["fsdp"]
        self.count = self.outer * self.deep

    def place(self):
        outer = lax.axis_index("dp")
        return (outer // 2, outer % 2, lax.axis_index("fsdp"))

    def swap(self, value, column=0, core=0, depth=0):
        pairs = []
        for device in range(self.count):
            outer, inner = divmod(device, self.deep)
            target = (((outer // 2) ^ column) * 2 + ((outer % 2) ^ core)) * self.deep + (
                inner ^ depth
            )
            pairs.append((device, target))
        return lax.ppermute(value, ("dp", "fsdp"), pairs)

    def line(self, shard, segments, after=()):
        pieces = [shard] + [self.swap(shard, depth=s) for s in range(1, self.deep)]
        rows, width = shard.shape

        def kernel(*refs):
            target = refs[self.deep]
            depth = lax.axis_index("fsdp")
            values = [ref[...].astype(f32) for ref in refs[: self.deep]]
            turned = []
            for j in range(self.deep):
                value = values[0]
                for s in range(1, self.deep):
                    value = jnp.where(depth == s ^ j, values[s], value)
                turned.append(value)
            out = []
            at = 0
            for count in segments:
                out += [value[at : at + count] for value in turned]
                at += count
            target[...] = jnp.concatenate(out, axis=0).astype(bf16)

        return call(
            kernel,
            shape((self.deep * rows, width), bf16),
            in_specs=[fixed((rows, width))] * self.deep,
            out_specs=fixed((self.deep * rows, width)),
            name="line",
            flops=self.deep**2 * rows * width,
            traffic=4 * self.deep * rows * width,
            after=after,
        )(*pieces)

    def spread(self, line, after=(), along=()):
        lines = [line] + [self.swap(line, column=s) for s in range(1, self.across)]
        extra = []
        if after:
            lines = gate(lines + list(along), after)
            lines, extra = lines[: self.across], lines[self.across :]
        out = []
        for part in lines:
            out += [part, self.swap(part, core=1)]
        return (out, extra) if along else out

    def merge_core(self, send, keep, used=None, after=()):
        across, rows, width = send.shape
        came = self.swap(send, core=1)
        if used is None:
            units = width // 128
            used, tile = width, 128 * max(k for k in range(1, 7) if units % k == 0)
        else:
            tile = used

        def kernel(keep_ref, came_ref, *outs):
            column = lax.axis_index("dp") // 2
            for s in range(across):
                value = keep_ref[column ^ s, :, :tile].astype(f32)
                value = value + came_ref[column ^ s, :, :tile].astype(f32)
                outs[s][...] = value.astype(outs[s].dtype)

        whole = pl.BlockSpec((across, rows, tile if tile < used else width), lambda i: (0, 0, i))
        part = pl.BlockSpec((rows, tile), lambda i: (0, i))
        return call(
            kernel,
            (shape((rows, used), f32),) + (shape((rows, used), bf16),) * (across - 1),
            grid=(used // tile,),
            in_specs=[whole, whole],
            out_specs=(part,) * across,
            name="merge_core",
            flops=across * rows * width,
            traffic=6 * across * rows * width,
            after=after,
        )(keep, came)

    def merge_columns(self, own, *sends, after=()):
        came = [self.swap(sends[s - 1], column=s) for s in range(1, self.across)]
        rows, width = own.shape
        tile = 768 if width % 768 == 0 else 128

        def kernel(own_ref, *refs):
            total = own_ref[...]
            for ref in refs[:-1]:
                total = total + ref[...].astype(f32)
            refs[-1][...] = total

        part = pl.BlockSpec((rows, tile), lambda i: (0, i))
        return call(
            kernel,
            shape((rows, width), f32),
            grid=(width // tile,),
            in_specs=[part] * self.across,
            out_specs=part,
            name="merge_columns",
            flops=self.across * rows * width,
            traffic=14 * rows * width,
            after=after,
        )(own, *came)

    def merge_deep(self, total):
        return lax.psum_scatter(total, "fsdp", scatter_dimension=0, tiled=True)

    def merge_line(self, own, *sends, after=()):
        came = [self.swap(sends[s - 1], column=s) for s in range(1, self.across)]
        rows, width = own.shape
        main = rows // self.deep

        def kernel(own_ref, *refs):
            total = own_ref[...]
            for ref in refs[: self.across - 1]:
                total = total + ref[...].astype(f32)
            outs = refs[self.across - 1 :]
            parts = [total[j * main : (j + 1) * main] for j in range(self.deep)]
            depth = lax.axis_index("fsdp")
            for s in range(self.deep):
                value = parts[0]
                for j in range(1, self.deep):
                    value = jnp.where(depth == s ^ j, parts[j], value)
                outs[s][...] = value.astype(outs[s].dtype)

        return call(
            kernel,
            (shape((main, width), f32),) + (shape((main, width), bf16),) * (self.deep - 1),
            in_specs=[fixed((rows, width))] * self.across,
            out_specs=(fixed((main, width)),) * self.deep,
            name="merge_line",
            flops=(self.across + self.deep) * rows * width,
            traffic=14 * rows * width,
            after=after,
        )(own, *came)

    def merge_depth(self, own, *sends):
        came = [self.swap(sends[s - 1], depth=s) for s in range(1, self.deep)]
        return sum((part.astype(f32) for part in came), own)

    def load(self, parts, rows, at, target, sems, base=0, start=True):
        outer = lax.axis_index("dp")
        copies = []
        for k, part in enumerate(parts):
            spot = pl.multiple_of((outer ^ k) * rows, 16)
            copies.append(
                pltpu.make_async_copy(
                    part.at[pl.ds(at, rows), pl.ds(0, target.shape[1])],
                    target.at[pl.ds(spot, rows)],
                    sems.at[base + k],
                )
            )
        if start:
            for copy in copies:
                copy.start()
        return copies


def rbf_tables(seg_rows, basis):
    centers = (jnp.arange(basis, dtype=f32) + 0.5) / basis

    def bumps(points):
        return jnp.exp(-0.5 * jnp.square((centers[:, None] - points[None, :]) * basis))

    old_points = 0.75 * centers
    new_points = 0.75 + 0.25 * (jnp.arange(seg_rows, dtype=f32) + 0.5) / seg_rows
    phi_old = bumps(old_points)
    phi_new = bumps(new_points)
    totals = jnp.sum(phi_old, axis=1) + jnp.sum(phi_new, axis=1)
    recon = bumps(centers)
    recon = recon / jnp.sum(recon, axis=0, keepdims=True)
    carry_table = jnp.dot(phi_old, recon.T, precision=lax.Precision.HIGH) / totals[:, None]
    fresh_table = phi_new / totals[:, None]
    return (carry_table, fresh_table)


def standardize(values):
    center = values - jnp.mean(values, axis=-1, keepdims=True)
    spread = jnp.mean(center * center, axis=-1, keepdims=True)
    scale = lax.rsqrt(spread + epsilon)
    return (center * scale, scale)


def norm_back(grad, gain, unit, scale):
    inner = grad * gain
    shift = jnp.mean(inner, axis=-1, keepdims=True)
    slope = jnp.mean(inner * unit, axis=-1, keepdims=True)
    return (inner - shift - unit * slope) * scale


def gate(values, after):
    count = len(values)

    def kernel(*refs):
        pass

    return pl.pallas_call(
        kernel,
        out_shape=[shape(v.shape, v.dtype) for v in values],
        in_specs=[hbm()] * (count + len(after)),
        out_specs=[hbm()] * count,
        input_output_aliases={k: k for k in range(count)},
        name="gate",
    )(*values, *after)


def pack(pieces, width, least, after=()):
    rows = max(sum(v.size for v in pieces) // width, least)

    def kernel(*refs):
        value = [ref[...].astype(f32) for ref in refs[:-1]]
        value = [
            v[:, k * width : (k + 1) * width] for v in value for k in range(v.shape[1] // width)
        ]
        value = jnp.concatenate(value, axis=0).astype(bf16)
        refs[-1][: value.shape[0]] = value
        if value.shape[0] < rows:
            refs[-1][value.shape[0] :] = jnp.zeros((rows - value.shape[0], width), bf16)

    return call(
        kernel,
        shape((rows, width), bf16),
        in_specs=[fixed(v.shape) for v in pieces],
        out_specs=fixed((rows, width)),
        name="pack",
        flops=rows * width,
        traffic=4 * rows * width,
        after=after,
    )(*pieces)


def regroup(deep, packed, first, height, blocks, segments, after=()):
    step, unit = packed.shape[0] // deep, packed.shape[1]
    rows, width = segments * deep * height, blocks * unit

    def kernel(packed_ref, target_ref):
        out = []
        for segment in range(segments):
            for z in range(deep):
                at = z * step + first + segment * blocks * height
                row = [
                    packed_ref[at + k * height : at + (k + 1) * height].astype(f32)
                    for k in range(blocks)
                ]
                out.append(jnp.concatenate(row, axis=1))
        target_ref[...] = jnp.concatenate(out, axis=0).astype(bf16)

    return call(
        kernel,
        shape((rows, width), bf16),
        in_specs=[fixed(packed.shape)],
        out_specs=fixed((rows, width)),
        name="regroup",
        flops=rows * width,
        traffic=4 * rows * width,
        after=after,
    )(packed)


def unpack(links, parts, width):
    line_rows = width // links.outer
    at = parts[0].shape[1] // 128 - 1

    def kernel(*refs):
        parts, (rows_ref, cols_ref) = refs[: links.outer], refs[links.outer :]
        outer = lax.axis_index("dp")
        for k, part in enumerate(parts):
            spot = pl.multiple_of((outer ^ k) * line_rows, 8)
            cols_ref[pl.ds(spot, line_rows)] = part[...].astype(f32)
        rows_ref[...] = cols_ref[...].T[:16]

    return call(
        kernel,
        (shape((16, width), f32), shape((width, 128), f32)),
        in_specs=[spec((line_rows, 128), lambda i: (0, at))] * links.outer,
        out_specs=(fixed((16, width)), fixed((width, 128))),
        name="unpack",
        flops=width * 128,
        traffic=8 * width * 128,
    )(*parts)


def project(links, tokens, memories, memory_low, vectors, group, parts, after=()):
    batch, rows, width = tokens.shape
    line_rows = width // links.outer
    wide = width // GROUPS
    leads = [v for memory in memories for v in memory] if memory_low is None else [memory_low]
    basis = leads[0].shape[-2]
    mine = slice(group * wide, (group + 1) * wide)

    def kernel(tokens_ref, vec_ref, *refs):
        lead, refs = refs[: len(leads)], refs[len(leads) :]
        parts, refs = refs[: links.outer], refs[links.outer :]
        q_ref, k_ref, v_ref = refs[:3]
        weight, sems = refs[-2:]
        step = pl.program_id(0)

        @pl.when(step == 0)
        def _():
            for copy in links.load(parts, line_rows, 0, weight, sems):
                copy.wait()

        vec = vec_ref[...]
        if memory_low is None:
            unit_ref, low_ref = refs[3:5]
            at = 0
            for m, memory in enumerate(memories):

                @pl.when(step == m)
                def _(at=at, memory=memory):
                    value = lead[at][...]
                    if len(memory) > 1:
                        value = value + lead[at + 1][...] * vec[0:1] + lead[at + 2][...] * vec[1:2]
                    low_ref[0] = value.astype(bf16)

                at += len(memory)
        else:
            low_ref = lead[0]
        unit, _ = standardize(tokens_ref[0].astype(f32))
        normed = (unit * vec[0:1] + vec[1:2]).astype(bf16)
        if memory_low is None:
            unit_ref[0] = unit.astype(bf16)
        memory = low_ref[0]
        q_ref[0] = ((dot(normed, weight[:, :wide]) + vec[2:3, mine]) * 0.125).astype(bf16)
        k_ref[0, :rows] = dot(normed, weight[:, wide : 2 * wide]).astype(bf16)
        v_ref[0, :rows] = (dot(normed, weight[:, 2 * wide :]) + vec[3:4, mine]).astype(bf16)
        k_ref[0, rows:] = dot(memory, weight[:, wide : 2 * wide]).astype(bf16)
        v_ref[0, rows:] = (dot(memory, weight[:, 2 * wide :]) + vec[3:4, mine]).astype(bf16)

    keys = rows + basis
    one = lambda r, w: spec((1, r, w), lambda m: (m, 0, 0))
    kinds = [(rows, wide), (keys, wide), (keys, wide)]
    if memory_low is None:
        kinds += [(rows, width), (basis, width)]
        lead_specs = [fixed(v.shape) for v in leads]
    else:
        lead_specs = [one(basis, width)]
    return call(
        kernel,
        tuple(shape((batch, r, w), bf16) for r, w in kinds),
        grid=(batch,),
        in_specs=[one(rows, width), fixed(vectors.shape)] + lead_specs + [hbm()] * links.outer,
        out_specs=tuple(one(r, w) for r, w in kinds),
        scratch=[pltpu.VMEM((width, 3 * wide), bf16), pltpu.SemaphoreType.DMA((links.outer,))],
        name="project",
        flops=2 * batch * width * wide * (3 * rows + 2 * basis),
        traffic=2 * (batch * width * 8 * rows + 3 * width * wide),
        after=after,
    )(tokens, vectors, *leads, *parts)


def lanes(head):
    lane = lax.broadcasted_iota(jnp.int32, (1, PAIR), 1)
    return (lane // HD == head, (lane == (1 - head) * HD))


def attend(queries, keys, values, starts_col, starts_row, after=()):
    batch, rows, width = queries.shape
    total = keys.shape[1]
    heads = width // HD
    half = rows // 2

    def kernel(q_ref, k_ref, v_ref, col_ref, row_ref, mix_ref, inv_ref, e_ref, mask):
        @pl.when(pl.program_id(1) == 0)
        def _():
            i = lax.broadcasted_iota(jnp.int32, (rows, rows), 0)
            j = lax.broadcasted_iota(jnp.int32, (rows, rows), 1)
            allowed = (j <= i) & (col_ref[0] == row_ref[0])
            mask[...] = jnp.where(allowed, 0.0, hidden_score)

        memory_bias = jnp.where(col_ref[0] == 0, 0.0, hidden_score).astype(bf16)
        for pair in range(STEP):
            mine = slice(pair * PAIR, (pair + 1) * PAIR)
            q, k, v = q_ref[0, :, mine], k_ref[0, :, mine], v_ref[0, :, mine]
            outs = []
            for head in range(2):
                inside, first = lanes(head)
                qh = jnp.where(inside, q, jnp.where(first, memory_bias, 0).astype(bf16))
                kl = jnp.where(inside, k[:rows], 0).astype(bf16)
                km = jnp.where(inside, k[rows:], jnp.where(first, 1, 0).astype(bf16))
                vh = jnp.where(inside, v, 1).astype(bf16)
                parts = []
                for block in range(2):
                    top, wide = block * half, (block + 1) * half
                    here = qh[top : top + half]
                    sl = dot_right(here, kl[:wide]) + mask[top : top + half, :wide]
                    sm = dot_right(here, km)
                    peak = jnp.maximum(
                        jnp.max(sl, axis=-1, keepdims=True), jnp.max(sm, axis=-1, keepdims=True)
                    )
                    el = jnp.exp(sl - peak).astype(bf16)
                    em = jnp.exp(sm - peak).astype(bf16)
                    e_ref[0, 2 * pair + head, top : top + half, :wide] = el
                    e_ref[0, 2 * pair + head, top : top + half, rows:] = em
                    parts.append(dot(el, vh[:wide]) + dot(em, vh[rows:]))
                outs.append(jnp.concatenate(parts, axis=0))
            inside, _ = lanes(0)
            mixed = jnp.where(inside, outs[0], outs[1])
            inverse = 1.0 / pltpu.roll(jnp.where(inside, outs[1], outs[0]), HD, 1)
            mix_ref[0, :, mine] = (mixed * inverse).astype(bf16)
            inv_ref[0, :, mine] = inverse

    pair = lambda r: spec((1, r, STEP * PAIR), lambda m, p: (m, 0, p))
    return call(
        kernel,
        (
            shape((batch, rows, width), bf16),
            shape((batch, rows, width), f32),
            shape((batch, heads, rows, total), bf16),
        ),
        grid=(batch, heads // 2 // STEP),
        in_specs=[
            pair(rows),
            pair(total),
            pair(total),
            spec((1, rows, 1), lambda m, p: (m, 0, 0)),
            spec((1, 1, rows), lambda m, p: (m, 0, 0)),
        ],
        out_specs=(
            pair(rows),
            pair(rows),
            spec((1, 2 * STEP, rows, total), lambda m, p: (m, p, 0, 0)),
        ),
        scratch=[pltpu.VMEM((rows, rows), f32)],
        name="attend",
        flops=16 * batch * heads * rows * total * HD,
        traffic=2 * batch * heads * rows * total,
        exps=batch * heads * rows * total,
        after=after,
    )(queries, keys, values, starts_col, starts_row)


def attend_back(queries, keys, values, exps, mixture, scaled, base, count, after=()):
    batch, rows, width = queries.shape
    total = keys.shape[1]
    half = rows // 2

    def kernel(q_ref, k_ref, v_ref, e_ref, mix_ref, g_ref, dq_ref, dk_ref, dv_ref):
        q, k, v, g = q_ref[0], k_ref[0], v_ref[0], g_ref[0]
        product = -(g.astype(f32) * mix_ref[0].astype(f32))
        product = pltpu.roll(product, HD, 1).astype(bf16)
        dqs, dks, dvs = [], [], []
        for head in range(2):
            inside, _ = lanes(head)
            gh = jnp.where(inside, g, product)
            vh = jnp.where(inside, v, 1).astype(bf16)
            near = (e_ref[0, head, :, :half].astype(f32) * dot_right(gh, vh[:half])).astype(bf16)
            late = e_ref[0, head, half:, half:rows].astype(f32) * dot_right(gh[half:], vh[half:rows])
            late = late.astype(bf16)
            far = (e_ref[0, head, :, rows:].astype(f32) * dot_right(gh, vh[rows:])).astype(bf16)
            mixed = dot(near, k[:half]) + dot(far, k[rows:])
            dqs.append(
                jnp.concatenate([mixed[:half], mixed[half:] + dot(late, k[half:rows])], axis=0)
            )
            e = e_ref[0, head]
            dks.append(
                [
                    dot_left(near, q),
                    dot_left(late, q[half:]),
                    dot_left(far, q),
                ]
            )
            dvs.append(
                [
                    dot_left(e[:, :half], g),
                    dot_left(e[half:, half:rows], g[half:]),
                    dot_left(e[:, rows:], g),
                ]
            )
        inside, _ = lanes(0)
        dq_ref[0] = (jnp.where(inside, dqs[0], dqs[1]) * 0.125).astype(bf16)
        for ref, pieces in ((dk_ref, dks), (dv_ref, dvs)):
            for i, (lo, hi) in enumerate(((0, half), (half, rows), (rows, total))):
                ref[0, lo:hi] = jnp.where(inside, pieces[0][i], pieces[1][i]).astype(bf16)

    pair = lambda r: spec((1, r, PAIR), lambda m, p: (m, 0, p + base))
    out = lambda r: spec((1, r, PAIR), lambda m, p: (m, 0, p))
    return call(
        kernel,
        (
            shape((batch, rows, count * PAIR), bf16),
            shape((batch, total, count * PAIR), bf16),
            shape((batch, total, count * PAIR), bf16),
        ),
        grid=(batch, count),
        in_specs=[
            pair(rows),
            pair(total),
            pair(total),
            spec((1, 2, rows, total), lambda m, p: (m, p + base, 0, 0)),
            pair(rows),
            pair(rows),
        ],
        out_specs=(out(rows), out(total), out(total)),
        name="attend_back",
        flops=64 * batch * count * rows * total * HD,
        traffic=4 * batch * count * rows * total,
        after=after,
    )(queries, keys, values, exps, mixture, scaled)


def tops(links, parts, rows, out_w, up_w, sems):
    copies = links.load(parts, rows, 0, out_w, sems)
    for j in range(up_w.shape[0]):
        copies += links.load(parts, rows, (1 + j) * rows, up_w.at[j], sems, (1 + j) * links.outer)
    return copies


def wait(copies):
    for copy in copies:
        copy.wait()


def lift(links, tokens, cot, mixture, vectors, up_bias, second, hidden, after=()):
    rows, width = tokens.shape
    fold = hidden // width
    line_rows = width // links.outer
    block = hidden // links.outer
    step = 256
    steps = rows // step

    def kernel(x_ref, cot_ref, mix_ref, vec_ref, bias_ref, *refs):
        parts, refs = refs[: links.outer], refs[links.outer :]
        res_ref, n_ref, act_ref, slope_ref, send_ref, keep_ref, acts, out_w, up_w, sems = refs
        at = pl.program_id(0)

        @pl.when(at < steps)
        def _():
            @pl.when(at == 0)
            def _():
                wait(tops(links, parts, line_rows, out_w, up_w, sems))

            residual = x_ref[...].astype(f32) + vec_ref[4:5] + dot(mix_ref[...], out_w[...])
            res_ref[...] = residual
            unit, _ = standardize(residual)
            normed = (unit * vec_ref[5:6] + vec_ref[6:7]).astype(bf16)
            n_ref[...] = normed
            here = pl.ds(pl.multiple_of(at * step, step), step)
            for j in range(fold):
                cols = slice(j * width, (j + 1) * width)
                u = dot(normed, up_w[j]) + bias_ref[:, cols]
                c0 = 0.7978845608028654
                square = u * u
                t = jnp.tanh(u * (c0 + (c0 * 0.044715) * square))
                half_up = 0.5 + 0.5 * t
                low = (u * half_up).astype(bf16)
                act_ref[:, cols] = low
                acts[j, here] = low
                slope = half_up + (u * (c0 + (3 * c0 * 0.044715) * square)) * (half_up * (1.0 - t))
                slope_ref[:, cols] = slope.astype(bf16)

        for j in range(fold):

            @pl.when(at == steps + j)
            def _(j=j):
                split_rows(dot_left(acts[j], cot_ref[...]), send_ref, keep_ref)

    early = lambda w: spec((step, w), lambda i: (jnp.minimum(i, steps - 1), 0))
    late = spec((width // (2 * block), block, width), lambda i: (jnp.maximum(i - steps, 0), 0, 0))
    return call(
        kernel,
        (
            shape((rows, width), f32),
            shape((rows, width), bf16),
            shape((rows, hidden), bf16),
            shape((rows, hidden), bf16),
        )
        + (shape((links.across, block, width), bf16),) * 2,
        grid=(steps + fold,),
        in_specs=[
            early(width),
            fixed((rows, width)),
            early(width),
            fixed(vectors.shape),
            fixed(up_bias.shape),
        ]
        + [hbm()] * links.outer,
        out_specs=(early(width), early(width), early(hidden), early(hidden), late, late),
        scratch=[
            pltpu.VMEM((fold, rows, width), bf16),
            pltpu.VMEM((width, width), bf16),
            pltpu.VMEM((fold, width, width), bf16),
            pltpu.SemaphoreType.DMA(((1 + fold) * links.outer,)),
        ],
        name="lift",
        flops=2 * rows * width * (width + 2 * hidden),
        traffic=4 * rows * hidden + 10 * rows * width,
        exps=rows * hidden,
        after=after,
    )(tokens, cot, mixture, vectors, up_bias, *second)


def settle(links, residual, slopes, cot, inverse, mixture, normed2, vectors, second, third, hidden, after=()):
    rows, width = residual.shape
    fold = hidden // width
    line_rows = width // links.outer
    step = 256
    steps = rows // step

    def kernel(res_ref, slope_ref, cot_ref, inv_ref, mix_ref, n_ref, vec_ref, *refs):
        parts, refs = refs[: links.outer], refs[links.outer :]
        lasts, refs = refs[: links.outer], refs[links.outer :]
        ag_ref, mg_ref, sums_ref, ub_ref, send_ref, keep_ref = refs[:6]
        ups, ags, out_w, up_w, down_w, sems = refs[6:]
        at = pl.program_id(0)

        @pl.when(at < steps)
        def _():
            @pl.when(at == 0)
            def _():
                copies = links.load(lasts, fold * line_rows, 0, down_w, sems, (1 + fold) * links.outer)
                wait(copies + tops(links, parts, line_rows, out_w, up_w, sems))
                sums_ref[...] = jnp.zeros_like(sums_ref)
                ub_ref[...] = jnp.zeros_like(ub_ref)

            residual = res_ref[...]
            cot = cot_ref[...]
            cot_f = cot.astype(f32)
            into = jnp.zeros((step, width), f32)
            here = pl.ds(pl.multiple_of(at * step, step), step)
            for j in range(fold):
                cols = slice(j * width, (j + 1) * width)
                grad = dot_right(cot, down_w[cols, :]) * slope_ref[:, cols].astype(f32)
                low = grad.astype(bf16)
                ups[j, here] = low
                ub_ref[0:1, cols] += jnp.sum(grad, axis=0, keepdims=True)
                into += dot_right(low, up_w[j])

            unit, scale = standardize(residual)
            residual_grad = cot_f + norm_back(into, vec_ref[5:6], unit, scale)
            low = residual_grad.astype(bf16)
            ag_ref[...] = low
            ags[here] = low
            mg_ref[...] = (dot_right(low, out_w[...]) * inv_ref[...]).astype(bf16)
            total = lambda v: jnp.sum(v, axis=0, keepdims=True)
            sums_ref[4:5] += total(residual_grad)
            sums_ref[5:6] += total(into * unit)
            sums_ref[6:7] += total(into)
            sums_ref[7:8] += total(cot_f)

        for j in range(fold):

            @pl.when(at == steps + j)
            def _(j=j):
                split_rows(dot_left(n_ref[...], ups[j]), send_ref, keep_ref)

        @pl.when(at == steps + fold)
        def _():
            split_rows(dot_left(mix_ref[...], ags[...]), send_ref, keep_ref)

    early = lambda w: spec((step, w), lambda i: (jnp.minimum(i, steps - 1), 0))
    late = spec((links.across, line_rows, width), lambda i: (0, 0, jnp.maximum(i - steps, 0)))
    return call(
        kernel,
        (shape((rows, width), bf16),) * 2
        + (shape((8, width), f32), shape((8, hidden), f32))
        + (shape((links.across, line_rows, width + hidden), bf16),) * 2,
        grid=(steps + fold + 1,),
        in_specs=[
            early(width),
            early(hidden),
            early(width),
            early(width),
            fixed((rows, width)),
            fixed((rows, width)),
            fixed(vectors.shape),
        ]
        + [hbm()] * (2 * links.outer),
        out_specs=(early(width),) * 2 + (fixed((8, width)), fixed((8, hidden)), late, late),
        scratch=[
            pltpu.VMEM((fold, rows, width), bf16),
            pltpu.VMEM((rows, width), bf16),
            pltpu.VMEM((width, width), bf16),
            pltpu.VMEM((fold, width, width), bf16),
            pltpu.VMEM((hidden, width), bf16),
            pltpu.SemaphoreType.DMA(((2 + fold) * links.outer,)),
        ],
        name="settle",
        flops=2 * rows * width * (2 * width + 3 * hidden),
        traffic=2 * rows * hidden + 14 * rows * width,
        after=after,
    )(residual, slopes, cot, inverse, mixture, normed2, vectors, *second, *third)


def close(links, residual, activated, tokens, attn_grad, groups, vectors, third, first, after=()):
    rows, width = residual.shape
    hidden = activated.shape[1]
    line_rows = width // links.outer
    wide = width // BACK
    each = groups[0][0].shape[1]
    step = 256
    steps = rows // step
    half = each // step

    def kernel(res_ref, act_ref, x_ref, ag_ref, vec_ref, *refs):
        grads, refs = refs[: 3 * BACK], refs[3 * BACK :]
        lasts, refs = refs[: links.outer], refs[links.outer :]
        parts, refs = refs[: links.outer], refs[links.outer :]
        y_ref, tg_ref, down_w, weight, sems = refs
        at = pl.program_id(0)
        qkv_load = lambda start: links.load(parts, line_rows, 0, weight, sems, links.outer, start)

        @pl.when(at < steps)
        def _():
            @pl.when(at == 0)
            def _():
                copies = links.load(lasts, hidden // links.outer, 0, down_w, sems)
                qkv_load(True)
                wait(copies)

            y_ref[...] = (res_ref[...] + dot(act_ref[...], down_w[...]) + vec_ref[7:8]).astype(bf16)

        @pl.when(at >= steps)
        def _():
            @pl.when(at == steps)
            def _():
                wait(qkv_load(False))

            left = [grads[3 * g + kind][0] for kind in range(3) for g in range(BACK)]
            grad = dot_right(jnp.concatenate(left, axis=1), weight[...])
            unit, scale = standardize(x_ref[...].astype(f32))
            tokens_grad = ag_ref[...].astype(f32) + norm_back(grad, vec_ref[0:1], unit, scale)
            tg_ref[...] = tokens_grad.astype(bf16)

    turn = lambda i: jnp.maximum(i - steps, 0)
    early = lambda w: spec((step, w), lambda i: (jnp.minimum(i, steps - 1), 0))
    late = lambda w: spec((step, w), lambda i: (turn(i), 0))
    some = spec((1, step, wide), lambda i: (turn(i) // half, turn(i) % half, 0))
    return call(
        kernel,
        (shape((rows, width), bf16),) * 2,
        grid=(2 * steps,),
        in_specs=[early(width), early(hidden), late(width), late(width), fixed(vectors.shape)]
        + [some] * (3 * BACK)
        + [hbm()] * (2 * links.outer),
        out_specs=(early(width), late(width)),
        scratch=[
            pltpu.VMEM((hidden, width), bf16),
            pltpu.VMEM((width, 3 * width), bf16),
            pltpu.SemaphoreType.DMA((2 * links.outer,)),
        ],
        name="close",
        flops=2 * rows * width * (hidden + 3 * width),
        traffic=2 * rows * hidden + 20 * rows * width,
        after=after,
    )(
        residual,
        activated,
        tokens,
        attn_grad,
        vectors,
        *[v for group in groups for v in group],
        *third,
        *first,
    )


def split_rows(value, send_ref, keep_ref):
    core = lax.axis_index("dp") % 2
    groups, block, _ = send_ref.shape
    for a in range(groups):
        low = value[2 * a * block : (2 * a + 1) * block]
        high = value[(2 * a + 1) * block : (2 * a + 2) * block]
        send_ref[a] = jnp.where(core == 0, high, low).astype(bf16)
        keep_ref[a] = jnp.where(core == 0, low, high).astype(bf16)


def qkv_grads(links, units, memory_low, groups, first, columns, sums, after=()):
    batch, rows, width = units.shape
    total = groups[0][1].shape[1]
    wide = width // BACK
    block = width // links.outer
    basis = memory_low.shape[1]
    count = 3 * BACK

    def kernel(u_ref, mem_ref, col_ref, sum_ref, *refs):
        sources, refs = refs[:count], refs[count:]
        parts, refs = refs[: links.outer], refs[links.outer :]
        send_ref, keep_ref, weight, ends, lines, *grads, sems, more_sems = refs
        step = pl.program_id(0)
        lane = lax.broadcasted_iota(jnp.int32, (1, 128), 1)
        across = lambda v: jnp.sum(v, axis=1, keepdims=True)
        down = lambda v: jnp.sum(v.astype(f32), axis=0, keepdims=True)
        fetch = lambda at: pltpu.make_async_copy(sources[at], grads[at], more_sems.at[at])
        for at in range(count):
            kind, g = at // BACK, at % BACK
            mine = slice(g * wide, (g + 1) * wide)

            @pl.when(step == at)
            def _(at=at, kind=kind, g=g, mine=mine):
                if at == 0:
                    fetch(0).start()
                    copies = links.load(parts, block, 0, weight, sems)
                    for later in range(1, count):
                        fetch(later).start()
                    lines[...] = jnp.zeros_like(lines)
                    lines[0:16] = sum_ref[...]
                    ends[...] = jnp.zeros_like(ends)
                fetch(at).wait()
                ref = grads[at]
                local = jnp.concatenate([ref[m, :rows] for m in range(batch)], axis=0)
                value = dot_left(u_ref[...].reshape(batch * rows, width), local)
                line = sum(down(ref[m, :rows]) for m in range(batch))
                if at == 0:
                    wait(copies)
                w = weight[:, kind * width + g * wide : kind * width + (g + 1) * wide].astype(f32)
                ends[...] += jnp.where(
                    lane == 0, across(w * value), jnp.where(lane == 1, across(w * line), 0.0)
                )
                value = col_ref[:, 0:1] * value + col_ref[:, 1:2] * line
                if kind:
                    far = jnp.concatenate([ref[m, rows:] for m in range(batch)], axis=0)
                    value += dot_left(mem_ref[...].reshape(batch * basis, width), far)
                if kind == 0:
                    lines[2:3, mine] = line
                if kind == 2:
                    lines[3:4, mine] = line + sum(down(ref[m, rows:]) for m in range(batch))
                split_rows(value, send_ref, keep_ref)

        @pl.when(step == count)
        def _():
            value = lines[...].T + ends[...]
            split_rows(value, send_ref.at[:, :, 0:128], keep_ref.at[:, :, 0:128])

    out = spec((links.across, block, wide), lambda i: (0, 0, i))
    kinds = [(batch, rows, wide)] * BACK + [(batch, total, wide)] * (2 * BACK)
    return call(
        kernel,
        (shape((links.across, block, 3 * width + wide), bf16),) * 2,
        grid=(count + 1,),
        in_specs=[
            fixed((batch, rows, width)),
            fixed((batch, basis, width)),
            fixed(columns.shape),
            fixed(sums.shape),
        ]
        + [hbm()] * (count + links.outer),
        out_specs=(out, out),
        scratch=[
            pltpu.VMEM((width, 3 * width), bf16),
            pltpu.VMEM((width, 128), f32),
            pltpu.VMEM((128, width), f32),
        ]
        + [pltpu.VMEM(kind, bf16) for kind in kinds]
        + [pltpu.SemaphoreType.DMA((links.outer,)), pltpu.SemaphoreType.DMA((count,))],
        name="qkv_grads",
        flops=2 * batch * width * width * (3 * rows + 2 * basis),
        traffic=2 * batch * width * 7 * rows,
        after=after,
    )(
        units,
        memory_low,
        columns,
        sums,
        *[group[kind] for kind in range(3) for group in groups],
        *first,
    )


def body(links, tokens, cotangent, doc_start, memory_init, *shards):
    (
        norm1_gain,
        norm1_bias,
        qkv_weight,
        query_bias,
        value_bias,
        out_weight,
        out_bias,
        norm2_gain,
        norm2_bias,
        up_weight,
        up_bias,
        down_weight,
        down_bias,
    ) = shards
    own, width = out_weight.shape
    hidden = up_weight.shape[1]
    fold = hidden // width
    n = links.count
    tokens, cotangent, doc_start, memory_init = (
        tokens[:, 0],
        cotangent[:, 0],
        doc_start[:, 0],
        memory_init[0],
    )
    batch, rows, _ = tokens.shape

    small = (norm1_gain, norm1_bias, query_bias, value_bias, out_bias, norm2_gain, norm2_bias, down_bias)
    small = jnp.concatenate([jnp.stack(small).T, up_bias.reshape(own, fold)], axis=1)
    small = jnp.pad(small, ((0, 0), (0, 128 - small.shape[1])))
    wide = width // GROUPS
    positions = jnp.arange(rows)
    before = positions[None, :] <= positions[:, None]
    documents = jnp.sum(jnp.where(before, doc_start[:, None, :], 0), axis=2)
    documents = (documents[:, :, None], documents[:, None, :])

    carry_table, fresh_table = rbf_tables(rows, memory_init.shape[0])
    high = functools.partial(jnp.dot, precision=lax.Precision.HIGH)
    memories = [(memory_init,)]
    carried, gained, biased = memory_init, None, None
    for m in range(batch - 1):
        keep_share = jnp.where(documents[0][m, -1, 0] == 0, 1.0, 0.0)
        unit, _ = standardize(tokens[m].astype(f32))
        table = keep_share * carry_table
        carried = high(table, carried)
        new_gained = high(fresh_table, unit)
        new_biased = jnp.sum(fresh_table, axis=1, keepdims=True)
        if m:
            new_gained += high(table, gained)
            new_biased += high(table, biased)
        gained, biased = new_gained, new_biased
        memories.append((carried, gained, biased))

    flat = lambda v: v.reshape(batch * rows, v.shape[-1])
    full = lambda v: v.reshape(batch, rows, v.shape[-1])
    line = links.line(jnp.concatenate([qkv_weight, small], axis=1), [own], after=[carry_table])
    early = [v for memory in memories[1:] for v in memory] + list(documents)
    first = links.spread(line, early)
    unit = width // 2
    least = -(-(2**20) // (2 * links.deep * unit))
    packed = pack([out_weight, up_weight, down_weight], unit, -(-least // 16) * 16)
    packed = lax.all_gather(packed, "fsdp", axis=0, tiled=True)
    vectors, columns = unpack(links, first, width)
    made = project(links, tokens, memories, None, vectors, 0, first)
    queries, keys, values, units, memory_low = made
    line = regroup(links.deep, packed, 0, own, 2, 1 + fold, after=made[:1])
    mixture, inverse, exps = attend(queries, keys, values, *documents, after=[line])
    second = links.spread(line, [mixture])
    line = regroup(links.deep, packed, 2 * own * (1 + fold), fold * own, 2, 1, after=second)
    up_bias_full = columns[:, 8 : 8 + fold].reshape(1, hidden)
    cot = flat(cotangent)
    made = lift(
        links, flat(tokens), cot, flat(mixture), vectors, up_bias_full, second, hidden, after=[line]
    )
    residual, normed2, activated, slopes = made[:4]
    down_parts = made[4:]
    third, down_parts = links.spread(line, made[:1], down_parts)
    down_parts = links.merge_core(*down_parts, after=third[-1:])
    made = settle(
        links,
        residual,
        slopes,
        cot,
        flat(inverse),
        flat(mixture),
        normed2,
        vectors,
        second,
        third,
        hidden,
        after=down_parts[:1],
    )
    attn_grad, scaled, sums, up_sums = made[:4]
    up_parts = made[4:]
    sums = jnp.concatenate(
        [sums, up_sums[0].reshape(width, fold).T, jnp.zeros((8 - fold, width), f32)], axis=0
    )
    groups = []
    down_total = links.merge_columns(*down_parts, after=[attn_grad])
    up_parts = gate(up_parts, [down_total])
    hold = [down_total]
    pairs = width // PAIR // BACK
    for g in range(BACK):
        groups.append(
            attend_back(
                queries, keys, values, exps, mixture, full(scaled), g * pairs, pairs, after=hold
            )
        )
        hold = list(groups[-1][:1])
        if g == 0:
            up_parts = links.merge_core(*up_parts, after=hold)
            hold = [up_parts[0]]
    down_grad = links.merge_deep(down_total)
    qkv_parts = qkv_grads(links, units, memory_low, groups, first, columns, sums)
    up_total = links.merge_columns(*up_parts, after=qkv_parts[:1])
    up_grad = links.merge_deep(up_total)
    qkv_parts = links.merge_core(*qkv_parts, 3 * width + 128, after=[up_total, down_grad])
    output, tokens_grad = close(
        links,
        residual,
        activated,
        flat(tokens),
        attn_grad,
        groups,
        vectors,
        third,
        first,
        after=qkv_parts[:1],
    )
    qkv_parts = links.merge_line(*qkv_parts, after=[tokens_grad, up_grad])
    qkv_grad = links.merge_depth(*qkv_parts)
    vec = [qkv_grad[:, 3 * width + k] for k in range(8)]
    lead = lambda v: v[:, None]
    return (
        lead(full(output)),
        lead(full(tokens_grad)),
        vec[0],
        vec[1],
        qkv_grad[:, : 3 * width],
        vec[2],
        vec[3],
        up_grad[:, hidden:],
        vec[4],
        vec[5],
        vec[6],
        up_grad[:, :hidden],
        qkv_grad[:, 3 * width + 8 : 3 * width + 8 + fold].reshape(fold * own),
        down_grad,
        vec[7],
    )


def solution(mesh):
    both = ("dp", "fsdp")
    vector, matrix = P(both), P(both, None)
    params = (
        vector,
        vector,
        matrix,
        vector,
        vector,
        matrix,
        vector,
        vector,
        vector,
        matrix,
        vector,
        matrix,
        vector,
    )
    stream = P(None, both, None, None)
    return jax.shard_map(
        functools.partial(body, Links(mesh)),
        mesh=mesh,
        in_specs=(stream, stream, P(None, both, None), P(both, None, None)) + params,
        out_specs=(stream, stream) + params,
        check_vma=False,
    )
```
